128 devices in a mesh: node: 8 (over x, core), local: 16 (over z, y).
Axes of the slice: x: 4, y: 4, z: 4, core: 2. Of those that a mesh axis runs over, the one named last changes fastest.
Arguments:
- tokens: bfloat16 [8192, 7168], P('node', 'local'), may hold values from -6 to 6
- norm_gain: float32 [7168], replicated, may hold values from 0.5 to 1.5
- dense_gate: bfloat16 [7168, 4096], P(None, 'local'), may hold values from -0.0625 to 0.0625
- dense_up: bfloat16 [7168, 4096], P(None, 'local'), may hold values from -0.0625 to 0.0625
- dense_down: bfloat16 [4096, 7168], P('local'), may hold values from -0.09375 to 0.09375
- expert_gate: bfloat16 [8, 7168, 4096], P('node', None, 'local'), may hold values from -0.0625 to 0.0625
- expert_up: bfloat16 [8, 7168, 4096], P('node', None, 'local'), may hold values from -0.0625 to 0.0625
- expert_down: bfloat16 [8, 4096, 7168], P('node', 'local'), may hold values from -0.09375 to 0.09375
- expert_ids: int32 [8192, 2], P('node'), may hold values from 0 to 127, all different within a row
- route_gates: float32 [8192, 2], P('node'), may hold values from 0.1 to 0.9
Outputs:
- layer_out: bfloat16 [8192, 7168], P('node', 'local')
The draws below stay inside these ranges and needn't reach their ends.
Inputs may be any that keep to these rules, and one draw needn't show every extreme that they name: `expert_ids`: each row names two different experts.
All inputs are finite; a program needn't handle non-finite values.
Results may differ from the reference program's by a relative error of at most 0.014.
Values may be sent and summed in bfloat16 or wider, within the bound.
No kernel may reach another device: no remote copies, remote signals or barrier semaphores. Data moves between devices by JAX's collectives and lax.ppermute only.
A program may use at most 128 MiB of HBM per device.

```python
import jax
import jax.numpy as jnp
from jax import lax

D = 7168
DH = 4096
EH = 4096
EXPERTS = 128
TOK_NODE = 1024
TOKENS = 8192
EXP_WIN = 8
NODE_CAP = 16
DH_DEV = 256
N_NODE = 8
N_LOCAL = 16


def level_of(key, extent, shards, low, top_value):
    loudness, own = 1.0, jax.random.fold_in(key, 6)
    for dim, blocks in shards:
        heights = jnp.exp(jax.random.uniform(jax.random.fold_in(own, dim), (blocks,), jnp.float32, low / len(shards), top_value / len(shards)))
        loudness = loudness * jnp.repeat(heights, extent[dim] // blocks).reshape([-1 if axis == dim else 1 for axis in range(len(extent))])
    return loudness


def choose_distinct(own_key, rows, amount, top, lift):
    sequence = jax.random.permutation(jax.random.fold_in(own_key, 1), amount)
    pull = sequence
    for power in range(3):
        pull = pull * pull // amount
    pull = pull * lift // amount
    lots = jax.random.randint(jax.random.fold_in(own_key, 2), (rows, amount), 0, 4096) + pull
    sure = jax.random.permutation(jax.random.fold_in(own_key, 3), rows)[jnp.arange(amount) % rows]
    lots = jnp.where(jnp.arange(rows)[:, None] == sure[None, :], 1 << 14, lots)
    score = lots * amount + jnp.arange(amount)
    return lax.top_k(score.astype(jnp.int32), top)[1].astype(jnp.int32)


def gaussian(stream_key, extent, width, most, shards=(), kind=jnp.bfloat16):
    factor_of = level_of(stream_key, extent, shards, -0.22, 0.18) if shards else 1.0
    array = jax.random.normal(stream_key, extent, jnp.float32) * width * factor_of
    return jnp.minimum(jnp.maximum(array, -most), most).astype(kind)


def setup_inputs(seed: int = 0) -> dict:
    keys = jax.random.split(jax.random.key(seed), 11)
    return {
        "tokens": gaussian(keys[0], (TOKENS, D), 1.0, 6.0, ((0, 8), (1, 16))),
        "norm_gain": jnp.clip(1.0 + 0.1 * jax.random.normal(keys[1], (D,), jnp.float32), 0.5, 1.5),
        "dense_gate": gaussian(keys[2], (D, DH), D ** -0.5, 0.0625, ((1, 16),)),
        "dense_up": gaussian(keys[3], (D, DH), D ** -0.5, 0.0625, ((1, 16),)),
        "dense_down": gaussian(keys[4], (DH, D), DH ** -0.5, 0.09375, ((0, 16),)),
        "expert_gate": gaussian(keys[5], (EXP_WIN, D, EH), D ** -0.5, 0.0625, ((0, 8), (2, 16))),
        "expert_up": gaussian(keys[6], (EXP_WIN, D, EH), D ** -0.5, 0.0625, ((0, 8), (2, 16))),
        "expert_down": gaussian(keys[7], (EXP_WIN, EH, D), EH ** -0.5, 0.09375, ((0, 8), (1, 16))),
        "expert_ids": choose_distinct(keys[8], TOKENS, EXPERTS, 2, 256),
        "route_gates": jnp.clip(0.1 + 0.79999997 * jax.random.uniform(keys[9], (TOKENS, 2), jnp.float32) ** level_of(keys[9], (TOKENS, 2), ((0, 8),), -0.2, 0.2), 0.1, 0.9),
    }


EPSILON = 1e-05

def rms_normed(rows_in, gain_vec):
    as_float = rows_in.astype(jnp.float32)
    inv_scale = lax.rsqrt(lax.optimization_barrier(jnp.mean(as_float * as_float, axis=-1, keepdims=True)) + EPSILON)
    return (as_float * inv_scale * gain_vec.astype(jnp.float32)).astype(jnp.bfloat16)

def route_ranks(ids_block, window):
    flat_ids = ids_block.reshape(-1)
    expert_range = jnp.arange(window, dtype=jnp.int32)
    member = (flat_ids[:, None] == expert_range[None, :]).astype(jnp.int32)
    before = jnp.cumsum(member, axis=0) - member
    route_rank = lax.optimization_barrier(jnp.sum(before * member, axis=1))
    in_window = lax.optimization_barrier(jnp.sum(member, axis=1)) > 0
    return (route_rank.reshape(ids_block.shape), in_window.reshape(ids_block.shape))

def swiglu_rows(normed_rows, gate_weight, up_weight):
    gate_value = jnp.dot(normed_rows, gate_weight, preferred_element_type=jnp.float32)
    up_value = jnp.dot(normed_rows, up_weight, preferred_element_type=jnp.float32)
    return (jax.nn.silu(gate_value) * up_value).astype(jnp.bfloat16)

def reference(tokens, norm_gain, dense_gate, dense_up, dense_down, expert_gate, expert_up, expert_down, expert_ids, route_gates):
    normed = rms_normed(tokens, norm_gain)
    dense_hidden = swiglu_rows(normed, dense_gate, dense_up)
    hidden_parts = dense_hidden.reshape(TOKENS, N_LOCAL, DH_DEV).transpose(1, 0, 2)
    down_parts = dense_down.reshape(N_LOCAL, DH_DEV, D)

    def add_part(running, pair):
        partial_value = jnp.dot(pair[0], pair[1], preferred_element_type=jnp.float32).astype(jnp.bfloat16)
        partial_value = lax.optimization_barrier(partial_value)
        return (running + partial_value.astype(jnp.float32), None)
    dense_sum, _ = lax.scan(add_part, jnp.zeros((TOKENS, D), jnp.float32), (hidden_parts, down_parts))
    ids_nodes = expert_ids.reshape(N_NODE, TOK_NODE, 2)
    route_rank, in_window = jax.vmap(lambda block_ids: route_ranks(block_ids, EXP_WIN))(ids_nodes)
    kept = in_window & (route_rank < NODE_CAP)
    shape3 = (N_NODE, TOK_NODE, 2)
    token_index = jnp.broadcast_to(jnp.arange(N_NODE, dtype=jnp.int32)[:, None, None] * TOK_NODE + jnp.arange(TOK_NODE, dtype=jnp.int32)[None, :, None], shape3)
    source = jnp.broadcast_to(jnp.arange(N_NODE, dtype=jnp.int32)[:, None, None], shape3)
    expert = jnp.where(kept, ids_nodes, 0).astype(jnp.int32)
    place = jnp.where(kept, route_rank, NODE_CAP).astype(jnp.int32)
    table = jnp.full((EXP_WIN, N_NODE, NODE_CAP), -1, jnp.int32).at[expert, source, place].set(token_index, mode='drop')
    gate_table = jnp.zeros((EXP_WIN, N_NODE, NODE_CAP), jnp.float32).at[expert, source, place].set(route_gates.reshape(shape3).astype(jnp.float32), mode='drop')
    flat_table = table.reshape(EXP_WIN, N_NODE * NODE_CAP)
    gathered = normed[jnp.maximum(flat_table, 0)]
    gathered = jnp.where(flat_table[:, :, None] >= 0, gathered, jnp.zeros_like(gathered))

    def expert_apply(inputs):
        expert_rows, gate_weight, up_weight, down_weight = inputs
        expert_hidden = swiglu_rows(expert_rows, gate_weight, up_weight)
        return jnp.dot(expert_hidden, down_weight, preferred_element_type=jnp.float32).astype(jnp.bfloat16)
    expert_out = lax.map(expert_apply, (gathered, expert_gate, expert_up, expert_down))
    expert_out = lax.optimization_barrier(expert_out)
    route_term = (gate_table.reshape(EXP_WIN, N_NODE * NODE_CAP, 1) * expert_out.astype(jnp.float32)).astype(jnp.bfloat16)
    route_term = lax.optimization_barrier(route_term)
    target = jnp.where(flat_table >= 0, flat_table, TOKENS).reshape(-1)
    expert_sum = jnp.zeros((TOKENS, D), jnp.float32).at[target].add(route_term.reshape(-1, D).astype(jnp.float32), mode='drop')
    return (tokens.astype(jnp.float32) + dense_sum + expert_sum).astype(jnp.bfloat16)
```

```python
import jax
import jax.numpy as jnp
from jax import lax
from jax.sharding import PartitionSpec as P

EPSILON = 1e-05
NODE_CAP = 16


def route_slots(ids_block, window):
    flat_ids = ids_block.reshape(-1)
    expert_range = jnp.arange(window, dtype=jnp.int32)
    member = (flat_ids[:, None] == expert_range[None, :]).astype(jnp.int32)
    before = jnp.cumsum(member, axis=0) - member
    route_rank = jnp.sum(before * member, axis=1)
    kept = (jnp.sum(member, axis=1) > 0) & (route_rank < NODE_CAP)
    slot = jnp.where(kept, flat_ids * NODE_CAP + route_rank, -1)
    return slot.reshape(ids_block.shape)


def shards(
    tokens,
    norm_gain,
    dense_gate,
    dense_up,
    dense_down,
    expert_gate,
    expert_up,
    expert_down,
    expert_ids,
    route_gates,
):
    local_count = lax.axis_size("local")
    node_count = lax.axis_size("node")
    slice_width = tokens.shape[1]
    width = slice_width * local_count
    hidden = dense_gate.shape[1]
    slot_count = node_count * NODE_CAP

    whole_rows = lax.all_gather(tokens, "local", axis=1, tiled=True)

    slot = route_slots(expert_ids, node_count)
    slot_range = jnp.arange(slot_count, dtype=jnp.int32)
    matched = slot[:, :, None] == slot_range[None, None, :]
    match_float = matched.astype(jnp.float32)
    chosen = jnp.sum(match_float, axis=1).astype(jnp.bfloat16)
    slot_gate = jnp.sum(match_float * route_gates[:, :, None], axis=(0, 1))
    send_rows = lax.dot_general(
        chosen, tokens, (((0,), (0,)), ((), ())), preferred_element_type=jnp.float32
    ).astype(jnp.bfloat16)
    arrived = lax.all_to_all(
        send_rows.reshape(node_count, NODE_CAP, slice_width), "node", split_axis=0, concat_axis=0, tiled=True
    ).reshape(slot_count, slice_width)
    spread = jnp.broadcast_to(arrived[None], (local_count, slot_count, slice_width))
    pooled = lax.all_to_all(spread, "local", split_axis=0, concat_axis=0, tiled=True)
    pooled = pooled.transpose(1, 0, 2).reshape(slot_count, width)

    as_float = tokens.astype(jnp.float32)
    square_sum = lax.psum(jnp.sum(as_float * as_float, axis=-1), "local")
    inv_scale = lax.rsqrt(square_sum / width + EPSILON)[:, None]
    pooled_float = pooled.astype(jnp.float32)
    pooled_scale = lax.rsqrt(jnp.mean(pooled_float * pooled_float, axis=-1, keepdims=True) + EPSILON)
    pooled_normed = (pooled_float * pooled_scale * norm_gain).astype(jnp.bfloat16)

    gain_column = norm_gain[:, None]
    both = jnp.concatenate(
        [
            (dense_gate.astype(jnp.float32) * gain_column).astype(jnp.bfloat16),
            (dense_up.astype(jnp.float32) * gain_column).astype(jnp.bfloat16),
        ],
        axis=1,
    )

    expert_gate_value = jnp.dot(pooled_normed, expert_gate[0], preferred_element_type=jnp.float32)
    expert_up_value = jnp.dot(pooled_normed, expert_up[0], preferred_element_type=jnp.float32)
    expert_hidden = (jax.nn.silu(expert_gate_value) * expert_up_value).astype(jnp.bfloat16)
    expert_partial = jnp.dot(expert_hidden, expert_down[0], preferred_element_type=jnp.float32).astype(jnp.bfloat16)
    partial_blocks = expert_partial.reshape(slot_count, local_count, slice_width).transpose(1, 0, 2)
    partial_blocks = lax.all_to_all(partial_blocks, "local", split_axis=0, concat_axis=0, tiled=True)
    expert_out = jnp.sum(partial_blocks.astype(jnp.float32), axis=0).astype(jnp.bfloat16)
    returned = lax.all_to_all(
        expert_out.reshape(node_count, NODE_CAP, slice_width), "node", split_axis=0, concat_axis=0, tiled=True
    ).reshape(slot_count, slice_width)
    route_term = (slot_gate[:, None] * returned.astype(jnp.float32)).astype(jnp.bfloat16)
    expert_part = jnp.dot(chosen, route_term, preferred_element_type=jnp.float32)

    gate_up = jnp.dot(whole_rows, both, preferred_element_type=jnp.float32) * inv_scale
    dense_hidden = (jax.nn.silu(gate_up[:, :hidden]) * gate_up[:, hidden:]).astype(jnp.bfloat16)
    partial_sum = jnp.dot(dense_hidden, dense_down, preferred_element_type=jnp.float32).astype(jnp.bfloat16)
    dense_part = lax.psum_scatter(partial_sum, "local", scatter_dimension=1, tiled=True).astype(jnp.float32)
    return (tokens.astype(jnp.float32) + dense_part + expert_part).astype(jnp.bfloat16)


def solution(mesh):
    return jax.shard_map(
        shards,
        mesh=mesh,
        in_specs=(
            P("node", "local"),
            P(),
            P(None, "local"),
            P(None, "local"),
            P("local", None),
            P("node", None, "local"),
            P("node", None, "local"),
            P("node", "local", None),
            P("node", None),
            P("node", None),
        ),
        out_specs=P("node", "local"),
        check_vma=False,
    )
```

```python
import functools

import jax
import jax.numpy as jnp
from jax import lax
from jax.experimental import pallas as pl
from jax.experimental.pallas import tpu as pltpu
from jax.sharding import PartitionSpec as P

EPSILON = 1e-05
NODE_CAP = 16
GRAY = (0, 1, 3, 2)

LOCAL_LABEL = [GRAY[i % 4] | GRAY[i // 4] << 2 for i in range(16)]
LOCAL_AT = {label: i for i, label in enumerate(LOCAL_LABEL)}
NODE_LABEL = [i % 2 | GRAY[i // 2] << 1 for i in range(8)]
NODE_AT = {label: i for i, label in enumerate(NODE_LABEL)}

STREAMS = ((0, 1, 2), (1, 2, 0), (2, 0, 1))


def stream_rows(rows):
    third = -(-rows // 48) * 16
    return (0, third), (third, 2 * third), (2 * third, rows)


def flip_local(array, bit):
    return lax.ppermute(array, "local", [(i, LOCAL_AT[LOCAL_LABEL[i] ^ (1 << bit)]) for i in range(16)])


def flip_node(array, bit):
    return lax.ppermute(array, "node", [(i, NODE_AT[NODE_LABEL[i] ^ (1 << bit)]) for i in range(8)])


def route_slots(ids_block, window):
    flat_ids = ids_block.reshape(-1)
    expert_range = jnp.arange(window, dtype=jnp.int32)
    member = (flat_ids[:, None] == expert_range[None, :]).astype(jnp.int32)
    before = jnp.cumsum(member, axis=0) - member
    route_rank = jnp.sum(before * member, axis=1)
    kept = (jnp.sum(member, axis=1) > 0) & (route_rank < NODE_CAP)
    slot = jnp.where(kept, flat_ids * NODE_CAP + route_rank, -1)
    return slot.reshape(ids_block.shape)


def transposed_dot(weight, rows):
    return lax.dot_general(weight, rows, (((0,), (0,)), ((), ())), preferred_element_type=jnp.float32)


def silu(value):
    return value / (1.0 + jnp.exp(-value))


def gate_up_kernel(blocks, features, with_scale, pair_ref, *refs):
    if with_scale:
        x0, x1, x2, weight, scale_in, hidden_ref, total = refs
    else:
        x0, x1, x2, weight, hidden_ref, scale_out, total, squares = refs
    step = pl.program_id(0)

    @pl.when(step == 0)
    def _():
        total[...] = jnp.zeros_like(total)
        if not with_scale:
            squares[...] = jnp.zeros_like(squares)

    rows = jnp.concatenate([x0[0], x1[0], x2[0]], axis=0)
    total[...] += transposed_dot(weight[0], rows)
    if not with_scale:
        as_float = rows.astype(jnp.float32)
        squares[...] += jnp.sum(as_float * as_float, axis=0, keepdims=True)

    @pl.when(step == blocks - 1)
    def _():
        if with_scale:
            scale = scale_in[...]
        else:
            scale = lax.rsqrt(squares[...] / features + EPSILON)
            scale_out[...] = scale
        half = total.shape[0] // 2
        hidden_ref[...] = (silu(total[:half] * scale) * (total[half:] * scale)).astype(jnp.bfloat16)


def gate_up(pair_of, streams, weight, scale=None):
    blocks, _, columns = streams[0].shape
    rows = sum(s.shape[1] for s in streams)
    both = weight.shape[-1]

    def stream_spec(s):
        a, b, c = STREAMS[s]

        def index(m, pair):
            return (((m >> a) & 1) | ((m >> b) & 1) << 1 | ((m >> c) & 1) << 2, 0, 0)

        return pl.BlockSpec((1, streams[s].shape[1], columns), index)

    in_specs = [stream_spec(s) for s in range(3)]
    in_specs.append(pl.BlockSpec((1, rows, both), lambda m, pair: (pair[m], 0, 0)))
    operands = [*streams, weight.reshape(blocks, rows, both)]
    out_shape = [jax.ShapeDtypeStruct((both // 2, columns), jnp.bfloat16)]
    out_specs = [pl.BlockSpec((both // 2, columns), lambda m, pair: (0, 0))]
    scratch = [pltpu.VMEM((both, columns), jnp.float32)]
    whole_scale = pl.BlockSpec((1, columns), lambda m, pair: (0, 0))
    if scale is None:
        out_shape.append(jax.ShapeDtypeStruct((1, columns), jnp.float32))
        out_specs.append(whole_scale)
        scratch.append(pltpu.VMEM((1, columns), jnp.float32))
    else:
        in_specs.append(whole_scale)
        operands.append(scale)
    return pl.pallas_call(
        functools.partial(gate_up_kernel, blocks, blocks * rows, scale is not None),
        grid_spec=pltpu.PrefetchScalarGridSpec(
            num_scalar_prefetch=1, grid=(blocks,), in_specs=in_specs, out_specs=out_specs, scratch_shapes=scratch
        ),
        out_shape=out_shape,
        compiler_params=pltpu.CompilerParams(vmem_limit_bytes=24 << 20),
        cost_estimate=pl.CostEstimate(
            flops=2 * blocks * rows * columns * both, bytes_accessed=2 * blocks * rows * (columns + both), transcendentals=0
        ),
    )(pair_of, *operands)


def down_kernel(spans, own_pair, other_pair, *refs):
    own, other = refs[0:3], refs[3:6]
    own_hidden, other_hidden = refs[6], refs[7]
    outs = refs[8:11]
    for s, (low, high) in enumerate(spans):
        part = jnp.dot(own[s][0, low:high], own_hidden[...], preferred_element_type=jnp.float32)
        part += jnp.dot(other[s][0, low:high], other_hidden[...], preferred_element_type=jnp.float32)
        outs[s][0] = part.astype(jnp.bfloat16)


def down(own_pair, other_pair, own_weight, other_weight, own_hidden, other_hidden, sent):
    blocks, rows, hidden = own_weight.shape
    columns = own_hidden.shape[1]
    spans = stream_rows(rows)

    def mask(s, j):
        a, b, c = STREAMS[s]
        return sent << a | ((j >> 1) & 1) << b | (j & 1) << c

    def own_spec(s):
        return pl.BlockSpec((1, rows, hidden), lambda j, p, q: (p[mask(s, j)], 0, 0))

    def other_spec(s):
        return pl.BlockSpec((1, rows, hidden), lambda j, p, q: (q[mask(s, j)], 0, 0))

    hidden_spec = pl.BlockSpec((hidden, columns), lambda j, p, q: (0, 0))
    half = blocks // 2
    return pl.pallas_call(
        functools.partial(down_kernel, spans),
        grid_spec=pltpu.PrefetchScalarGridSpec(
            num_scalar_prefetch=2,
            grid=(half,),
            in_specs=[own_spec(s) for s in range(3)] + [other_spec(s) for s in range(3)] + [hidden_spec] * 2,
            out_specs=[pl.BlockSpec((1, high - low, columns), lambda j, p, q: (j, 0, 0)) for low, high in spans],
        ),
        out_shape=[jax.ShapeDtypeStruct((half, high - low, columns), jnp.bfloat16) for low, high in spans],
        compiler_params=pltpu.CompilerParams(vmem_limit_bytes=24 << 20),
        cost_estimate=pl.CostEstimate(
            flops=4 * half * rows * hidden * columns,
            bytes_accessed=2 * half * rows * (6 * hidden + columns),
            transcendentals=0,
        ),
    )(own_pair, other_pair, *[own_weight] * 3, *[other_weight] * 3, own_hidden, other_hidden)


def expert_kernel(blocks, features, at_ref, x_ref, gate_ref, up_ref, gain_ref, hidden_ref, gate_total, up_total, squares):
    step = pl.program_id(0)

    @pl.when(step == 0)
    def _():
        gate_total[...] = jnp.zeros_like(gate_total)
        up_total[...] = jnp.zeros_like(up_total)
        squares[...] = jnp.zeros_like(squares)

    as_float = x_ref[0].astype(jnp.float32)
    squares[...] += jnp.sum(as_float * as_float, axis=0, keepdims=True)
    rows = (as_float * gain_ref[...]).astype(jnp.bfloat16)
    gate_total[...] += transposed_dot(gate_ref[0], rows)
    up_total[...] += transposed_dot(up_ref[0], rows)

    @pl.when(step == blocks - 1)
    def _():
        scale = lax.rsqrt(squares[...] / features + EPSILON)
        hidden_ref[...] = (silu(gate_total[...] * scale) * (up_total[...] * scale)).astype(jnp.bfloat16)


def expert_gate_up(slice_of, pooled, gate_weight, up_weight, gain_column):
    blocks, rows, columns = pooled.shape
    hidden = gate_weight.shape[-1]
    weight_spec = pl.BlockSpec((1, rows, hidden), lambda m, at: (0, at[m], 0))
    return pl.pallas_call(
        functools.partial(expert_kernel, blocks, blocks * rows),
        grid_spec=pltpu.PrefetchScalarGridSpec(
            num_scalar_prefetch=1,
            grid=(blocks,),
            in_specs=[
                pl.BlockSpec((1, rows, columns), lambda m, at: (m, 0, 0)),
                weight_spec,
                weight_spec,
                pl.BlockSpec((rows, 1), lambda m, at: (at[m], 0)),
            ],
            out_specs=pl.BlockSpec((hidden, columns), lambda m, at: (0, 0)),
            scratch_shapes=[
                pltpu.VMEM((hidden, columns), jnp.float32),
                pltpu.VMEM((hidden, columns), jnp.float32),
                pltpu.VMEM((1, columns), jnp.float32),
            ],
        ),
        out_shape=jax.ShapeDtypeStruct((hidden, columns), jnp.bfloat16),
        compiler_params=pltpu.CompilerParams(vmem_limit_bytes=24 << 20),
        cost_estimate=pl.CostEstimate(
            flops=4 * blocks * rows * columns * hidden,
            bytes_accessed=2 * blocks * rows * (columns + 2 * hidden),
            transcendentals=0,
        ),
    )(slice_of, pooled, gate_weight, up_weight, gain_column)


def add_pair(kept, got):
    return (kept.astype(jnp.float32) + got.astype(jnp.float32)).astype(jnp.bfloat16)


def shards(
    tokens,
    norm_gain,
    dense_gate,
    dense_up,
    dense_down,
    expert_gate,
    expert_up,
    expert_down,
    expert_ids,
    route_gates,
):
    node_count = lax.axis_size("node")
    node_index = lax.axis_index("node")
    local_index = lax.axis_index("local")
    tok_node, slice_width = tokens.shape
    width = slice_width * 16
    pair_width = 2 * slice_width
    half_tokens = tok_node // 2
    slot_count = node_count * NODE_CAP
    spans = stream_rows(pair_width)

    label = jnp.asarray(LOCAL_LABEL, jnp.int32)[local_index]
    own_half = label & 1
    odd = (local_index & 1) == 1
    pair_table = [[LOCAL_AT[LOCAL_LABEL[i] ^ (2 * m)] // 2 for m in range(8)] for i in range(16)]
    pair_of = jnp.asarray(pair_table, jnp.int32)[local_index]
    slice_table = [[LOCAL_AT[LOCAL_LABEL[i] ^ m] for m in range(16)] for i in range(16)]
    slice_of = jnp.asarray(slice_table, jnp.int32)[local_index]
    place_table = [[0] * 8 for _ in range(8)]
    for i in range(8):
        for j in range(8):
            diff = NODE_LABEL[i] ^ NODE_LABEL[j]
            place_table[i][j] = ((diff >> 1) & 1) | ((diff >> 2) & 1) << 1 | (diff & 1) << 2
    other_of = jnp.asarray(place_table, jnp.int32)[node_index][pair_of]

    columns = tokens.T
    mine = lax.dynamic_slice_in_dim(columns, own_half * half_tokens, half_tokens, 1)
    give = lax.dynamic_slice_in_dim(columns, (1 - own_half) * half_tokens, half_tokens, 1)
    got = flip_local(give, 0)

    block_start = node_index * pair_width

    def folded(gate_rows, up_rows, gain_rows):
        gain_rows = gain_rows[:, None]
        return jnp.concatenate(
            [
                (gate_rows.astype(jnp.float32) * gain_rows).astype(jnp.bfloat16),
                (up_rows.astype(jnp.float32) * gain_rows).astype(jnp.bfloat16),
            ],
            axis=1,
        )

    piece = folded(
        lax.dynamic_slice_in_dim(dense_gate, block_start, pair_width, 0),
        lax.dynamic_slice_in_dim(dense_up, block_start, pair_width, 0),
        lax.dynamic_slice_in_dim(norm_gain, block_start, pair_width, 0),
    )
    piece = flip_local(piece, 0)
    other_both = lax.all_gather(piece, "node", axis=0, tiled=True)
    down_piece = flip_local(lax.dynamic_slice_in_dim(dense_down, block_start, pair_width, 1).T, 0)[None]
    for bit in (1, 2, 0):
        down_piece = jnp.concatenate([down_piece, flip_node(down_piece, bit)], axis=0)

    pair_block = jnp.where(odd, jnp.concatenate([got, mine], axis=0), jnp.concatenate([mine, got], axis=0))
    streams = [pair_block[None, low:high] for low, high in spans]
    for step in range(3):
        arrived = [flip_local(streams[s], 1 + STREAMS[s][step]) for s in range(3)]
        streams = [jnp.concatenate([streams[s], arrived[s]], axis=0) for s in range(3)]

    own_both = folded(dense_gate, dense_up, norm_gain)
    own_down = dense_down.T.reshape(8, pair_width, dense_down.shape[0])

    slot = route_slots(expert_ids, node_count)
    slot_range = jnp.arange(slot_count, dtype=jnp.int32)
    match_float = (slot[:, :, None] == slot_range[None, None, :]).astype(jnp.float32)
    chosen = jnp.sum(match_float, axis=1).astype(jnp.bfloat16)
    slot_gate = jnp.sum(match_float * route_gates[:, :, None], axis=(0, 1))
    send_rows = lax.dot_general(
        chosen, tokens, (((0,), (0,)), ((), ())), preferred_element_type=jnp.float32
    ).astype(jnp.bfloat16)
    pooled = lax.all_to_all(
        send_rows.reshape(node_count, NODE_CAP, slice_width), "node", split_axis=0, concat_axis=0, tiled=True
    )
    pooled = pooled.reshape(slot_count, slice_width).T[None]
    for bit in range(4):
        pooled = jnp.concatenate([pooled, flip_local(pooled, bit)], axis=0)
    expert_hidden = expert_gate_up(slice_of, pooled, expert_gate, expert_up, norm_gain[:, None])
    expert_partial = transposed_dot(expert_down[0], expert_hidden).astype(jnp.bfloat16)
    expert_partial = expert_partial.reshape(16, slice_width, slot_count)
    position = local_index
    for bit in (3, 2, 1, 0):
        half = 1 << bit
        upper = position // half
        keep = lax.dynamic_slice_in_dim(expert_partial, upper * half, half, 0)
        send = lax.dynamic_slice_in_dim(expert_partial, (1 - upper) * half, half, 0)
        expert_partial = add_pair(keep, flip_local(send, bit))
        position = position - upper * half
    expert_out = expert_partial[0].T
    returned = lax.all_to_all(
        expert_out.reshape(node_count, NODE_CAP, slice_width), "node", split_axis=0, concat_axis=0, tiled=True
    ).reshape(slot_count, slice_width)
    route_term = (slot_gate[:, None] * returned.astype(jnp.float32)).astype(jnp.bfloat16)
    expert_part = lax.dot_general(
        route_term, chosen, (((0,), (1,)), ((), ())), preferred_element_type=jnp.float32
    )

    own_hidden, scale = gate_up(pair_of, streams, own_both)
    (other_hidden,) = gate_up(pair_of, streams, other_both, scale)
    sent = down(pair_of, other_of, own_down, down_piece, own_hidden, other_hidden, 1)
    arrived = [flip_local(sent[s], 1 + STREAMS[s][0]) for s in range(3)]
    kept = down(pair_of, other_of, own_down, down_piece, own_hidden, other_hidden, 0)
    sums = [add_pair(kept[s], arrived[s]) for s in range(3)]
    for step in (1, 2):
        half = sums[0].shape[0] // 2
        arrived = [flip_local(sums[s][half:], 1 + STREAMS[s][step]) for s in range(3)]
        sums = [add_pair(sums[s][:half], arrived[s]) for s in range(3)]
    pair_sum = jnp.concatenate([sums[s][0] for s in range(3)], axis=0)
    even_rows, odd_rows = pair_sum[:slice_width], pair_sum[slice_width:]
    mine = jnp.where(odd, odd_rows, even_rows)
    got = flip_local(jnp.where(odd, even_rows, odd_rows), 0)
    dense_part = jnp.where(
        own_half == 1, jnp.concatenate([got, mine], axis=1), jnp.concatenate([mine, got], axis=1)
    ).astype(jnp.float32)
    return (columns.astype(jnp.float32) + dense_part + expert_part).astype(jnp.bfloat16).T


def solution(mesh):
    return jax.shard_map(
        shards,
        mesh=mesh,
        in_specs=(
            P("node", "local"),
            P(),
            P(None, "local"),
            P(None, "local"),
            P("local", None),
            P("node", None, "local"),
            P("node", None, "local"),
            P("node", "local", None),
            P("node", None),
            P("node", None),
        ),
        out_specs=P("node", "local"),
        check_vma=False,
    )
```

```python
import functools

import jax
import jax.numpy as jnp
from jax import lax
from jax.experimental import pallas as pl
from jax.experimental.pallas import tpu as pltpu
from jax.sharding import PartitionSpec as P

EPSILON = 1e-05
NODE_CAP = 16
GRAY = (0, 1, 3, 2)

LOCAL_LABEL = [GRAY[i % 4] | GRAY[i // 4] << 2 for i in range(16)]
LOCAL_AT = {label: i for i, label in enumerate(LOCAL_LABEL)}
NODE_LABEL = [i % 2 | GRAY[i // 2] << 1 for i in range(8)]
NODE_AT = {label: i for i, label in enumerate(NODE_LABEL)}

STREAMS = ((0, 1, 2), (1, 2, 0), (2, 0, 1))
ROW_BITS = (1, 2, 3, 0)


def stream_rows(rows):
    third = -(-rows // 48) * 16
    return (0, third), (third, 2 * third), (2 * third, rows)


def flip_local(array, bit):
    return lax.ppermute(array, "local", [(i, LOCAL_AT[LOCAL_LABEL[i] ^ (1 << bit)]) for i in range(16)])


def flip_node(array, bit):
    return lax.ppermute(array, "node", [(i, NODE_AT[NODE_LABEL[i] ^ (1 << bit)]) for i in range(8)])


def route_slots(ids_block, window):
    flat_ids = ids_block.reshape(-1)
    expert_range = jnp.arange(window, dtype=jnp.int32)
    member = (flat_ids[:, None] == expert_range[None, :]).astype(jnp.int32)
    before = jnp.cumsum(member, axis=0) - member
    route_rank = jnp.sum(before * member, axis=1)
    kept = (jnp.sum(member, axis=1) > 0) & (route_rank < NODE_CAP)
    slot = jnp.where(kept, flat_ids * NODE_CAP + route_rank, -1)
    return slot.reshape(ids_block.shape)


def transposed_dot(weight, rows):
    return lax.dot_general(weight, rows, (((0,), (0,)), ((), ())), preferred_element_type=jnp.float32)


def silu(value):
    return value / (1.0 + jnp.exp(-value))


def gate_up_kernel(last, features, count, *refs):
    refs = refs[1:]
    x, gains, refs = refs[0:3], refs[3:6], refs[6:]
    weights, refs = [refs[s * count : (s + 1) * count] for s in range(3)], refs[3 * count :]
    if last:
        total_in, squares_in, result, squares_out, total, squares = refs
    else:
        result, squares_out, total, squares = refs
    step = pl.program_id(0)

    @pl.when(step == 0)
    def _():
        total[...] = total_in[...] if last else jnp.zeros_like(total)
        squares[...] = squares_in[...] if last else jnp.zeros_like(squares)

    wide = total.shape[0] // count
    for s in range(3):
        as_float = x[s][0].astype(jnp.float32)
        squares[...] += jnp.sum(as_float * as_float, axis=0, keepdims=True)
        rows = (as_float * gains[s][...]).astype(jnp.bfloat16)
        for i in range(count):
            total[i * wide : (i + 1) * wide] += transposed_dot(weights[s][i][...], rows)

    @pl.when(step == pl.num_programs(0) - 1)
    def _():
        squares_out[...] = squares[...]
        if last:
            scale = lax.rsqrt(squares[...] / features + EPSILON)
            half = total.shape[0] // 2
            result[...] = (silu(total[:half] * scale) * (total[half:] * scale)).astype(jnp.bfloat16)
        else:
            result[...] = total[...]


def gate_up(pair_of, streams, gain_column, weights, before=None):
    last = int(before is not None)
    blocks, _, columns = streams[0].shape
    features = weights[0].shape[0]
    pair_rows = features // (2 * blocks)
    spans = stream_rows(pair_rows)
    both = sum(w.shape[1] for w in weights)

    def row_spec(s, wide):
        a, b, c = STREAMS[s]
        low, high = spans[s]

        def index(j, pair):
            mask = (j & 1) << a | ((j >> 1) & 1) << b | last << c
            return pl.multiple_of(pair[mask] * pair_rows + low, 16), 0

        return pl.BlockSpec((pl.Element(high - low), pl.Element(wide)), index)

    def whole(rows):
        return pl.BlockSpec((rows, columns), lambda j, pair: (0, 0))

    in_specs = [pl.BlockSpec((1, high - low, columns), lambda j, pair: (j, 0, 0)) for low, high in spans]
    in_specs += [row_spec(s, 1) for s in range(3)]
    in_specs += [row_spec(s, w.shape[1]) for s in range(3) for w in weights]
    operands = [*streams, *[gain_column] * 3, *[w for _ in range(3) for w in weights]]
    if last:
        in_specs += [whole(both), whole(1)]
        operands += before
        result = jax.ShapeDtypeStruct((both // 2, columns), jnp.bfloat16)
    else:
        result = jax.ShapeDtypeStruct((both, columns), jnp.float32)
    return pl.pallas_call(
        functools.partial(gate_up_kernel, last, features, len(weights)),
        grid_spec=pltpu.PrefetchScalarGridSpec(
            num_scalar_prefetch=1,
            grid=(blocks,),
            in_specs=in_specs,
            out_specs=[whole(result.shape[0]), whole(1)],
            scratch_shapes=[pltpu.VMEM((both, columns), jnp.float32), pltpu.VMEM((1, columns), jnp.float32)],
        ),
        out_shape=[result, jax.ShapeDtypeStruct((1, columns), jnp.float32)],
        compiler_params=pltpu.CompilerParams(vmem_limit_bytes=24 << 20),
        cost_estimate=pl.CostEstimate(
            flops=features * columns * both, bytes_accessed=features * (columns + both), transcendentals=0
        ),
    )(pair_of, *operands)


def down_kernel(spans, own_pair, other_pair, own, other, own_hidden, other_hidden, *outs):
    step = pl.program_id(0)
    part = transposed_dot(own[...], own_hidden[...]) + transposed_dot(other[0], other_hidden[...])
    for s, (low, high) in enumerate(spans):
        rows = part[low:high].astype(jnp.bfloat16)
        is_sent = ((step >> STREAMS[s][0]) & 1) == 1

        @pl.when(is_sent)
        def _():
            outs[s][0] = rows

        @pl.when(jnp.logical_not(is_sent))
        def _():
            outs[3 + s][0] = rows


def down(own_pair, other_pair, own_weight, other_weight, own_hidden, other_hidden):
    blocks, hidden, rows = other_weight.shape
    columns = own_hidden.shape[1]
    spans = stream_rows(rows)

    def out_spec(s, sent):
        a, b, c = STREAMS[s]
        low, high = spans[s]

        def index(m, p, q):
            if sent:
                here = jnp.where((m >> a) & 1 == 1, m, ((m >> a) | 1) << a)
            else:
                here = jnp.where((m >> a) & 1 == 0, m, jnp.minimum(((m >> a) + 1) << a, (blocks - 1) ^ (1 << a)))
            return ((here >> b) & 1) << 1 | ((here >> c) & 1), 0, 0

        return pl.BlockSpec((1, high - low, columns), index)

    hidden_spec = pl.BlockSpec((hidden, columns), lambda m, p, q: (0, 0))
    return pl.pallas_call(
        functools.partial(down_kernel, spans),
        grid_spec=pltpu.PrefetchScalarGridSpec(
            num_scalar_prefetch=2,
            grid=(blocks,),
            in_specs=[
                pl.BlockSpec((hidden, rows), lambda m, p, q: (0, p[m])),
                pl.BlockSpec((1, hidden, rows), lambda m, p, q: (q[m], 0, 0)),
                hidden_spec,
                hidden_spec,
            ],
            out_specs=[out_spec(s, sent) for sent in (1, 0) for s in range(3)],
        ),
        out_shape=[jax.ShapeDtypeStruct((blocks // 2, high - low, columns), jnp.bfloat16) for low, high in spans] * 2,
        compiler_params=pltpu.CompilerParams(vmem_limit_bytes=24 << 20),
        cost_estimate=pl.CostEstimate(
            flops=4 * blocks * rows * hidden * columns,
            bytes_accessed=2 * blocks * rows * (2 * hidden + columns),
            transcendentals=0,
        ),
    )(own_pair, other_pair, own_weight, other_weight, own_hidden, other_hidden)


def expert_kernel(blocks, features, at_ref, x_ref, gate_ref, up_ref, gain_ref, hidden_ref, gate_total, up_total, squares):
    step = pl.program_id(0)

    @pl.when(step == 0)
    def _():
        gate_total[...] = jnp.zeros_like(gate_total)
        up_total[...] = jnp.zeros_like(up_total)
        squares[...] = jnp.zeros_like(squares)

    as_float = x_ref[0].astype(jnp.float32)
    squares[...] += jnp.sum(as_float * as_float, axis=0, keepdims=True)
    rows = (as_float * gain_ref[...]).astype(jnp.bfloat16)
    gate_total[...] += transposed_dot(gate_ref[0], rows)
    up_total[...] += transposed_dot(up_ref[0], rows)

    @pl.when(step == blocks - 1)
    def _():
        scale = lax.rsqrt(squares[...] / features + EPSILON)
        hidden_ref[...] = (silu(gate_total[...] * scale) * (up_total[...] * scale)).astype(jnp.bfloat16)


def expert_gate_up(slice_of, pooled, gate_weight, up_weight, gain_column):
    blocks, rows, columns = pooled.shape
    hidden = gate_weight.shape[-1]
    weight_spec = pl.BlockSpec((1, rows, hidden), lambda m, at: (0, at[m], 0))
    return pl.pallas_call(
        functools.partial(expert_kernel, blocks, blocks * rows),
        grid_spec=pltpu.PrefetchScalarGridSpec(
            num_scalar_prefetch=1,
            grid=(blocks,),
            in_specs=[
                pl.BlockSpec((1, rows, columns), lambda m, at: (m, 0, 0)),
                weight_spec,
                weight_spec,
                pl.BlockSpec((rows, 1), lambda m, at: (at[m], 0)),
            ],
            out_specs=pl.BlockSpec((hidden, columns), lambda m, at: (0, 0)),
            scratch_shapes=[
                pltpu.VMEM((hidden, columns), jnp.float32),
                pltpu.VMEM((hidden, columns), jnp.float32),
                pltpu.VMEM((1, columns), jnp.float32),
            ],
        ),
        out_shape=jax.ShapeDtypeStruct((hidden, columns), jnp.bfloat16),
        compiler_params=pltpu.CompilerParams(vmem_limit_bytes=24 << 20),
        cost_estimate=pl.CostEstimate(
            flops=4 * blocks * rows * columns * hidden,
            bytes_accessed=2 * blocks * rows * (columns + 2 * hidden),
            transcendentals=0,
        ),
    )(slice_of, pooled, gate_weight, up_weight, gain_column)


def add_pair(kept, got):
    return (kept.astype(jnp.float32) + got.astype(jnp.float32)).astype(jnp.bfloat16)


def shards(
    tokens,
    norm_gain,
    dense_gate,
    dense_up,
    dense_down,
    expert_gate,
    expert_up,
    expert_down,
    expert_ids,
    route_gates,
):
    node_count = lax.axis_size("node")
    node_index = lax.axis_index("node")
    local_index = lax.axis_index("local")
    tok_node, slice_width = tokens.shape
    width = slice_width * 16
    pair_width = 2 * slice_width
    half_tokens = tok_node // 2
    slot_count = node_count * NODE_CAP
    spans = stream_rows(pair_width)

    label = jnp.asarray(LOCAL_LABEL, jnp.int32)[local_index]
    own_half = label & 1
    odd = (local_index & 1) == 1
    pair_table = [[LOCAL_AT[LOCAL_LABEL[i] ^ (2 * m)] // 2 for m in range(8)] for i in range(16)]
    pair_of = jnp.asarray(pair_table, jnp.int32)[local_index]
    slice_table = [
        [LOCAL_AT[LOCAL_LABEL[i] ^ sum(((q >> t) & 1) << bit for t, bit in enumerate(ROW_BITS))] for q in range(16)]
        for i in range(16)
    ]
    slice_of = jnp.asarray(slice_table, jnp.int32)[local_index]
    place_table = [[0] * 8 for _ in range(8)]
    for i in range(8):
        for j in range(8):
            diff = NODE_LABEL[i] ^ NODE_LABEL[j]
            place_table[i][j] = ((diff >> 1) & 1) | ((diff >> 2) & 1) << 1 | (diff & 1) << 2
    other_of = jnp.asarray(place_table, jnp.int32)[node_index][pair_of]
    block_start = node_index * pair_width

    columns = tokens.T
    mine = lax.dynamic_slice_in_dim(columns, own_half * half_tokens, half_tokens, 1)
    give = lax.dynamic_slice_in_dim(columns, (1 - own_half) * half_tokens, half_tokens, 1)
    got = flip_local(give, 0)

    slot = route_slots(expert_ids, node_count)
    slot_range = jnp.arange(slot_count, dtype=jnp.int32)
    match_float = (slot[:, :, None] == slot_range[None, None, :]).astype(jnp.float32)
    chosen = jnp.sum(match_float, axis=1).astype(jnp.bfloat16)
    slot_gate = jnp.sum(match_float * route_gates[:, :, None], axis=(0, 1))
    send_rows = lax.dot_general(
        chosen, tokens, (((0,), (0,)), ((), ())), preferred_element_type=jnp.float32
    ).astype(jnp.bfloat16)
    got, send_rows = lax.optimization_barrier((got, send_rows))
    pooled = lax.all_to_all(
        send_rows.reshape(node_count, NODE_CAP, slice_width), "node", split_axis=0, concat_axis=0, tiled=True
    )

    piece = jnp.concatenate(
        [lax.dynamic_slice_in_dim(w, block_start, pair_width, 0) for w in (dense_gate, dense_up)], axis=1
    )
    piece, _ = lax.optimization_barrier((piece, got))
    piece = flip_local(piece, 0)

    pair_block = jnp.where(odd, jnp.concatenate([got, mine], axis=0), jnp.concatenate([mine, got], axis=0))
    streams = [pair_block[None, low:high] for low, high in spans]
    arrived = [flip_local(streams[s], 1 + STREAMS[s][0]) for s in range(3)]
    pooled = pooled.reshape(slot_count, slice_width).T[None]
    gain_column = norm_gain[:, None]
    arrived, pooled, gain_column = lax.optimization_barrier((arrived, pooled, gain_column))
    streams = [jnp.concatenate([streams[s], arrived[s]], axis=0) for s in range(3)]
    arrived = [flip_local(streams[s], 1 + STREAMS[s][1]) for s in range(3)]
    for bit in ROW_BITS[:2]:
        pooled = jnp.concatenate([pooled, flip_local(pooled, bit)], axis=0)
    pooled, arrived, piece = lax.optimization_barrier((pooled, arrived, piece))
    other_both = lax.all_gather(piece, "node", axis=0, tiled=True)
    down_piece = lax.dynamic_slice_in_dim(dense_down, block_start, pair_width, 1)
    down_piece, _ = lax.optimization_barrier((down_piece, arrived[0]))
    down_piece = flip_local(down_piece, 0)[None]
    streams = [jnp.concatenate([streams[s], arrived[s]], axis=0) for s in range(3)]
    arrived = [flip_local(streams[s], 1 + STREAMS[s][2]) for s in range(3)]
    own_weights = (dense_gate, dense_up)
    own_before = gate_up(pair_of, streams, gain_column, own_weights)
    pooled = jnp.concatenate([pooled, flip_local(pooled, ROW_BITS[2])], axis=0)
    own_before, down_piece, pooled = lax.optimization_barrier((own_before, down_piece, pooled))
    pooled_other = flip_local(pooled, ROW_BITS[3])
    down_piece = jnp.concatenate([down_piece, flip_node(down_piece, 1)], axis=0)
    down_piece, own_before, arrived = lax.optimization_barrier((down_piece, own_before, arrived))
    down_other = flip_node(down_piece, 2)
    own_hidden, _ = gate_up(pair_of, arrived, gain_column, own_weights, own_before)

    own_hidden, pooled_other = lax.optimization_barrier((own_hidden, pooled_other))
    pooled = jnp.concatenate([pooled, pooled_other], axis=0)
    expert_hidden = expert_gate_up(slice_of, pooled, expert_gate, expert_up, gain_column)
    expert_hidden, down_other = lax.optimization_barrier((expert_hidden, down_other))
    down_piece = jnp.concatenate([down_piece, down_other], axis=0)
    down_other = flip_node(down_piece, 0)
    expert_partial = transposed_dot(expert_down[0], expert_hidden).astype(jnp.bfloat16)
    expert_partial = expert_partial.reshape(2, 2, 2, 2, slice_width, slot_count)

    def halve(array, bit):
        axis = 3 - bit
        upper = (local_index >> bit) & 1
        keep = lax.dynamic_slice_in_dim(array, upper, 1, axis)
        return keep, lax.dynamic_slice_in_dim(array, 1 - upper, 1, axis)

    halves = [lax.slice_in_dim(expert_partial, i, i + 1, axis=2) for i in (0, 1)]
    keep, send = [
        jnp.concatenate([lax.dynamic_slice_in_dim(h, bit ^ i, 1, 3) for i, h in enumerate(halves)], axis=2)
        for bit in (own_half, 1 - own_half)
    ]
    keep, send, other_both = lax.optimization_barrier((keep, send, other_both))
    expert_got = flip_local(send, 0)

    other_before = gate_up(pair_of, streams, gain_column, (other_both,))
    other_hidden, _ = gate_up(pair_of, arrived, gain_column, (other_both,), other_before)
    down_piece = jnp.concatenate([down_piece, down_other], axis=0)
    parts = down(pair_of, other_of, dense_down, down_piece, own_hidden, other_hidden)
    sent, sums = parts[:3], parts[3:]
    arrived = [flip_local(sent[s], 1 + STREAMS[s][0]) for s in range(3)]
    expert_got, _ = lax.optimization_barrier((expert_got, sums))
    for step in (1, 2):
        keep, send = halve(add_pair(keep, expert_got), 4 - step)
        expert_got = flip_local(send, 4 - step)
        if step == 2:
            arrived, expert_got = lax.optimization_barrier((arrived, expert_got))
        half = sums[0].shape[0] // 2
        came = [flip_local(add_pair(sums[s][half:], arrived[s][half:]), 1 + STREAMS[s][step]) for s in range(3)]
        sums = [add_pair(sums[s][:half], arrived[s][:half]) for s in range(3)]
        arrived = came
    keep, send = halve(add_pair(keep, expert_got), 1)
    expert_got = flip_local(send, 1)
    sums = [add_pair(sums[s], arrived[s]) for s in range(3)]
    pair_sum = jnp.concatenate([sums[s][0] for s in range(3)], axis=0)
    even_rows, odd_rows = pair_sum[:slice_width], pair_sum[slice_width:]
    mine = jnp.where(odd, odd_rows, even_rows)
    got = flip_local(jnp.where(odd, even_rows, odd_rows), 0)
    expert_out = add_pair(keep, expert_got).reshape(slice_width, slot_count).T
    returned = lax.all_to_all(
        expert_out.reshape(node_count, NODE_CAP, slice_width), "node", split_axis=0, concat_axis=0, tiled=True
    ).reshape(slot_count, slice_width)
    route_term = (slot_gate[:, None] * returned.astype(jnp.float32)).astype(jnp.bfloat16)
    expert_part = lax.dot_general(
        route_term, chosen, (((0,), (1,)), ((), ())), preferred_element_type=jnp.float32
    )
    dense_part = jnp.where(
        own_half == 1, jnp.concatenate([got, mine], axis=1), jnp.concatenate([mine, got], axis=1)
    ).astype(jnp.float32)
    return (columns.astype(jnp.float32) + dense_part + expert_part).astype(jnp.bfloat16).T


def solution(mesh):
    return jax.shard_map(
        shards,
        mesh=mesh,
        in_specs=(
            P("node", "local"),
            P(),
            P(None, "local"),
            P(None, "local"),
            P("local", None),
            P("node", None, "local"),
            P("node", None, "local"),
            P("node", "local", None),
            P("node", None),
            P("node", None),
        ),
        out_specs=P("node", "local"),
        check_vma=False,
    )
```

```python
import functools

import jax
import jax.numpy as jnp
from jax import lax
from jax.experimental import pallas as pl
from jax.experimental.pallas import tpu as pltpu
from jax.sharding import PartitionSpec as P

EPSILON = 1e-05
NODE_CAP = 16
GRAY = (0, 1, 3, 2)

LOCAL_LABEL = [GRAY[i % 4] | GRAY[i // 4] << 2 for i in range(16)]
LOCAL_AT = {label: i for i, label in enumerate(LOCAL_LABEL)}

STREAMS = ((0, 1, 2, 3), (1, 2, 3, 0), (2, 3, 0, 1), (3, 0, 1, 2))


def flip_local(array, bit):
    return lax.ppermute(array, "local", [(i, LOCAL_AT[LOCAL_LABEL[i] ^ (1 << bit)]) for i in range(16)])


def route_slots(ids_block, window):
    flat_ids = ids_block.reshape(-1)
    expert_range = jnp.arange(window, dtype=jnp.int32)
    member = (flat_ids[:, None] == expert_range[None, :]).astype(jnp.int32)
    before = jnp.cumsum(member, axis=0) - member
    route_rank = jnp.sum(before * member, axis=1)
    kept = (jnp.sum(member, axis=1) > 0) & (route_rank < NODE_CAP)
    slot = jnp.where(kept, flat_ids * NODE_CAP + route_rank, -1)
    return slot.reshape(ids_block.shape)


def transposed_dot(weight, rows):
    return lax.dot_general(weight, rows, (((0,), (0,)), ((), ())), preferred_element_type=jnp.float32)


def silu(value):
    return value / (1.0 + jnp.exp(-value))


def gate_up_kernel(features, weight_ref, x_ref, hidden_ref, total, squares):
    step = pl.program_id(0)
    as_float = x_ref[...].astype(jnp.float32)
    square_sum = jnp.sum(as_float * as_float, axis=0, keepdims=True)
    part = jnp.dot(weight_ref[...], x_ref[...], preferred_element_type=jnp.float32)

    @pl.when(step == 0)
    def _():
        total[...] = part
        squares[...] = square_sum

    @pl.when(step > 0)
    def _():
        total[...] += part
        squares[...] += square_sum

    @pl.when(step == pl.num_programs(0) - 1)
    def _():
        scale = lax.rsqrt(squares[...] / features + EPSILON)
        half = total.shape[0] // 2
        hidden_ref[...] = (silu(total[:half] * scale) * (total[half:] * scale)).astype(jnp.bfloat16)


def gate_up(weight, rows):
    both, features = weight.shape
    columns = rows.shape[1]
    deep = 1024
    return pl.pallas_call(
        functools.partial(gate_up_kernel, features),
        grid=(features // deep,),
        in_specs=[pl.BlockSpec((both, deep), lambda m: (0, m)), pl.BlockSpec((deep, columns), lambda m: (m, 0))],
        out_specs=pl.BlockSpec((both // 2, columns), lambda m: (0, 0)),
        out_shape=jax.ShapeDtypeStruct((both // 2, columns), jnp.bfloat16),
        scratch_shapes=[pltpu.VMEM((both, columns), jnp.float32), pltpu.VMEM((1, columns), jnp.float32)],
        compiler_params=pltpu.CompilerParams(vmem_limit_bytes=56 << 20),
        cost_estimate=pl.CostEstimate(
            flops=2 * features * columns * both, bytes_accessed=2 * features * (columns + both), transcendentals=0
        ),
    )(weight, rows)


def down_kernel(slice_ref, *refs):
    weights, hidden_ref, outs = refs[:4], refs[4], refs[5:]
    columns = outs[0].shape[-1]
    for s in range(4):
        part = jnp.dot(
            weights[s][0], hidden_ref[:, s * columns : (s + 1) * columns], preferred_element_type=jnp.float32
        )
        outs[s][0] = part.astype(jnp.bfloat16)


def down(slice_of, weight, hidden, sent):
    blocks, rows, deep = weight.shape
    columns = hidden.shape[1] // 4

    def weight_spec(s):
        a, b, c, d = STREAMS[s]

        def index(j, at):
            return at[sent << a | ((j >> 2) & 1) << b | ((j >> 1) & 1) << c | (j & 1) << d], 0, 0

        return pl.BlockSpec((1, rows, deep), index)

    return pl.pallas_call(
        down_kernel,
        grid_spec=pltpu.PrefetchScalarGridSpec(
            num_scalar_prefetch=1,
            grid=(blocks // 2,),
            in_specs=[weight_spec(s) for s in range(4)] + [pl.BlockSpec(hidden.shape, lambda j, at: (0, 0))],
            out_specs=[pl.BlockSpec((1, rows, columns), lambda j, at: (j, 0, 0))] * 4,
        ),
        out_shape=[jax.ShapeDtypeStruct((blocks // 2, rows, columns), jnp.bfloat16)] * 4,
        compiler_params=pltpu.CompilerParams(vmem_limit_bytes=24 << 20),
        cost_estimate=pl.CostEstimate(
            flops=4 * blocks * rows * deep * columns, bytes_accessed=4 * blocks * rows * (deep + columns), transcendentals=0
        ),
    )(slice_of, *[weight] * 4, hidden)


def expert_kernel(blocks, features, at_ref, x_ref, gate_ref, up_ref, gain_ref, hidden_ref, gate_total, up_total, squares):
    step = pl.program_id(0)

    @pl.when(step == 0)
    def _():
        gate_total[...] = jnp.zeros_like(gate_total)
        up_total[...] = jnp.zeros_like(up_total)
        squares[...] = jnp.zeros_like(squares)

    as_float = x_ref[0].astype(jnp.float32)
    squares[...] += jnp.sum(as_float * as_float, axis=0, keepdims=True)
    rows = (as_float * gain_ref[...]).astype(jnp.bfloat16)
    gate_total[...] += transposed_dot(gate_ref[0], rows)
    up_total[...] += transposed_dot(up_ref[0], rows)

    @pl.when(step == blocks - 1)
    def _():
        scale = lax.rsqrt(squares[...] / features + EPSILON)
        hidden_ref[...] = (silu(gate_total[...] * scale) * (up_total[...] * scale)).astype(jnp.bfloat16)


def expert_gate_up(slice_of, pooled, gate_weight, up_weight, gain_column):
    blocks, rows, columns = pooled.shape
    hidden = gate_weight.shape[-1]
    weight_spec = pl.BlockSpec((1, rows, hidden), lambda m, at: (0, at[m], 0))
    return pl.pallas_call(
        functools.partial(expert_kernel, blocks, blocks * rows),
        grid_spec=pltpu.PrefetchScalarGridSpec(
            num_scalar_prefetch=1,
            grid=(blocks,),
            in_specs=[
                pl.BlockSpec((1, rows, columns), lambda m, at: (m, 0, 0)),
                weight_spec,
                weight_spec,
                pl.BlockSpec((rows, 1), lambda m, at: (at[m], 0)),
            ],
            out_specs=pl.BlockSpec((hidden, columns), lambda m, at: (0, 0)),
            scratch_shapes=[
                pltpu.VMEM((hidden, columns), jnp.float32),
                pltpu.VMEM((hidden, columns), jnp.float32),
                pltpu.VMEM((1, columns), jnp.float32),
            ],
        ),
        out_shape=jax.ShapeDtypeStruct((hidden, columns), jnp.bfloat16),
        compiler_params=pltpu.CompilerParams(vmem_limit_bytes=24 << 20),
        cost_estimate=pl.CostEstimate(
            flops=4 * blocks * rows * columns * hidden,
            bytes_accessed=2 * blocks * rows * (columns + 2 * hidden),
            transcendentals=0,
        ),
    )(slice_of, pooled, gate_weight, up_weight, gain_column)


def add_pair(kept, got):
    return (kept.astype(jnp.float32) + got.astype(jnp.float32)).astype(jnp.bfloat16)


def shards(
    tokens,
    norm_gain,
    dense_gate,
    dense_up,
    dense_down,
    expert_gate,
    expert_up,
    expert_down,
    expert_ids,
    route_gates,
):
    node_count = lax.axis_size("node")
    local_index = lax.axis_index("local")
    slice_width = tokens.shape[1]
    slot_count = node_count * NODE_CAP
    slice_table = [[LOCAL_AT[LOCAL_LABEL[i] ^ m] for m in range(16)] for i in range(16)]
    slice_of = jnp.asarray(slice_table, jnp.int32)[local_index]

    columns = tokens.T
    whole_columns = lax.all_gather(columns, "local", axis=0, tiled=True)

    slot = route_slots(expert_ids, node_count)
    slot_range = jnp.arange(slot_count, dtype=jnp.int32)
    match_float = (slot[:, :, None] == slot_range[None, None, :]).astype(jnp.float32)
    chosen = jnp.sum(match_float, axis=1).astype(jnp.bfloat16)
    slot_gate = jnp.sum(match_float * route_gates[:, :, None], axis=(0, 1))
    send_rows = lax.dot_general(
        chosen, tokens, (((0,), (0,)), ((), ())), preferred_element_type=jnp.float32
    ).astype(jnp.bfloat16)
    pooled = lax.all_to_all(
        send_rows.reshape(node_count, NODE_CAP, slice_width), "node", split_axis=0, concat_axis=0, tiled=True
    )
    pooled = pooled.reshape(slot_count, slice_width).T[None]

    gain_column = norm_gain[:, None]
    for bit in range(4):
        got = flip_local(pooled, bit)
        if bit == 1:
            dense_gate, dense_up, _ = lax.optimization_barrier((dense_gate, dense_up, pooled))
            weight = jnp.concatenate(
                [(w.astype(jnp.float32) * gain_column).astype(jnp.bfloat16).T for w in (dense_gate, dense_up)], axis=0
            )
            got, weight = lax.optimization_barrier((got, weight))
        if bit == 2:
            dense_down, _ = lax.optimization_barrier((dense_down, pooled))
            turned_down = dense_down.T.reshape(16, slice_width, dense_down.shape[0])
            got, turned_down = lax.optimization_barrier((got, turned_down))
        pooled = jnp.concatenate([pooled, got], axis=0)
    expert_hidden = expert_gate_up(slice_of, pooled, expert_gate, expert_up, gain_column)
    expert_partial = transposed_dot(expert_down[0], expert_hidden).astype(jnp.bfloat16)
    expert_partial = expert_partial.reshape(16, slice_width, slot_count)

    def halve(array, bit):
        half = 1 << bit
        upper = (local_index >> bit) & 1
        keep = lax.dynamic_slice_in_dim(array, upper * half, half, 0)
        return keep, lax.dynamic_slice_in_dim(array, (1 - upper) * half, half, 0)

    keep, send = halve(expert_partial, 3)
    keep, send, whole_columns = lax.optimization_barrier((keep, send, whole_columns))
    expert_got = flip_local(send, 3)

    hidden = gate_up(weight, whole_columns)
    hidden, expert_got = lax.optimization_barrier((hidden, expert_got))
    keep, send = halve(add_pair(keep, expert_got), 2)
    expert_got = flip_local(send, 2)
    sent = down(slice_of, turned_down, hidden, 1)
    arrived = [flip_local(sent[s], STREAMS[s][0]) for s in range(4)]
    hidden, _ = lax.optimization_barrier((hidden, sent))
    sums = down(slice_of, turned_down, hidden, 0)
    expert_got, sums = lax.optimization_barrier((expert_got, sums))
    for step in (1, 2, 3):
        if step < 3:
            keep, send = halve(add_pair(keep, expert_got), 2 - step)
            expert_got = flip_local(send, 2 - step)
        half = sums[0].shape[0] // 2
        came = [flip_local(add_pair(sums[s][half:], arrived[s][half:]), STREAMS[s][step]) for s in range(4)]
        sums = [add_pair(sums[s][:half], arrived[s][:half]) for s in range(4)]
        arrived = came
        if step == 1:
            sums, expert_got = lax.optimization_barrier((sums, expert_got))
        if step == 2:
            expert_out = add_pair(keep, expert_got)[0].T
            returned = lax.all_to_all(
                expert_out.reshape(node_count, NODE_CAP, slice_width), "node", split_axis=0, concat_axis=0, tiled=True
            ).reshape(slot_count, slice_width)
            route_term = (slot_gate[:, None] * returned.astype(jnp.float32)).astype(jnp.bfloat16)
            arrived[3], route_term = lax.optimization_barrier((arrived[3], route_term))
    expert_part = lax.dot_general(
        route_term, chosen, (((0,), (1,)), ((), ())), preferred_element_type=jnp.float32
    )
    dense_part = jnp.concatenate(
        [sums[s][0].astype(jnp.float32) + arrived[s][0].astype(jnp.float32) for s in range(4)], axis=1
    )
    return (columns.astype(jnp.float32) + dense_part + expert_part).astype(jnp.bfloat16).T


def solution(mesh):
    return jax.shard_map(
        shards,
        mesh=mesh,
        in_specs=(
            P("node", "local"),
            P(),
            P(None, "local"),
            P(None, "local"),
            P("local", None),
            P("node", None, "local"),
            P("node", None, "local"),
            P("node", "local", None),
            P("node", None),
            P("node", None),
        ),
        out_specs=P("node", "local"),
        check_vma=False,
    )
```

```python
import functools

import jax
import jax.numpy as jnp
from jax import lax
from jax.experimental import pallas as pl
from jax.experimental.pallas import tpu as pltpu
from jax.sharding import PartitionSpec as P

EPSILON = 1e-05
NODE_CAP = 16
GRAY = (0, 1, 3, 2)

LOCAL_LABEL = [GRAY[i % 4] | GRAY[i // 4] << 2 for i in range(16)]
LOCAL_AT = {label: i for i, label in enumerate(LOCAL_LABEL)}

STREAMS = ((0, 1, 2, 3), (1, 2, 3, 0), (2, 3, 0, 1), (3, 0, 1, 2))


def flip_local(array, bit):
    return lax.ppermute(array, "local", [(i, LOCAL_AT[LOCAL_LABEL[i] ^ (1 << bit)]) for i in range(16)])


def route_slots(ids_block, window):
    flat_ids = ids_block.reshape(-1)
    expert_range = jnp.arange(window, dtype=jnp.int32)
    member = (flat_ids[:, None] == expert_range[None, :]).astype(jnp.int32)
    before = jnp.cumsum(member, axis=0) - member
    route_rank = jnp.sum(before * member, axis=1)
    kept = (jnp.sum(member, axis=1) > 0) & (route_rank < NODE_CAP)
    slot = jnp.where(kept, flat_ids * NODE_CAP + route_rank, -1)
    return slot.reshape(ids_block.shape)


def transposed_dot(weight, rows):
    return lax.dot_general(weight, rows, (((0,), (0,)), ((), ())), preferred_element_type=jnp.float32)


def silu(value):
    return value / (1.0 + jnp.exp(-value))


def quarter_kernel(masks, deep, slice_ref, weight_ref, turned_ref, x_ref, scale_ref, hidden_ref, sent_ref, total):
    step = pl.program_id(0)
    here = pl.ds(pl.multiple_of(step * deep, 128), deep)
    part = jnp.dot(weight_ref[:, here], x_ref[...], preferred_element_type=jnp.float32)

    @pl.when(step == 0)
    def _():
        total[...] = part

    @pl.when(step > 0)
    def _():
        total[...] += part

    @pl.when(step == pl.num_programs(0) - 1)
    def _():
        scale = scale_ref[...]
        half = total.shape[0] // 2
        hidden = (silu(total[:half] * scale) * (total[half:] * scale)).astype(jnp.bfloat16)
        hidden_ref[...] = hidden
        for j, mask in enumerate(masks):
            out = jnp.dot(turned_ref[slice_ref[mask]], hidden, preferred_element_type=jnp.float32)
            sent_ref[j] = out.astype(jnp.bfloat16)


def stream_masks(s, sent):
    a, b, c, d = STREAMS[s]
    return [sent << a | ((j >> 2) & 1) << b | ((j >> 1) & 1) << c | (j & 1) << d for j in range(8)]


def quarter(s, slice_of, weight, turned, rows, scale):
    both, features = weight.shape
    columns = rows.shape[1] // 4
    blocks, slice_rows, _ = turned.shape
    deep = features // 4
    return pl.pallas_call(
        functools.partial(quarter_kernel, stream_masks(s, 1), deep),
        grid_spec=pltpu.PrefetchScalarGridSpec(
            num_scalar_prefetch=1,
            grid=(features // deep,),
            in_specs=[
                pl.BlockSpec(memory_space=pltpu.VMEM),
                pl.BlockSpec(memory_space=pltpu.VMEM),
                pl.BlockSpec((deep, columns), lambda m, at: (m, s)),
                pl.BlockSpec((1, columns), lambda m, at: (0, s)),
            ],
            out_specs=[
                pl.BlockSpec((both // 2, columns), lambda m, at: (0, 0)),
                pl.BlockSpec((blocks // 2, slice_rows, columns), lambda m, at: (0, 0, 0)),
            ],
            scratch_shapes=[pltpu.VMEM((both, columns), jnp.float32)],
        ),
        out_shape=[
            jax.ShapeDtypeStruct((both // 2, columns), jnp.bfloat16),
            jax.ShapeDtypeStruct((blocks // 2, slice_rows, columns), jnp.bfloat16),
        ],
        compiler_params=pltpu.CompilerParams(vmem_limit_bytes=36 << 20),
        cost_estimate=pl.CostEstimate(
            flops=3 * features * columns * both, bytes_accessed=2 * features * (columns + both), transcendentals=0
        ),
    )(slice_of, weight, turned, rows, scale)


def keep_kernel(slice_ref, *refs):
    weights, hidden, outs = refs[:4], refs[4:8], refs[8:]
    for s in range(4):
        outs[s][0] = jnp.dot(weights[s][0], hidden[s][...], preferred_element_type=jnp.float32).astype(jnp.bfloat16)


def kept_parts(slice_of, turned, hidden):
    blocks, rows, deep = turned.shape
    columns = hidden[0].shape[1]

    def weight_spec(s):
        a, b, c, d = STREAMS[s]
        return pl.BlockSpec(
            (1, rows, deep), lambda j, at: (at[((j >> 2) & 1) << b | ((j >> 1) & 1) << c | (j & 1) << d], 0, 0)
        )

    return pl.pallas_call(
        keep_kernel,
        grid_spec=pltpu.PrefetchScalarGridSpec(
            num_scalar_prefetch=1,
            grid=(blocks // 2,),
            in_specs=[weight_spec(s) for s in range(4)] + [pl.BlockSpec((deep, columns), lambda j, at: (0, 0))] * 4,
            out_specs=[pl.BlockSpec((1, rows, columns), lambda j, at: (j, 0, 0))] * 4,
        ),
        out_shape=[jax.ShapeDtypeStruct((blocks // 2, rows, columns), jnp.bfloat16)] * 4,
        compiler_params=pltpu.CompilerParams(vmem_limit_bytes=24 << 20),
        cost_estimate=pl.CostEstimate(
            flops=4 * blocks * rows * deep * columns, bytes_accessed=4 * blocks * rows * (deep + columns), transcendentals=0
        ),
    )(slice_of, *[turned] * 4, *hidden)


def expert_kernel(blocks, features, at_ref, x_ref, gate_ref, up_ref, gain_ref, hidden_ref, gate_total, up_total, squares):
    step = pl.program_id(0)

    @pl.when(step == 0)
    def _():
        gate_total[...] = jnp.zeros_like(gate_total)
        up_total[...] = jnp.zeros_like(up_total)
        squares[...] = jnp.zeros_like(squares)

    as_float = x_ref[0].astype(jnp.float32)
    squares[...] += jnp.sum(as_float * as_float, axis=0, keepdims=True)
    rows = (as_float * gain_ref[...]).astype(jnp.bfloat16)
    gate_total[...] += transposed_dot(gate_ref[0], rows)
    up_total[...] += transposed_dot(up_ref[0], rows)

    @pl.when(step == blocks - 1)
    def _():
        scale = lax.rsqrt(squares[...] / features + EPSILON)
        hidden_ref[...] = (silu(gate_total[...] * scale) * (up_total[...] * scale)).astype(jnp.bfloat16)


def expert_gate_up(slice_of, pooled, gate_weight, up_weight, gain_column):
    blocks, rows, columns = pooled.shape
    hidden = gate_weight.shape[-1]
    weight_spec = pl.BlockSpec((1, rows, hidden), lambda m, at: (0, at[m], 0))
    return pl.pallas_call(
        functools.partial(expert_kernel, blocks, blocks * rows),
        grid_spec=pltpu.PrefetchScalarGridSpec(
            num_scalar_prefetch=1,
            grid=(blocks,),
            in_specs=[
                pl.BlockSpec((1, rows, columns), lambda m, at: (m, 0, 0)),
                weight_spec,
                weight_spec,
                pl.BlockSpec((rows, 1), lambda m, at: (at[m], 0)),
            ],
            out_specs=pl.BlockSpec((hidden, columns), lambda m, at: (0, 0)),
            scratch_shapes=[
                pltpu.VMEM((hidden, columns), jnp.float32),
                pltpu.VMEM((hidden, columns), jnp.float32),
                pltpu.VMEM((1, columns), jnp.float32),
            ],
        ),
        out_shape=jax.ShapeDtypeStruct((hidden, columns), jnp.bfloat16),
        compiler_params=pltpu.CompilerParams(vmem_limit_bytes=24 << 20),
        cost_estimate=pl.CostEstimate(
            flops=4 * blocks * rows * columns * hidden,
            bytes_accessed=2 * blocks * rows * (columns + 2 * hidden),
            transcendentals=0,
        ),
    )(slice_of, pooled, gate_weight, up_weight, gain_column)


def add_pair(kept, got):
    return (kept.astype(jnp.float32) + got.astype(jnp.float32)).astype(jnp.bfloat16)


def shards(
    tokens,
    norm_gain,
    dense_gate,
    dense_up,
    dense_down,
    expert_gate,
    expert_up,
    expert_down,
    expert_ids,
    route_gates,
):
    node_count = lax.axis_size("node")
    local_index = lax.axis_index("local")
    slice_width = tokens.shape[1]
    width = slice_width * 16
    slot_count = node_count * NODE_CAP
    slice_table = [[LOCAL_AT[LOCAL_LABEL[i] ^ m] for m in range(16)] for i in range(16)]
    slice_of = jnp.asarray(slice_table, jnp.int32)[local_index]

    columns = tokens.T
    whole_columns = lax.all_gather(columns, "local", axis=0, tiled=True)

    slot = route_slots(expert_ids, node_count)
    slot_range = jnp.arange(slot_count, dtype=jnp.int32)
    match_float = (slot[:, :, None] == slot_range[None, None, :]).astype(jnp.float32)
    chosen = jnp.sum(match_float, axis=1).astype(jnp.bfloat16)
    slot_gate = jnp.sum(match_float * route_gates[:, :, None], axis=(0, 1))
    send_rows = lax.dot_general(
        chosen, tokens, (((0,), (0,)), ((), ())), preferred_element_type=jnp.float32
    ).astype(jnp.bfloat16)
    routed = lax.all_to_all(
        send_rows.reshape(node_count, NODE_CAP, slice_width), "node", split_axis=0, concat_axis=0, tiled=True
    )
    routed = routed.reshape(slot_count, slice_width).T

    as_float = columns.astype(jnp.float32)
    square_sum = lax.psum(jnp.sum(as_float * as_float, axis=0), "local")
    scale = lax.rsqrt(square_sum / width + EPSILON)[None, :]
    gain_column = norm_gain[:, None]
    weight = jnp.concatenate(
        [(w.astype(jnp.float32) * gain_column).astype(jnp.bfloat16).T for w in (dense_gate, dense_up)], axis=0
    )
    turned = dense_down.T.reshape(16, slice_width, dense_down.shape[0])
    weight, turned, scale, routed, whole_columns = lax.optimization_barrier(
        (weight, turned, scale, routed, whole_columns)
    )
    pooled = lax.all_gather(routed, "local", axis=0, tiled=True)

    quarters = [quarter(s, slice_of, weight, turned, whole_columns, scale) for s in range(4)]
    arrived = [flip_local(quarters[s][1], STREAMS[s][0]) for s in range(4)]
    sums = kept_parts(slice_of, turned, [q[0] for q in quarters])

    pooled, sums = lax.optimization_barrier((pooled, sums))
    expert_hidden = expert_gate_up(
        jnp.arange(16, dtype=jnp.int32), pooled.reshape(16, slice_width, slot_count), expert_gate, expert_up, gain_column
    )
    expert_partial = transposed_dot(expert_down[0], expert_hidden).astype(jnp.bfloat16)
    expert_partial, arrived[0] = lax.optimization_barrier((expert_partial, arrived[0]))
    expert_out = lax.psum_scatter(expert_partial, "local", scatter_dimension=0, tiled=True)
    for step in (1, 2, 3):
        half = sums[0].shape[0] // 2
        came = [flip_local(add_pair(sums[s][half:], arrived[s][half:]), STREAMS[s][step]) for s in range(4)]
        sums = [add_pair(sums[s][:half], arrived[s][:half]) for s in range(4)]
        arrived = came
    returned = lax.all_to_all(
        expert_out.T.reshape(node_count, NODE_CAP, slice_width), "node", split_axis=0, concat_axis=0, tiled=True
    ).reshape(slot_count, slice_width)
    route_term = (slot_gate[:, None] * returned.astype(jnp.float32)).astype(jnp.bfloat16)
    expert_part = lax.dot_general(
        route_term, chosen, (((0,), (1,)), ((), ())), preferred_element_type=jnp.float32
    )
    dense_part = jnp.concatenate(
        [sums[s][0].astype(jnp.float32) + arrived[s][0].astype(jnp.float32) for s in range(4)], axis=1
    )
    return (columns.astype(jnp.float32) + dense_part + expert_part).astype(jnp.bfloat16).T


def solution(mesh):
    return jax.shard_map(
        shards,
        mesh=mesh,
        in_specs=(
            P("node", "local"),
            P(),
            P(None, "local"),
            P(None, "local"),
            P("local", None),
            P("node", None, "local"),
            P("node", None, "local"),
            P("node", "local", None),
            P("node", None),
            P("node", None),
        ),
        out_specs=P("node", "local"),
        check_vma=False,
    )
```

```python
import functools

import jax
import jax.numpy as jnp
from jax import lax
from jax.experimental import pallas as pl
from jax.experimental.pallas import tpu as pltpu
from jax.sharding import PartitionSpec as P

EPSILON = 1e-05
NODE_CAP = 16
GRAY = (0, 1, 3, 2)

LOCAL_LABEL = [GRAY[i % 4] | GRAY[i // 4] << 2 for i in range(16)]
LOCAL_AT = {label: i for i, label in enumerate(LOCAL_LABEL)}

STREAMS = ((0, 1, 2, 3), (1, 2, 3, 0), (2, 3, 0, 1), (3, 0, 1, 2))


def flip_local(array, bit):
    return lax.ppermute(array, "local", [(i, LOCAL_AT[LOCAL_LABEL[i] ^ (1 << bit)]) for i in range(16)])


def route_slots(ids_block, window):
    flat_ids = ids_block.reshape(-1)
    expert_range = jnp.arange(window, dtype=jnp.int32)
    member = (flat_ids[:, None] == expert_range[None, :]).astype(jnp.int32)
    before = jnp.cumsum(member, axis=0) - member
    route_rank = jnp.sum(before * member, axis=1)
    kept = (jnp.sum(member, axis=1) > 0) & (route_rank < NODE_CAP)
    slot = jnp.where(kept, flat_ids * NODE_CAP + route_rank, -1)
    return slot.reshape(ids_block.shape)


def transposed_dot(weight, rows):
    return lax.dot_general(weight, rows, (((0,), (0,)), ((), ())), preferred_element_type=jnp.float32)


def silu(value):
    return value / (1.0 + jnp.exp(-value))


def send_kernel(first, slice_ref, gate_up_ref, scale_ref, turned_ref, hidden_ref, *outs):
    step = pl.program_id(0)

    @pl.when(step == 0)
    def _():
        half = gate_up_ref.shape[0] // 2
        scale = scale_ref[...]
        hidden_ref[...] = (silu(gate_up_ref[:half] * scale) * (gate_up_ref[half:] * scale)).astype(jnp.bfloat16)

    columns = outs[0].shape[-1]
    for i, out in enumerate(outs):
        at = slice_ref[stream_mask(first + i, 1, step)]
        hidden = hidden_ref[:, i * columns : (i + 1) * columns]
        out[0] = jnp.dot(turned_ref[at], hidden, preferred_element_type=jnp.float32).astype(jnp.bfloat16)


def stream_mask(s, sent, j):
    a, b, c, d = STREAMS[s]
    return sent << a | ((j >> 2) & 1) << b | ((j >> 1) & 1) << c | (j & 1) << d


def sent_parts(first, slice_of, gate_up, scale, turned):
    both = gate_up.shape[0]
    columns = gate_up.shape[1] // 4
    blocks, slice_rows, deep = turned.shape
    pair = first // 2
    return pl.pallas_call(
        functools.partial(send_kernel, first),
        grid_spec=pltpu.PrefetchScalarGridSpec(
            num_scalar_prefetch=1,
            grid=(blocks // 2,),
            in_specs=[
                pl.BlockSpec((both, 2 * columns), lambda j, at: (0, pair)),
                pl.BlockSpec((1, 2 * columns), lambda j, at: (0, pair)),
                pl.BlockSpec(memory_space=pltpu.VMEM),
            ],
            out_specs=[pl.BlockSpec((deep, 2 * columns), lambda j, at: (0, 0))]
            + [pl.BlockSpec((1, slice_rows, columns), lambda j, at: (j, 0, 0))] * 2,
        ),
        out_shape=[jax.ShapeDtypeStruct((deep, 2 * columns), jnp.bfloat16)]
        + [jax.ShapeDtypeStruct((blocks // 2, slice_rows, columns), jnp.bfloat16)] * 2,
        compiler_params=pltpu.CompilerParams(vmem_limit_bytes=24 << 20),
        cost_estimate=pl.CostEstimate(
            flops=2 * blocks * slice_rows * deep * columns,
            bytes_accessed=2 * blocks * slice_rows * (deep + columns),
            transcendentals=0,
        ),
    )(slice_of, gate_up, scale, turned)


def keep_kernel(slice_ref, *refs):
    weights, hidden, outs = refs[:4], refs[4:6], refs[6:]
    columns = outs[0].shape[-1]
    for s in range(4):
        rows = hidden[s // 2][:, s % 2 * columns : (s % 2 + 1) * columns]
        outs[s][0] = jnp.dot(weights[s][0], rows, preferred_element_type=jnp.float32).astype(jnp.bfloat16)


def kept_parts(slice_of, turned, hidden):
    blocks, rows, deep = turned.shape
    columns = hidden[0].shape[1] // 2

    def weight_spec(s):
        return pl.BlockSpec((1, rows, deep), lambda j, at: (at[stream_mask(s, 0, j)], 0, 0))

    return pl.pallas_call(
        keep_kernel,
        grid_spec=pltpu.PrefetchScalarGridSpec(
            num_scalar_prefetch=1,
            grid=(blocks // 2,),
            in_specs=[weight_spec(s) for s in range(4)] + [pl.BlockSpec((deep, 2 * columns), lambda j, at: (0, 0))] * 2,
            out_specs=[pl.BlockSpec((1, rows, columns), lambda j, at: (j, 0, 0))] * 4,
        ),
        out_shape=[jax.ShapeDtypeStruct((blocks // 2, rows, columns), jnp.bfloat16)] * 4,
        compiler_params=pltpu.CompilerParams(vmem_limit_bytes=24 << 20),
        cost_estimate=pl.CostEstimate(
            flops=4 * blocks * rows * deep * columns, bytes_accessed=4 * blocks * rows * (deep + columns), transcendentals=0
        ),
    )(slice_of, *[turned] * 4, *hidden)


def expert_kernel(blocks, features, at_ref, x0, x1, x2, x3, gate_ref, up_ref, gain_ref, hidden_ref, gate_total, up_total, squares):
    step = pl.program_id(0)

    @pl.when(step == 0)
    def _():
        gate_total[...] = jnp.zeros_like(gate_total)
        up_total[...] = jnp.zeros_like(up_total)
        squares[...] = jnp.zeros_like(squares)

    as_float = jnp.concatenate([x0[0], x1[0], x2[0], x3[0]], axis=0).astype(jnp.float32)
    squares[...] += jnp.sum(as_float * as_float, axis=0, keepdims=True)
    rows = (as_float * gain_ref[...]).astype(jnp.bfloat16)
    gate_total[...] += transposed_dot(gate_ref[0], rows)
    up_total[...] += transposed_dot(up_ref[0], rows)

    @pl.when(step == blocks - 1)
    def _():
        scale = lax.rsqrt(squares[...] / features + EPSILON)
        hidden_ref[...] = (silu(gate_total[...] * scale) * (up_total[...] * scale)).astype(jnp.bfloat16)


def expert_gate_up(slice_of, pooled, gate_weight, up_weight, gain_column):
    blocks, quarter_rows, columns = pooled[0].shape
    rows = 4 * quarter_rows
    hidden = gate_weight.shape[-1]
    weight_spec = pl.BlockSpec((1, rows, hidden), lambda m, at: (0, at[m], 0))

    def stream_spec(s):
        a, b, c, d = STREAMS[s]

        def index(m, at):
            return ((m >> a) & 1) | ((m >> b) & 1) << 1 | ((m >> c) & 1) << 2 | ((m >> d) & 1) << 3, 0, 0

        return pl.BlockSpec((1, quarter_rows, columns), index)

    return pl.pallas_call(
        functools.partial(expert_kernel, blocks, blocks * rows),
        grid_spec=pltpu.PrefetchScalarGridSpec(
            num_scalar_prefetch=1,
            grid=(blocks,),
            in_specs=[stream_spec(s) for s in range(4)]
            + [weight_spec, weight_spec, pl.BlockSpec((rows, 1), lambda m, at: (at[m], 0))],
            out_specs=pl.BlockSpec((hidden, columns), lambda m, at: (0, 0)),
            scratch_shapes=[
                pltpu.VMEM((hidden, columns), jnp.float32),
                pltpu.VMEM((hidden, columns), jnp.float32),
                pltpu.VMEM((1, columns), jnp.float32),
            ],
        ),
        out_shape=jax.ShapeDtypeStruct((hidden, columns), jnp.bfloat16),
        compiler_params=pltpu.CompilerParams(vmem_limit_bytes=24 << 20),
        cost_estimate=pl.CostEstimate(
            flops=4 * blocks * rows * columns * hidden,
            bytes_accessed=2 * blocks * rows * (columns + 2 * hidden),
            transcendentals=0,
        ),
    )(slice_of, *pooled, gate_weight, up_weight, gain_column)


def add_pair(kept, got):
    return (kept.astype(jnp.float32) + got.astype(jnp.float32)).astype(jnp.bfloat16)


def shards(
    tokens,
    norm_gain,
    dense_gate,
    dense_up,
    dense_down,
    expert_gate,
    expert_up,
    expert_down,
    expert_ids,
    route_gates,
):
    node_count = lax.axis_size("node")
    local_index = lax.axis_index("local")
    slice_width = tokens.shape[1]
    width = slice_width * 16
    slot_count = node_count * NODE_CAP
    slice_table = [[LOCAL_AT[LOCAL_LABEL[i] ^ m] for m in range(16)] for i in range(16)]
    slice_of = jnp.asarray(slice_table, jnp.int32)[local_index]

    columns = tokens.T
    whole_columns = lax.all_gather(columns, "local", axis=0, tiled=True)

    slot = route_slots(expert_ids, node_count)
    slot_range = jnp.arange(slot_count, dtype=jnp.int32)
    match_float = (slot[:, :, None] == slot_range[None, None, :]).astype(jnp.float32)
    chosen = jnp.sum(match_float, axis=1).astype(jnp.bfloat16)
    slot_gate = jnp.sum(match_float * route_gates[:, :, None], axis=(0, 1))
    send_rows = lax.dot_general(
        chosen, tokens, (((0,), (0,)), ((), ())), preferred_element_type=jnp.float32
    ).astype(jnp.bfloat16)
    routed = lax.all_to_all(
        send_rows.reshape(node_count, NODE_CAP, slice_width), "node", split_axis=0, concat_axis=0, tiled=True
    )
    routed = routed.reshape(slot_count, slice_width).T

    as_float = columns.astype(jnp.float32)
    square_sum = jnp.sum(as_float * as_float, axis=0, keepdims=True)
    gain_column = norm_gain[:, None]
    part = slice_width // 4
    pooled = [routed[None, s * part : (s + 1) * part] for s in range(4)]
    for step in range(4):
        got = [flip_local(pooled[s], STREAMS[s][step]) for s in range(4)]
        square_sum = square_sum + flip_local(square_sum, step)
        if step == 1:
            dense_gate, dense_up, _ = lax.optimization_barrier((dense_gate, dense_up, pooled))
            weight = jnp.concatenate(
                [(w.astype(jnp.float32) * gain_column).astype(jnp.bfloat16) for w in (dense_gate, dense_up)], axis=1
            )
            got, weight = lax.optimization_barrier((got, weight))
        if step == 2:
            dense_down, _ = lax.optimization_barrier((dense_down, pooled))
            turned = dense_down.T.reshape(16, slice_width, dense_down.shape[0])
            got, turned = lax.optimization_barrier((got, turned))
        pooled = [jnp.concatenate([pooled[s], got[s]], axis=0) for s in range(4)]
    scale = lax.rsqrt(square_sum / width + EPSILON)

    expert_hidden = expert_gate_up(slice_of, pooled, expert_gate, expert_up, gain_column)
    expert_partial = transposed_dot(expert_down[0], expert_hidden).astype(jnp.bfloat16)
    expert_partial, scale, whole_columns = lax.optimization_barrier((expert_partial, scale, whole_columns))
    expert_out = lax.psum_scatter(expert_partial, "local", scatter_dimension=0, tiled=True)

    gate_up = transposed_dot(weight, whole_columns)
    low_hidden, *sent = sent_parts(0, slice_of, gate_up, scale, turned)
    high_hidden, *more = sent_parts(2, slice_of, gate_up, scale, turned)
    sent += more
    arrived = [flip_local(sent[s], STREAMS[s][0]) for s in range(4)]
    sums = kept_parts(slice_of, turned, (low_hidden, high_hidden))
    for step in (1, 2, 3):
        half = sums[0].shape[0] // 2
        came = [flip_local(add_pair(sums[s][half:], arrived[s][half:]), STREAMS[s][step]) for s in range(4)]
        sums = [add_pair(sums[s][:half], arrived[s][:half]) for s in range(4)]
        arrived = came
        if step == 2:
            arrived[3], expert_out = lax.optimization_barrier((arrived[3], expert_out))
    returned = lax.all_to_all(
        expert_out.T.reshape(node_count, NODE_CAP, slice_width), "node", split_axis=0, concat_axis=0, tiled=True
    ).reshape(slot_count, slice_width)
    route_term = (slot_gate[:, None] * returned.astype(jnp.float32)).astype(jnp.bfloat16)
    expert_part = lax.dot_general(
        route_term, chosen, (((0,), (1,)), ((), ())), preferred_element_type=jnp.float32
    )
    dense_part = jnp.concatenate(
        [sums[s][0].astype(jnp.float32) + arrived[s][0].astype(jnp.float32) for s in range(4)], axis=1
    )
    return (columns.astype(jnp.float32) + dense_part + expert_part).astype(jnp.bfloat16).T


def solution(mesh):
    return jax.shard_map(
        shards,
        mesh=mesh,
        in_specs=(
            P("node", "local"),
            P(),
            P(None, "local"),
            P(None, "local"),
            P("local", None),
            P("node", None, "local"),
            P("node", None, "local"),
            P("node", "local", None),
            P("node", None),
            P("node", None),
        ),
        out_specs=P("node", "local"),
        check_vma=False,
    )
```

```python
import functools

import jax
import jax.numpy as jnp
from jax import lax
from jax.experimental import pallas as pl
from jax.experimental.pallas import tpu as pltpu
from jax.sharding import PartitionSpec as P

EPSILON = 1e-05
NODE_CAP = 16
GRAY = (0, 1, 3, 2)

LOCAL_LABEL = [GRAY[i % 4] | GRAY[i // 4] << 2 for i in range(16)]
LOCAL_AT = {label: i for i, label in enumerate(LOCAL_LABEL)}

STREAMS = ((0, 1, 2, 3), (1, 2, 3, 0), (2, 3, 0, 1), (3, 0, 1, 2))


def flip_local(array, bit):
    return lax.ppermute(array, "local", [(i, LOCAL_AT[LOCAL_LABEL[i] ^ (1 << bit)]) for i in range(16)])


def route_slots(ids_block, window):
    flat_ids = ids_block.reshape(-1)
    expert_range = jnp.arange(window, dtype=jnp.int32)
    member = (flat_ids[:, None] == expert_range[None, :]).astype(jnp.int32)
    before = jnp.cumsum(member, axis=0) - member
    route_rank = jnp.sum(before * member, axis=1)
    kept = (jnp.sum(member, axis=1) > 0) & (route_rank < NODE_CAP)
    slot = jnp.where(kept, flat_ids * NODE_CAP + route_rank, -1)
    return slot.reshape(ids_block.shape)


def transposed_dot(weight, rows):
    return lax.dot_general(weight, rows, (((0,), (0,)), ((), ())), preferred_element_type=jnp.float32)


def silu(value):
    return value / (1.0 + jnp.exp(-value))


def send_kernel(first, slice_ref, gate_up_ref, scale_ref, turned_ref, hidden_ref, *outs):
    half = gate_up_ref.shape[0] // 2
    columns = outs[0].shape[-1]
    for i, out in enumerate(outs):
        here = slice((first + i) * columns, (first + i + 1) * columns)
        scale = scale_ref[:, here]
        hidden = (silu(gate_up_ref[:half, here] * scale) * (gate_up_ref[half:, here] * scale)).astype(jnp.bfloat16)
        hidden_ref[:, i * columns : (i + 1) * columns] = hidden
        for j in range(out.shape[0]):
            at = slice_ref[stream_mask(first + i, 1, j)]
            out[j] = jnp.dot(turned_ref[at], hidden, preferred_element_type=jnp.float32).astype(jnp.bfloat16)


def stream_mask(s, sent, j):
    a, b, c, d = STREAMS[s]
    return sent << a | ((j >> 2) & 1) << b | ((j >> 1) & 1) << c | (j & 1) << d


def sent_parts(first, slice_of, gate_up, scale, turned):
    both = gate_up.shape[0]
    columns = gate_up.shape[1] // 4
    blocks, slice_rows, deep = turned.shape
    in_vmem = pl.BlockSpec(memory_space=pltpu.VMEM)
    return pl.pallas_call(
        functools.partial(send_kernel, first),
        in_specs=[pl.BlockSpec(memory_space=pltpu.SMEM), in_vmem, in_vmem, in_vmem],
        out_specs=[in_vmem] * 3,
        out_shape=[jax.ShapeDtypeStruct((deep, 2 * columns), jnp.bfloat16)]
        + [jax.ShapeDtypeStruct((blocks // 2, slice_rows, columns), jnp.bfloat16)] * 2,
        compiler_params=pltpu.CompilerParams(vmem_limit_bytes=24 << 20),
        cost_estimate=pl.CostEstimate(
            flops=2 * blocks * slice_rows * deep * columns,
            bytes_accessed=2 * blocks * slice_rows * (deep + columns),
            transcendentals=0,
        ),
    )(slice_of, gate_up, scale, turned)


def keep_kernel(slice_ref, *refs):
    weights, hidden, outs = refs[:4], refs[4:6], refs[6:]
    columns = outs[0].shape[-1]
    for s in range(4):
        rows = hidden[s // 2][:, s % 2 * columns : (s % 2 + 1) * columns]
        outs[s][0] = jnp.dot(weights[s][0], rows, preferred_element_type=jnp.float32).astype(jnp.bfloat16)


def kept_parts(slice_of, turned, hidden):
    blocks, rows, deep = turned.shape
    columns = hidden[0].shape[1] // 2

    def weight_spec(s):
        return pl.BlockSpec((1, rows, deep), lambda j, at: (at[stream_mask(s, 0, j)], 0, 0))

    return pl.pallas_call(
        keep_kernel,
        grid_spec=pltpu.PrefetchScalarGridSpec(
            num_scalar_prefetch=1,
            grid=(blocks // 2,),
            in_specs=[weight_spec(s) for s in range(4)] + [pl.BlockSpec((deep, 2 * columns), lambda j, at: (0, 0))] * 2,
            out_specs=[pl.BlockSpec((1, rows, columns), lambda j, at: (j, 0, 0))] * 4,
        ),
        out_shape=[jax.ShapeDtypeStruct((blocks // 2, rows, columns), jnp.bfloat16)] * 4,
        compiler_params=pltpu.CompilerParams(vmem_limit_bytes=24 << 20),
        cost_estimate=pl.CostEstimate(
            flops=4 * blocks * rows * deep * columns, bytes_accessed=4 * blocks * rows * (deep + columns), transcendentals=0
        ),
    )(slice_of, *[turned] * 4, *hidden)


def expert_kernel(blocks, features, at_ref, x0, x1, x2, x3, gate_ref, up_ref, gain_ref, hidden_ref, gate_total, up_total, squares):
    step = pl.program_id(0)

    @pl.when(step == 0)
    def _():
        gate_total[...] = jnp.zeros_like(gate_total)
        up_total[...] = jnp.zeros_like(up_total)
        squares[...] = jnp.zeros_like(squares)

    as_float = jnp.concatenate([x0[0], x1[0], x2[0], x3[0]], axis=0).astype(jnp.float32)
    squares[...] += jnp.sum(as_float * as_float, axis=0, keepdims=True)
    rows = (as_float * gain_ref[...]).astype(jnp.bfloat16)
    gate_total[...] += transposed_dot(gate_ref[0], rows)
    up_total[...] += transposed_dot(up_ref[0], rows)

    @pl.when(step == blocks - 1)
    def _():
        scale = lax.rsqrt(squares[...] / features + EPSILON)
        hidden_ref[...] = (silu(gate_total[...] * scale) * (up_total[...] * scale)).astype(jnp.bfloat16)


def expert_gate_up(slice_of, pooled, gate_weight, up_weight, gain_column):
    blocks, quarter_rows, columns = pooled[0].shape
    rows = 4 * quarter_rows
    hidden = gate_weight.shape[-1]
    weight_spec = pl.BlockSpec((1, rows, hidden), lambda m, at: (0, at[m], 0))

    def stream_spec(s):
        a, b, c, d = STREAMS[s]

        def index(m, at):
            return ((m >> a) & 1) | ((m >> b) & 1) << 1 | ((m >> c) & 1) << 2 | ((m >> d) & 1) << 3, 0, 0

        return pl.BlockSpec((1, quarter_rows, columns), index)

    return pl.pallas_call(
        functools.partial(expert_kernel, blocks, blocks * rows),
        grid_spec=pltpu.PrefetchScalarGridSpec(
            num_scalar_prefetch=1,
            grid=(blocks,),
            in_specs=[stream_spec(s) for s in range(4)]
            + [weight_spec, weight_spec, pl.BlockSpec((rows, 1), lambda m, at: (at[m], 0))],
            out_specs=pl.BlockSpec((hidden, columns), lambda m, at: (0, 0)),
            scratch_shapes=[
                pltpu.VMEM((hidden, columns), jnp.float32),
                pltpu.VMEM((hidden, columns), jnp.float32),
                pltpu.VMEM((1, columns), jnp.float32),
            ],
        ),
        out_shape=jax.ShapeDtypeStruct((hidden, columns), jnp.bfloat16),
        compiler_params=pltpu.CompilerParams(vmem_limit_bytes=24 << 20),
        cost_estimate=pl.CostEstimate(
            flops=4 * blocks * rows * columns * hidden,
            bytes_accessed=2 * blocks * rows * (columns + 2 * hidden),
            transcendentals=0,
        ),
    )(slice_of, *pooled, gate_weight, up_weight, gain_column)


def expert_down_kernel(weight_ref, hidden_ref, out_ref):
    out_ref[...] = transposed_dot(weight_ref[0], hidden_ref[...]).astype(jnp.bfloat16)


def expert_down_parts(weight, hidden):
    _, deep, features = weight.shape
    columns = hidden.shape[1]
    wide = features // 4
    return pl.pallas_call(
        expert_down_kernel,
        grid=(features // wide,),
        in_specs=[
            pl.BlockSpec((1, deep, wide), lambda m: (0, 0, m)),
            pl.BlockSpec((deep, columns), lambda m: (0, 0)),
        ],
        out_specs=pl.BlockSpec((wide, columns), lambda m: (m, 0)),
        out_shape=jax.ShapeDtypeStruct((features, columns), jnp.bfloat16),
        compiler_params=pltpu.CompilerParams(vmem_limit_bytes=24 << 20),
        cost_estimate=pl.CostEstimate(
            flops=2 * features * deep * columns, bytes_accessed=2 * features * (deep + columns), transcendentals=0
        ),
    )(weight, hidden)


def shards(
    tokens,
    norm_gain,
    dense_gate,
    dense_up,
    dense_down,
    expert_gate,
    expert_up,
    expert_down,
    expert_ids,
    route_gates,
):
    node_count = lax.axis_size("node")
    local_index = lax.axis_index("local")
    slice_width = tokens.shape[1]
    width = slice_width * 16
    slot_count = node_count * NODE_CAP
    slice_table = [[LOCAL_AT[LOCAL_LABEL[i] ^ m] for m in range(16)] for i in range(16)]
    slice_of = jnp.asarray(slice_table, jnp.int32)[local_index]

    columns = tokens.T
    whole_columns = lax.all_gather(columns, "local", axis=0, tiled=True)

    slot = route_slots(expert_ids, node_count)
    slot_range = jnp.arange(slot_count, dtype=jnp.int32)
    match_float = (slot[:, :, None] == slot_range[None, None, :]).astype(jnp.float32)
    chosen = jnp.sum(match_float, axis=1).astype(jnp.bfloat16)
    slot_gate = jnp.sum(match_float * route_gates[:, :, None], axis=(0, 1))
    send_rows = lax.dot_general(
        chosen, tokens, (((0,), (0,)), ((), ())), preferred_element_type=jnp.float32
    ).astype(jnp.bfloat16)
    routed = lax.all_to_all(
        send_rows.reshape(node_count, NODE_CAP, slice_width), "node", split_axis=0, concat_axis=0, tiled=True
    )
    routed = routed.reshape(slot_count, slice_width).T

    as_float = columns.astype(jnp.float32)
    square_sum = jnp.sum(as_float * as_float, axis=0, keepdims=True)
    gain_column = norm_gain[:, None]
    part = slice_width // 4
    pooled = [routed[None, s * part : (s + 1) * part] for s in range(4)]
    for step in range(4):
        got = [flip_local(pooled[s], STREAMS[s][step]) for s in range(4)]
        square_sum = square_sum + flip_local(square_sum, step)
        if step == 1:
            dense_gate, dense_up, _ = lax.optimization_barrier((dense_gate, dense_up, pooled))
            weight = jnp.concatenate(
                [(w.astype(jnp.float32) * gain_column).astype(jnp.bfloat16) for w in (dense_gate, dense_up)], axis=1
            )
            got, weight = lax.optimization_barrier((got, weight))
        if step == 2:
            dense_down, _ = lax.optimization_barrier((dense_down, pooled))
            turned = dense_down.T.reshape(16, slice_width, dense_down.shape[0])
            got, turned = lax.optimization_barrier((got, turned))
        pooled = [jnp.concatenate([pooled[s], got[s]], axis=0) for s in range(4)]
    scale = lax.rsqrt(square_sum / width + EPSILON)

    expert_hidden = expert_gate_up(slice_of, pooled, expert_gate, expert_up, gain_column)
    expert_partial = expert_down_parts(expert_down, expert_hidden)
    expert_partial, scale, whole_columns = lax.optimization_barrier((expert_partial, scale, whole_columns))
    expert_out = lax.psum_scatter(expert_partial, "local", scatter_dimension=0, tiled=True)

    gate_up = transposed_dot(weight, whole_columns)
    low_hidden, *sent = sent_parts(0, slice_of, gate_up, scale, turned)
    high_hidden, *more = sent_parts(2, slice_of, gate_up, scale, turned)
    sent += more
    arrived = [flip_local(sent[s], STREAMS[s][0]) for s in range(4)]
    sums = kept_parts(slice_of, turned, (low_hidden, high_hidden))
    terms = [[sums[s], arrived[s]] for s in range(4)]

    def added(s, low, high):
        return sum(term[low:high].astype(jnp.float32) for term in terms[s])

    for step in (1, 2, 3):
        half = 8 >> step
        for s in range(4):
            terms[s].append(flip_local(added(s, half, 2 * half).astype(jnp.bfloat16), STREAMS[s][step]))
        if step == 1:
            terms[3][-1], expert_out = lax.optimization_barrier((terms[3][-1], expert_out))
            returned = lax.all_to_all(
                expert_out.T.reshape(node_count, NODE_CAP, slice_width), "node", split_axis=0, concat_axis=0, tiled=True
            ).reshape(slot_count, slice_width)
            route_term = (slot_gate[:, None] * returned.astype(jnp.float32)).astype(jnp.bfloat16)
        if step == 2:
            terms[3][-1], route_term = lax.optimization_barrier((terms[3][-1], route_term))
    expert_part = lax.dot_general(
        route_term, chosen, (((0,), (1,)), ((), ())), preferred_element_type=jnp.float32
    )
    dense_part = jnp.concatenate([added(s, 0, 1)[0] for s in range(4)], axis=1)
    return (columns.astype(jnp.float32) + dense_part + expert_part).astype(jnp.bfloat16).T


def solution(mesh):
    return jax.shard_map(
        shards,
        mesh=mesh,
        in_specs=(
            P("node", "local"),
            P(),
            P(None, "local"),
            P(None, "local"),
            P("local", None),
            P("node", None, "local"),
            P("node", None, "local"),
            P("node", "local", None),
            P("node", None),
            P("node", None),
        ),
        out_specs=P("node", "local"),
        check_vma=False,
    )
```

```python
import functools

import jax
import jax.numpy as jnp
from jax import lax
from jax.experimental import pallas as pl
from jax.experimental.pallas import tpu as pltpu
from jax.sharding import PartitionSpec as P

EPSILON = 1e-05
NODE_CAP = 16
GRAY = (0, 1, 3, 2)

LOCAL_LABEL = [GRAY[i % 4] | GRAY[i // 4] << 2 for i in range(16)]
LOCAL_AT = {label: i for i, label in enumerate(LOCAL_LABEL)}

STREAMS = ((0, 1, 2, 3), (1, 2, 3, 0), (2, 3, 0, 1), (3, 0, 1, 2))


def flip_local(array, bit):
    return lax.ppermute(array, "local", [(i, LOCAL_AT[LOCAL_LABEL[i] ^ (1 << bit)]) for i in range(16)])


def route_slots(ids_block, window):
    flat_ids = ids_block.reshape(-1)
    expert_range = jnp.arange(window, dtype=jnp.int32)
    member = (flat_ids[:, None] == expert_range[None, :]).astype(jnp.int32)
    before = jnp.cumsum(member, axis=0) - member
    route_rank = jnp.sum(before * member, axis=1)
    kept = (jnp.sum(member, axis=1) > 0) & (route_rank < NODE_CAP)
    slot = jnp.where(kept, flat_ids * NODE_CAP + route_rank, -1)
    return slot.reshape(ids_block.shape)


def transposed_dot(weight, rows):
    return lax.dot_general(weight, rows, (((0,), (0,)), ((), ())), preferred_element_type=jnp.float32)


def silu(value):
    return value / (1.0 + jnp.exp(-value))


def send_kernel(first, slice_ref, gate_up_ref, scale_ref, turned_ref, hidden_ref, *outs):
    half = gate_up_ref.shape[0] // 2
    columns = outs[0].shape[-1]
    for i, out in enumerate(outs):
        here = slice((first + i) * columns, (first + i + 1) * columns)
        scale = scale_ref[:, here]
        hidden = (silu(gate_up_ref[:half, here] * scale) * (gate_up_ref[half:, here] * scale)).astype(jnp.bfloat16)
        hidden_ref[:, i * columns : (i + 1) * columns] = hidden
        for j in range(out.shape[0]):
            at = slice_ref[stream_mask(first + i, 1, j)]
            out[j] = jnp.dot(turned_ref[at], hidden, preferred_element_type=jnp.float32).astype(jnp.bfloat16)


def stream_mask(s, sent, j):
    a, b, c, d = STREAMS[s]
    return sent << a | ((j >> 2) & 1) << b | ((j >> 1) & 1) << c | (j & 1) << d


def sent_parts(first, slice_of, gate_up, scale, turned):
    both = gate_up.shape[0]
    columns = gate_up.shape[1] // 4
    blocks, slice_rows, deep = turned.shape
    in_vmem = pl.BlockSpec(memory_space=pltpu.VMEM)
    return pl.pallas_call(
        functools.partial(send_kernel, first),
        in_specs=[pl.BlockSpec(memory_space=pltpu.SMEM), in_vmem, in_vmem, in_vmem],
        out_specs=[in_vmem] * 3,
        out_shape=[jax.ShapeDtypeStruct((deep, 2 * columns), jnp.bfloat16)]
        + [jax.ShapeDtypeStruct((blocks // 2, slice_rows, columns), jnp.bfloat16)] * 2,
        compiler_params=pltpu.CompilerParams(vmem_limit_bytes=24 << 20),
        cost_estimate=pl.CostEstimate(
            flops=2 * blocks * slice_rows * deep * columns,
            bytes_accessed=2 * blocks * slice_rows * (deep + columns),
            transcendentals=0,
        ),
    )(slice_of, gate_up, scale, turned)


def keep_kernel(slice_ref, *refs):
    weights, hidden, outs = refs[:4], refs[4:6], refs[6:]
    columns = outs[0].shape[-1]
    for s in range(4):
        rows = hidden[s // 2][:, s % 2 * columns : (s % 2 + 1) * columns]
        outs[s][0] = jnp.dot(weights[s][0], rows, preferred_element_type=jnp.float32).astype(jnp.bfloat16)


def kept_parts(slice_of, turned, hidden):
    blocks, rows, deep = turned.shape
    columns = hidden[0].shape[1] // 2

    def weight_spec(s):
        return pl.BlockSpec((1, rows, deep), lambda j, at: (at[stream_mask(s, 0, j)], 0, 0))

    return pl.pallas_call(
        keep_kernel,
        grid_spec=pltpu.PrefetchScalarGridSpec(
            num_scalar_prefetch=1,
            grid=(blocks // 2,),
            in_specs=[weight_spec(s) for s in range(4)] + [pl.BlockSpec((deep, 2 * columns), lambda j, at: (0, 0))] * 2,
            out_specs=[pl.BlockSpec((1, rows, columns), lambda j, at: (j, 0, 0))] * 4,
        ),
        out_shape=[jax.ShapeDtypeStruct((blocks // 2, rows, columns), jnp.bfloat16)] * 4,
        compiler_params=pltpu.CompilerParams(vmem_limit_bytes=24 << 20),
        cost_estimate=pl.CostEstimate(
            flops=4 * blocks * rows * deep * columns, bytes_accessed=4 * blocks * rows * (deep + columns), transcendentals=0
        ),
    )(slice_of, *[turned] * 4, *hidden)


def expert_kernel(blocks, features, at_ref, x0, x1, x2, x3, gate_ref, up_ref, gain_ref, hidden_ref, gate_total, up_total, squares):
    step = pl.program_id(0)

    @pl.when(step == 0)
    def _():
        gate_total[...] = jnp.zeros_like(gate_total)
        up_total[...] = jnp.zeros_like(up_total)
        squares[...] = jnp.zeros_like(squares)

    as_float = jnp.concatenate([x0[0], x1[0], x2[0], x3[0]], axis=0).astype(jnp.float32)
    squares[...] += jnp.sum(as_float * as_float, axis=0, keepdims=True)
    rows = (as_float * gain_ref[...]).astype(jnp.bfloat16)
    gate_total[...] += transposed_dot(gate_ref[0], rows)
    up_total[...] += transposed_dot(up_ref[0], rows)

    @pl.when(step == blocks - 1)
    def _():
        scale = lax.rsqrt(squares[...] / features + EPSILON)
        hidden_ref[...] = (silu(gate_total[...] * scale) * (up_total[...] * scale)).astype(jnp.bfloat16)


def expert_gate_up(slice_of, pooled, gate_weight, up_weight, gain_column):
    blocks, quarter_rows, columns = pooled[0].shape
    rows = 4 * quarter_rows
    hidden = gate_weight.shape[-1]
    weight_spec = pl.BlockSpec((1, rows, hidden), lambda m, at: (0, at[m], 0))

    def stream_spec(s):
        a, b, c, d = STREAMS[s]

        def index(m, at):
            return ((m >> a) & 1) | ((m >> b) & 1) << 1 | ((m >> c) & 1) << 2 | ((m >> d) & 1) << 3, 0, 0

        return pl.BlockSpec((1, quarter_rows, columns), index)

    return pl.pallas_call(
        functools.partial(expert_kernel, blocks, blocks * rows),
        grid_spec=pltpu.PrefetchScalarGridSpec(
            num_scalar_prefetch=1,
            grid=(blocks,),
            in_specs=[stream_spec(s) for s in range(4)]
            + [weight_spec, weight_spec, pl.BlockSpec((rows, 1), lambda m, at: (at[m], 0))],
            out_specs=pl.BlockSpec((hidden, columns), lambda m, at: (0, 0)),
            scratch_shapes=[
                pltpu.VMEM((hidden, columns), jnp.float32),
                pltpu.VMEM((hidden, columns), jnp.float32),
                pltpu.VMEM((1, columns), jnp.float32),
            ],
        ),
        out_shape=jax.ShapeDtypeStruct((hidden, columns), jnp.bfloat16),
        compiler_params=pltpu.CompilerParams(vmem_limit_bytes=24 << 20),
        cost_estimate=pl.CostEstimate(
            flops=4 * blocks * rows * columns * hidden,
            bytes_accessed=2 * blocks * rows * (columns + 2 * hidden),
            transcendentals=0,
        ),
    )(slice_of, *pooled, gate_weight, up_weight, gain_column)


def expert_down_kernel(weight_ref, hidden_ref, out_ref):
    out_ref[...] = transposed_dot(weight_ref[0], hidden_ref[...]).astype(jnp.bfloat16)


def expert_down_parts(weight, hidden):
    _, deep, features = weight.shape
    columns = hidden.shape[1]
    wide = features // 4
    return pl.pallas_call(
        expert_down_kernel,
        grid=(features // wide,),
        in_specs=[
            pl.BlockSpec((1, deep, wide), lambda m: (0, 0, m)),
            pl.BlockSpec((deep, columns), lambda m: (0, 0)),
        ],
        out_specs=pl.BlockSpec((wide, columns), lambda m: (m, 0)),
        out_shape=jax.ShapeDtypeStruct((features, columns), jnp.bfloat16),
        compiler_params=pltpu.CompilerParams(vmem_limit_bytes=24 << 20),
        cost_estimate=pl.CostEstimate(
            flops=2 * features * deep * columns, bytes_accessed=2 * features * (deep + columns), transcendentals=0
        ),
    )(weight, hidden)


def add_pair(kept, got):
    return (kept.astype(jnp.float32) + got.astype(jnp.float32)).astype(jnp.bfloat16)


def shards(
    tokens,
    norm_gain,
    dense_gate,
    dense_up,
    dense_down,
    expert_gate,
    expert_up,
    expert_down,
    expert_ids,
    route_gates,
):
    node_count = lax.axis_size("node")
    local_index = lax.axis_index("local")
    slice_width = tokens.shape[1]
    width = slice_width * 16
    slot_count = node_count * NODE_CAP
    slice_table = [[LOCAL_AT[LOCAL_LABEL[i] ^ m] for m in range(16)] for i in range(16)]
    slice_of = jnp.asarray(slice_table, jnp.int32)[local_index]

    columns = tokens.T
    whole_columns = lax.all_gather(columns, "local", axis=0, tiled=True)

    slot = route_slots(expert_ids, node_count)
    slot_range = jnp.arange(slot_count, dtype=jnp.int32)
    match_float = (slot[:, :, None] == slot_range[None, None, :]).astype(jnp.float32)
    chosen = jnp.sum(match_float, axis=1).astype(jnp.bfloat16)
    slot_gate = jnp.sum(match_float * route_gates[:, :, None], axis=(0, 1))
    send_rows = lax.dot_general(
        chosen, tokens, (((0,), (0,)), ((), ())), preferred_element_type=jnp.float32
    ).astype(jnp.bfloat16)
    routed = lax.all_to_all(
        send_rows.reshape(node_count, NODE_CAP, slice_width), "node", split_axis=0, concat_axis=0, tiled=True
    )
    routed = routed.reshape(slot_count, slice_width).T

    as_float = columns.astype(jnp.float32)
    square_sum = jnp.sum(as_float * as_float, axis=0, keepdims=True)
    gain_column = norm_gain[:, None]
    part = slice_width // 4
    pooled = [routed[None, s * part : (s + 1) * part] for s in range(4)]
    for step in range(4):
        got = [flip_local(pooled[s], STREAMS[s][step]) for s in range(4)]
        square_sum = square_sum + flip_local(square_sum, step)
        if step == 1:
            dense_gate, dense_up, _ = lax.optimization_barrier((dense_gate, dense_up, pooled))
            weight = jnp.concatenate(
                [(w.astype(jnp.float32) * gain_column).astype(jnp.bfloat16) for w in (dense_gate, dense_up)], axis=1
            )
            got, weight = lax.optimization_barrier((got, weight))
        if step == 2:
            dense_down, _ = lax.optimization_barrier((dense_down, pooled))
            turned = dense_down.T.reshape(16, slice_width, dense_down.shape[0])
            got, turned = lax.optimization_barrier((got, turned))
        pooled = [jnp.concatenate([pooled[s], got[s]], axis=0) for s in range(4)]
    scale = lax.rsqrt(square_sum / width + EPSILON)

    expert_hidden = expert_gate_up(slice_of, pooled, expert_gate, expert_up, gain_column)
    expert_partial = expert_down_parts(expert_down, expert_hidden)
    expert_partial, scale = lax.optimization_barrier((expert_partial, scale))
    def halve(array, bit):
        half = 1 << bit
        upper = (local_index >> bit) & 1
        keep = lax.dynamic_slice_in_dim(array, upper * half, half, 0)
        return keep, lax.dynamic_slice_in_dim(array, (1 - upper) * half, half, 0)

    expert_keep, expert_send = halve(expert_partial.reshape(16, slice_width, slot_count), 3)
    expert_keep, expert_send, whole_columns = lax.optimization_barrier((expert_keep, expert_send, whole_columns))
    expert_got = flip_local(expert_send, 3)

    gate_up = transposed_dot(weight, whole_columns)
    low_hidden, *sent = sent_parts(0, slice_of, gate_up, scale, turned)
    high_hidden, *more = sent_parts(2, slice_of, gate_up, scale, turned)
    sent += more
    sent[3], expert_got = lax.optimization_barrier((sent[3], expert_got))
    arrived = [flip_local(sent[s], STREAMS[s][0]) for s in range(4)]
    sums = kept_parts(slice_of, turned, (low_hidden, high_hidden))
    arrived[3], expert_got = lax.optimization_barrier((arrived[3], expert_got))
    terms = [[sums[s], arrived[s]] for s in range(4)]

    def added(s, low, high):
        return sum(term[low:high].astype(jnp.float32) for term in terms[s])

    for step in (1, 2, 3):
        half = 8 >> step
        for s in range(4):
            terms[s].append(flip_local(added(s, half, 2 * half).astype(jnp.bfloat16), STREAMS[s][step]))
        if step < 3:
            expert_keep, expert_send = halve(add_pair(expert_keep, expert_got), (3, 2, 0)[step])
            expert_got = flip_local(expert_send, (3, 2, 0)[step])
            if step == 1:
                terms[0][-1], expert_got = lax.optimization_barrier((terms[0][-1], expert_got))
        if step == 1:
            expert_keep, expert_send = halve(add_pair(expert_keep, expert_got), 1)
            expert_got = flip_local(expert_send, 1)
            terms[3][-1], expert_got = lax.optimization_barrier((terms[3][-1], expert_got))
        if step == 2:
            expert_out = add_pair(expert_keep, expert_got)[0]
            terms[1][-1], expert_out = lax.optimization_barrier((terms[1][-1], expert_out))
            returned = lax.all_to_all(
                expert_out.T.reshape(node_count, NODE_CAP, slice_width), "node", split_axis=0, concat_axis=0, tiled=True
            ).reshape(slot_count, slice_width)
            route_term = (slot_gate[:, None] * returned.astype(jnp.float32)).astype(jnp.bfloat16)
    expert_part = lax.dot_general(
        route_term, chosen, (((0,), (1,)), ((), ())), preferred_element_type=jnp.float32
    )
    dense_part = jnp.concatenate([added(s, 0, 1)[0] for s in range(4)], axis=1)
    return (columns.astype(jnp.float32) + dense_part + expert_part).astype(jnp.bfloat16).T


def solution(mesh):
    return jax.shard_map(
        shards,
        mesh=mesh,
        in_specs=(
            P("node", "local"),
            P(),
            P(None, "local"),
            P(None, "local"),
            P("local", None),
            P("node", None, "local"),
            P("node", None, "local"),
            P("node", "local", None),
            P("node", None),
            P("node", None),
        ),
        out_specs=P("node", "local"),
        check_vma=False,
    )
```

```python
import functools

import jax
import jax.numpy as jnp
from jax import lax
from jax.experimental import pallas as pl
from jax.experimental.pallas import tpu as pltpu
from jax.sharding import PartitionSpec as P

EPSILON = 1e-05
NODE_CAP = 16
GRAY = (0, 1, 3, 2)

LOCAL_LABEL = [GRAY[i % 4] | GRAY[i // 4] << 2 for i in range(16)]
LOCAL_AT = {label: i for i, label in enumerate(LOCAL_LABEL)}

STREAMS = ((0, 1, 2, 3), (1, 2, 3, 0), (2, 3, 0, 1), (3, 0, 1, 2))


def flip_local(array, bit):
    return lax.ppermute(array, "local", [(i, LOCAL_AT[LOCAL_LABEL[i] ^ (1 << bit)]) for i in range(16)])


def route_slots(ids_block, window):
    flat_ids = ids_block.reshape(-1)
    expert_range = jnp.arange(window, dtype=jnp.int32)
    member = (flat_ids[:, None] == expert_range[None, :]).astype(jnp.int32)
    before = jnp.cumsum(member, axis=0) - member
    route_rank = jnp.sum(before * member, axis=1)
    kept = (jnp.sum(member, axis=1) > 0) & (route_rank < NODE_CAP)
    slot = jnp.where(kept, flat_ids * NODE_CAP + route_rank, -1)
    return slot.reshape(ids_block.shape)


def transposed_dot(weight, rows):
    return lax.dot_general(weight, rows, (((0,), (0,)), ((), ())), preferred_element_type=jnp.float32)


def silu(value):
    return value / (1.0 + jnp.exp(-value))


def send_kernel(first, slice_ref, gate_up_ref, scale_ref, turned_ref, hidden_ref, *outs):
    half = gate_up_ref.shape[0] // 2
    columns = outs[0].shape[-1]
    for i, out in enumerate(outs):
        here = slice((first + i) * columns, (first + i + 1) * columns)
        scale = scale_ref[:, here]
        hidden = (silu(gate_up_ref[:half, here] * scale) * (gate_up_ref[half:, here] * scale)).astype(jnp.bfloat16)
        hidden_ref[:, i * columns : (i + 1) * columns] = hidden
        for j in range(out.shape[0]):
            at = slice_ref[stream_mask(first + i, 1, j)]
            out[j] = jnp.dot(turned_ref[at], hidden, preferred_element_type=jnp.float32).astype(jnp.bfloat16)


def stream_mask(s, sent, j):
    a, b, c, d = STREAMS[s]
    return sent << a | ((j >> 2) & 1) << b | ((j >> 1) & 1) << c | (j & 1) << d


def sent_parts(first, slice_of, gate_up, scale, turned):
    both = gate_up.shape[0]
    columns = gate_up.shape[1] // 4
    blocks, slice_rows, deep = turned.shape
    in_vmem = pl.BlockSpec(memory_space=pltpu.VMEM)
    return pl.pallas_call(
        functools.partial(send_kernel, first),
        in_specs=[pl.BlockSpec(memory_space=pltpu.SMEM), in_vmem, in_vmem, in_vmem],
        out_specs=[in_vmem] * 3,
        out_shape=[jax.ShapeDtypeStruct((deep, 2 * columns), jnp.bfloat16)]
        + [jax.ShapeDtypeStruct((blocks // 2, slice_rows, columns), jnp.bfloat16)] * 2,
        compiler_params=pltpu.CompilerParams(vmem_limit_bytes=24 << 20),
        cost_estimate=pl.CostEstimate(
            flops=2 * blocks * slice_rows * deep * columns,
            bytes_accessed=2 * blocks * slice_rows * (deep + columns),
            transcendentals=0,
        ),
    )(slice_of, gate_up, scale, turned)


def keep_kernel(slice_ref, *refs):
    weights, hidden, outs = refs[:4], refs[4:6], refs[6:]
    columns = outs[0].shape[-1]
    for s in range(4):
        rows = hidden[s // 2][:, s % 2 * columns : (s % 2 + 1) * columns]
        outs[s][0] = jnp.dot(weights[s][0], rows, preferred_element_type=jnp.float32).astype(jnp.bfloat16)


def kept_parts(slice_of, turned, hidden):
    blocks, rows, deep = turned.shape
    columns = hidden[0].shape[1] // 2

    def weight_spec(s):
        return pl.BlockSpec((1, rows, deep), lambda j, at: (at[stream_mask(s, 0, j)], 0, 0))

    return pl.pallas_call(
        keep_kernel,
        grid_spec=pltpu.PrefetchScalarGridSpec(
            num_scalar_prefetch=1,
            grid=(blocks // 2,),
            in_specs=[weight_spec(s) for s in range(4)] + [pl.BlockSpec((deep, 2 * columns), lambda j, at: (0, 0))] * 2,
            out_specs=[pl.BlockSpec((1, rows, columns), lambda j, at: (j, 0, 0))] * 4,
        ),
        out_shape=[jax.ShapeDtypeStruct((blocks // 2, rows, columns), jnp.bfloat16)] * 4,
        compiler_params=pltpu.CompilerParams(vmem_limit_bytes=24 << 20),
        cost_estimate=pl.CostEstimate(
            flops=4 * blocks * rows * deep * columns, bytes_accessed=4 * blocks * rows * (deep + columns), transcendentals=0
        ),
    )(slice_of, *[turned] * 4, *hidden)


def expert_kernel(blocks, features, at_ref, x0, x1, x2, x3, gate_ref, up_ref, gain_ref, hidden_ref, gate_total, up_total, squares):
    step = pl.program_id(0)

    @pl.when(step == 0)
    def _():
        gate_total[...] = jnp.zeros_like(gate_total)
        up_total[...] = jnp.zeros_like(up_total)
        squares[...] = jnp.zeros_like(squares)

    as_float = jnp.concatenate([x0[0], x1[0], x2[0], x3[0]], axis=0).astype(jnp.float32)
    squares[...] += jnp.sum(as_float * as_float, axis=0, keepdims=True)
    rows = (as_float * gain_ref[...]).astype(jnp.bfloat16)
    gate_total[...] += transposed_dot(gate_ref[0], rows)
    up_total[...] += transposed_dot(up_ref[0], rows)

    @pl.when(step == blocks - 1)
    def _():
        scale = lax.rsqrt(squares[...] / features + EPSILON)
        hidden_ref[...] = (silu(gate_total[...] * scale) * (up_total[...] * scale)).astype(jnp.bfloat16)


def expert_gate_up(slice_of, pooled, gate_weight, up_weight, gain_column):
    blocks, quarter_rows, columns = pooled[0].shape
    rows = 4 * quarter_rows
    hidden = gate_weight.shape[-1]
    weight_spec = pl.BlockSpec((1, rows, hidden), lambda m, at: (0, at[m], 0))

    def stream_spec(s):
        a, b, c, d = STREAMS[s]

        def index(m, at):
            return ((m >> a) & 1) | ((m >> b) & 1) << 1 | ((m >> c) & 1) << 2 | ((m >> d) & 1) << 3, 0, 0

        return pl.BlockSpec((1, quarter_rows, columns), index)

    return pl.pallas_call(
        functools.partial(expert_kernel, blocks, blocks * rows),
        grid_spec=pltpu.PrefetchScalarGridSpec(
            num_scalar_prefetch=1,
            grid=(blocks,),
            in_specs=[stream_spec(s) for s in range(4)]
            + [weight_spec, weight_spec, pl.BlockSpec((rows, 1), lambda m, at: (at[m], 0))],
            out_specs=pl.BlockSpec((hidden, columns), lambda m, at: (0, 0)),
            scratch_shapes=[
                pltpu.VMEM((hidden, columns), jnp.float32),
                pltpu.VMEM((hidden, columns), jnp.float32),
                pltpu.VMEM((1, columns), jnp.float32),
            ],
        ),
        out_shape=jax.ShapeDtypeStruct((hidden, columns), jnp.bfloat16),
        compiler_params=pltpu.CompilerParams(vmem_limit_bytes=24 << 20),
        cost_estimate=pl.CostEstimate(
            flops=4 * blocks * rows * columns * hidden,
            bytes_accessed=2 * blocks * rows * (columns + 2 * hidden),
            transcendentals=0,
        ),
    )(slice_of, *pooled, gate_weight, up_weight, gain_column)


def expert_down_kernel(weight_ref, hidden_ref, out_ref):
    out_ref[...] = transposed_dot(weight_ref[0], hidden_ref[...]).astype(jnp.bfloat16)


def expert_down_parts(weight, hidden):
    _, deep, features = weight.shape
    columns = hidden.shape[1]
    wide = features // 4
    return pl.pallas_call(
        expert_down_kernel,
        grid=(features // wide,),
        in_specs=[
            pl.BlockSpec((1, deep, wide), lambda m: (0, 0, m)),
            pl.BlockSpec((deep, columns), lambda m: (0, 0)),
        ],
        out_specs=pl.BlockSpec((wide, columns), lambda m: (m, 0)),
        out_shape=jax.ShapeDtypeStruct((features, columns), jnp.bfloat16),
        compiler_params=pltpu.CompilerParams(vmem_limit_bytes=24 << 20),
        cost_estimate=pl.CostEstimate(
            flops=2 * features * deep * columns, bytes_accessed=2 * features * (deep + columns), transcendentals=0
        ),
    )(weight, hidden)


def shards(
    tokens,
    norm_gain,
    dense_gate,
    dense_up,
    dense_down,
    expert_gate,
    expert_up,
    expert_down,
    expert_ids,
    route_gates,
):
    node_count = lax.axis_size("node")
    local_index = lax.axis_index("local")
    slice_width = tokens.shape[1]
    width = slice_width * 16
    slot_count = node_count * NODE_CAP
    slice_table = [[LOCAL_AT[LOCAL_LABEL[i] ^ m] for m in range(16)] for i in range(16)]
    slice_of = jnp.asarray(slice_table, jnp.int32)[local_index]

    columns = tokens.T
    whole_columns = lax.all_gather(columns, "local", axis=0, tiled=True)

    slot = route_slots(expert_ids, node_count)
    slot_range = jnp.arange(slot_count, dtype=jnp.int32)
    match_float = (slot[:, :, None] == slot_range[None, None, :]).astype(jnp.float32)
    chosen = jnp.sum(match_float, axis=1).astype(jnp.bfloat16)
    slot_gate = jnp.sum(match_float * route_gates[:, :, None], axis=(0, 1))
    send_rows = lax.dot_general(
        chosen, tokens, (((0,), (0,)), ((), ())), preferred_element_type=jnp.float32
    ).astype(jnp.bfloat16)
    routed = lax.all_to_all(
        send_rows.reshape(node_count, NODE_CAP, slice_width), "node", split_axis=0, concat_axis=0, tiled=True
    )
    routed = routed.reshape(slot_count, slice_width).T

    as_float = columns.astype(jnp.float32)
    square_sum = jnp.sum(as_float * as_float, axis=0, keepdims=True)
    gain_column = norm_gain[:, None]
    part = slice_width // 4
    pooled = [routed[None, s * part : (s + 1) * part] for s in range(4)]
    for step in range(4):
        got = [flip_local(pooled[s], STREAMS[s][step]) for s in range(4)]
        square_sum = square_sum + flip_local(square_sum, step)
        if step == 1:
            dense_gate, dense_up, _ = lax.optimization_barrier((dense_gate, dense_up, pooled))
            weight = jnp.concatenate(
                [(w.astype(jnp.float32) * gain_column).astype(jnp.bfloat16) for w in (dense_gate, dense_up)], axis=1
            )
            got, weight = lax.optimization_barrier((got, weight))
        if step == 2:
            dense_down, _ = lax.optimization_barrier((dense_down, pooled))
            turned = dense_down.T.reshape(16, slice_width, dense_down.shape[0])
            got, turned = lax.optimization_barrier((got, turned))
        pooled = [jnp.concatenate([pooled[s], got[s]], axis=0) for s in range(4)]
    scale = lax.rsqrt(square_sum / width + EPSILON)

    expert_hidden = expert_gate_up(slice_of, pooled, expert_gate, expert_up, gain_column)
    expert_partial = expert_down_parts(expert_down, expert_hidden)
    expert_partial, scale, whole_columns = lax.optimization_barrier((expert_partial, scale, whole_columns))
    expert_out = lax.psum_scatter(expert_partial, "local", scatter_dimension=0, tiled=True)

    gate_up = transposed_dot(weight, whole_columns)
    low_hidden, *sent = sent_parts(0, slice_of, gate_up, scale, turned)
    high_hidden, *more = sent_parts(2, slice_of, gate_up, scale, turned)
    sent += more
    arrived = [flip_local(sent[s], STREAMS[s][0]) for s in range(4)]
    sums = kept_parts(slice_of, turned, (low_hidden, high_hidden))
    terms = [[sums[s], arrived[s]] for s in range(4)]

    def added(s, low, high):
        return sum(term[low:high].astype(jnp.float32) for term in terms[s])

    for step in (1, 2, 3):
        half = 8 >> step
        for s in range(4):
            terms[s].append(flip_local(added(s, half, 2 * half).astype(jnp.bfloat16), STREAMS[s][step]))
        if step == 1:
            terms[0][-1], expert_out = lax.optimization_barrier((terms[0][-1], expert_out))
            returned = lax.all_to_all(
                expert_out.T.reshape(node_count, NODE_CAP, slice_width), "node", split_axis=0, concat_axis=0, tiled=True
            ).reshape(slot_count, slice_width)
            route_term = (slot_gate[:, None] * returned.astype(jnp.float32)).astype(jnp.bfloat16)
        if step == 2:
            terms[3][-1], route_term = lax.optimization_barrier((terms[3][-1], route_term))
    expert_part = lax.dot_general(
        route_term, chosen, (((0,), (1,)), ((), ())), preferred_element_type=jnp.float32
    )
    dense_part = jnp.concatenate([added(s, 0, 1)[0] for s in range(4)], axis=1)
    return (columns.astype(jnp.float32) + dense_part + expert_part).astype(jnp.bfloat16).T


def solution(mesh):
    return jax.shard_map(
        shards,
        mesh=mesh,
        in_specs=(
            P("node", "local"),
            P(),
            P(None, "local"),
            P(None, "local"),
            P("local", None),
            P("node", None, "local"),
            P("node", None, "local"),
            P("node", "local", None),
            P("node", None),
            P("node", None),
        ),
        out_specs=P("node", "local"),
        check_vma=False,
    )
```

```python
import functools

import jax
import jax.numpy as jnp
from jax import lax
from jax.experimental import pallas as pl
from jax.experimental.pallas import tpu as pltpu
from jax.sharding import PartitionSpec as P

EPSILON = 1e-05
NODE_CAP = 16
GRAY = (0, 1, 3, 2)

LOCAL_LABEL = [GRAY[i % 4] | GRAY[i // 4] << 2 for i in range(16)]
LOCAL_AT = {label: i for i, label in enumerate(LOCAL_LABEL)}

STREAMS = ((0, 1, 2, 3), (1, 2, 3, 0), (2, 3, 0, 1), (3, 0, 1, 2))


def flip_local(array, bit):
    return lax.ppermute(array, "local", [(i, LOCAL_AT[LOCAL_LABEL[i] ^ (1 << bit)]) for i in range(16)])


def route_slots(ids_block, window):
    flat_ids = ids_block.reshape(-1)
    expert_range = jnp.arange(window, dtype=jnp.int32)
    member = (flat_ids[:, None] == expert_range[None, :]).astype(jnp.int32)
    before = jnp.cumsum(member, axis=0) - member
    route_rank = jnp.sum(before * member, axis=1)
    kept = (jnp.sum(member, axis=1) > 0) & (route_rank < NODE_CAP)
    slot = jnp.where(kept, flat_ids * NODE_CAP + route_rank, -1)
    return slot.reshape(ids_block.shape)


def transposed_dot(weight, rows):
    return lax.dot_general(weight, rows, (((0,), (0,)), ((), ())), preferred_element_type=jnp.float32)


def silu(value):
    return value / (1.0 + jnp.exp(-value))


def send_kernel(first, slice_ref, gate_up_ref, scale_ref, turned_ref, hidden_ref, *outs):
    half = gate_up_ref.shape[0] // 2
    columns = outs[0].shape[-1]
    for i, out in enumerate(outs):
        here = slice((first + i) * columns, (first + i + 1) * columns)
        scale = scale_ref[:, here]
        hidden = (silu(gate_up_ref[:half, here] * scale) * (gate_up_ref[half:, here] * scale)).astype(jnp.bfloat16)
        hidden_ref[:, i * columns : (i + 1) * columns] = hidden
        for j in range(out.shape[0]):
            at = slice_ref[stream_mask(first + i, 1, j)]
            out[j] = jnp.dot(turned_ref[at], hidden, preferred_element_type=jnp.float32).astype(jnp.bfloat16)


def stream_mask(s, sent, j):
    a, b, c, d = STREAMS[s]
    return sent << a | ((j >> 2) & 1) << b | ((j >> 1) & 1) << c | (j & 1) << d


def sent_parts(first, slice_of, gate_up, scale, turned):
    both = gate_up.shape[0]
    columns = gate_up.shape[1] // 4
    blocks, slice_rows, deep = turned.shape
    in_vmem = pl.BlockSpec(memory_space=pltpu.VMEM)
    return pl.pallas_call(
        functools.partial(send_kernel, first),
        in_specs=[pl.BlockSpec(memory_space=pltpu.SMEM), in_vmem, in_vmem, in_vmem],
        out_specs=[in_vmem] * 3,
        out_shape=[jax.ShapeDtypeStruct((deep, 2 * columns), jnp.bfloat16)]
        + [jax.ShapeDtypeStruct((blocks // 2, slice_rows, columns), jnp.bfloat16)] * 2,
        compiler_params=pltpu.CompilerParams(vmem_limit_bytes=24 << 20),
        cost_estimate=pl.CostEstimate(
            flops=2 * blocks * slice_rows * deep * columns,
            bytes_accessed=2 * blocks * slice_rows * (deep + columns),
            transcendentals=0,
        ),
    )(slice_of, gate_up, scale, turned)


def keep_kernel(slice_ref, *refs):
    weights, hidden, outs = refs[:4], refs[4:6], refs[6:]
    columns = outs[0].shape[-1]
    for s in range(4):
        rows = hidden[s // 2][:, s % 2 * columns : (s % 2 + 1) * columns]
        outs[s][0] = jnp.dot(weights[s][0], rows, preferred_element_type=jnp.float32).astype(jnp.bfloat16)


def kept_parts(slice_of, turned, hidden):
    blocks, rows, deep = turned.shape
    columns = hidden[0].shape[1] // 2

    def weight_spec(s):
        return pl.BlockSpec((1, rows, deep), lambda j, at: (at[stream_mask(s, 0, j)], 0, 0))

    return pl.pallas_call(
        keep_kernel,
        grid_spec=pltpu.PrefetchScalarGridSpec(
            num_scalar_prefetch=1,
            grid=(blocks // 2,),
            in_specs=[weight_spec(s) for s in range(4)] + [pl.BlockSpec((deep, 2 * columns), lambda j, at: (0, 0))] * 2,
            out_specs=[pl.BlockSpec((1, rows, columns), lambda j, at: (j, 0, 0))] * 4,
        ),
        out_shape=[jax.ShapeDtypeStruct((blocks // 2, rows, columns), jnp.bfloat16)] * 4,
        compiler_params=pltpu.CompilerParams(vmem_limit_bytes=24 << 20),
        cost_estimate=pl.CostEstimate(
            flops=4 * blocks * rows * deep * columns, bytes_accessed=4 * blocks * rows * (deep + columns), transcendentals=0
        ),
    )(slice_of, *[turned] * 4, *hidden)


def expert_kernel(blocks, features, at_ref, x0, x1, x2, x3, gate_ref, up_ref, gain_ref, hidden_ref, gate_total, up_total, squares):
    step = pl.program_id(0)

    @pl.when(step == 0)
    def _():
        gate_total[...] = jnp.zeros_like(gate_total)
        up_total[...] = jnp.zeros_like(up_total)
        squares[...] = jnp.zeros_like(squares)

    as_float = jnp.concatenate([x0[0], x1[0], x2[0], x3[0]], axis=0).astype(jnp.float32)
    squares[...] += jnp.sum(as_float * as_float, axis=0, keepdims=True)
    rows = (as_float * gain_ref[...]).astype(jnp.bfloat16)
    gate_total[...] += transposed_dot(gate_ref[0], rows)
    up_total[...] += transposed_dot(up_ref[0], rows)

    @pl.when(step == blocks - 1)
    def _():
        scale = lax.rsqrt(squares[...] / features + EPSILON)
        hidden_ref[...] = (silu(gate_total[...] * scale) * (up_total[...] * scale)).astype(jnp.bfloat16)


def expert_gate_up(slice_of, pooled, gate_weight, up_weight, gain_column):
    blocks, quarter_rows, columns = pooled[0].shape
    rows = 4 * quarter_rows
    hidden = gate_weight.shape[-1]
    weight_spec = pl.BlockSpec((1, rows, hidden), lambda m, at: (0, at[m], 0))

    def stream_spec(s):
        a, b, c, d = STREAMS[s]

        def index(m, at):
            return ((m >> a) & 1) | ((m >> b) & 1) << 1 | ((m >> c) & 1) << 2 | ((m >> d) & 1) << 3, 0, 0

        return pl.BlockSpec((1, quarter_rows, columns), index)

    return pl.pallas_call(
        functools.partial(expert_kernel, blocks, blocks * rows),
        grid_spec=pltpu.PrefetchScalarGridSpec(
            num_scalar_prefetch=1,
            grid=(blocks,),
            in_specs=[stream_spec(s) for s in range(4)]
            + [weight_spec, weight_spec, pl.BlockSpec((rows, 1), lambda m, at: (at[m], 0))],
            out_specs=pl.BlockSpec((hidden, columns), lambda m, at: (0, 0)),
            scratch_shapes=[
                pltpu.VMEM((hidden, columns), jnp.float32),
                pltpu.VMEM((hidden, columns), jnp.float32),
                pltpu.VMEM((1, columns), jnp.float32),
            ],
        ),
        out_shape=jax.ShapeDtypeStruct((hidden, columns), jnp.bfloat16),
        compiler_params=pltpu.CompilerParams(vmem_limit_bytes=24 << 20),
        cost_estimate=pl.CostEstimate(
            flops=4 * blocks * rows * columns * hidden,
            bytes_accessed=2 * blocks * rows * (columns + 2 * hidden),
            transcendentals=0,
        ),
    )(slice_of, *pooled, gate_weight, up_weight, gain_column)


def expert_down_kernel(weight_ref, hidden_ref, out_ref):
    out_ref[...] = transposed_dot(weight_ref[0], hidden_ref[...]).astype(jnp.bfloat16)


def expert_down_parts(weight, hidden):
    _, deep, features = weight.shape
    columns = hidden.shape[1]
    wide = features // 4
    return pl.pallas_call(
        expert_down_kernel,
        grid=(features // wide,),
        in_specs=[
            pl.BlockSpec((1, deep, wide), lambda m: (0, 0, m)),
            pl.BlockSpec((deep, columns), lambda m: (0, 0)),
        ],
        out_specs=pl.BlockSpec((wide, columns), lambda m: (m, 0)),
        out_shape=jax.ShapeDtypeStruct((features, columns), jnp.bfloat16),
        compiler_params=pltpu.CompilerParams(vmem_limit_bytes=24 << 20),
        cost_estimate=pl.CostEstimate(
            flops=2 * features * deep * columns, bytes_accessed=2 * features * (deep + columns), transcendentals=0
        ),
    )(weight, hidden)


def shards(
    tokens,
    norm_gain,
    dense_gate,
    dense_up,
    dense_down,
    expert_gate,
    expert_up,
    expert_down,
    expert_ids,
    route_gates,
):
    node_count = lax.axis_size("node")
    local_index = lax.axis_index("local")
    slice_width = tokens.shape[1]
    width = slice_width * 16
    slot_count = node_count * NODE_CAP
    slice_table = [[LOCAL_AT[LOCAL_LABEL[i] ^ m] for m in range(16)] for i in range(16)]
    slice_of = jnp.asarray(slice_table, jnp.int32)[local_index]

    columns = tokens.T
    whole_columns = lax.all_gather(columns, "local", axis=0, tiled=True)

    slot = route_slots(expert_ids, node_count)
    slot_range = jnp.arange(slot_count, dtype=jnp.int32)
    match_float = (slot[:, :, None] == slot_range[None, None, :]).astype(jnp.float32)
    chosen = jnp.sum(match_float, axis=1).astype(jnp.bfloat16)
    slot_gate = jnp.sum(match_float * route_gates[:, :, None], axis=(0, 1))
    send_rows = lax.dot_general(
        chosen, tokens, (((0,), (0,)), ((), ())), preferred_element_type=jnp.float32
    ).astype(jnp.bfloat16)
    routed = lax.all_to_all(
        send_rows.reshape(node_count, NODE_CAP, slice_width), "node", split_axis=0, concat_axis=0, tiled=True
    )
    routed = routed.reshape(slot_count, slice_width).T

    as_float = columns.astype(jnp.float32)
    square_sum = jnp.sum(as_float * as_float, axis=0, keepdims=True)
    gain_column = norm_gain[:, None]
    part = slice_width // 4
    pooled = [routed[None, s * part : (s + 1) * part] for s in range(4)]
    for step in range(4):
        got = [flip_local(pooled[s], STREAMS[s][step]) for s in range(4)]
        square_sum = square_sum + flip_local(square_sum, step)
        if step == 1:
            dense_gate, dense_up, _ = lax.optimization_barrier((dense_gate, dense_up, pooled))
            weight = jnp.concatenate(
                [(w.astype(jnp.float32) * gain_column).astype(jnp.bfloat16) for w in (dense_gate, dense_up)], axis=1
            )
            got, weight = lax.optimization_barrier((got, weight))
        if step == 2:
            dense_down, _ = lax.optimization_barrier((dense_down, pooled))
            turned = dense_down.T.reshape(16, slice_width, dense_down.shape[0])
            got, turned = lax.optimization_barrier((got, turned))
        pooled = [jnp.concatenate([pooled[s], got[s]], axis=0) for s in range(4)]
    scale = lax.rsqrt(square_sum / width + EPSILON)

    expert_hidden = expert_gate_up(slice_of, pooled, expert_gate, expert_up, gain_column)
    expert_partial = expert_down_parts(expert_down, expert_hidden)
    expert_partial, scale, whole_columns = lax.optimization_barrier((expert_partial, scale, whole_columns))
    expert_parts = lax.all_to_all(
        expert_partial.reshape(16, slice_width, slot_count), "local", split_axis=0, concat_axis=0, tiled=True
    )

    gate_up = transposed_dot(weight, whole_columns)
    low_hidden, *sent = sent_parts(0, slice_of, gate_up, scale, turned)
    high_hidden, *more = sent_parts(2, slice_of, gate_up, scale, turned)
    sent += more
    arrived = [flip_local(sent[s], STREAMS[s][0]) for s in range(4)]
    low_hidden, expert_parts = lax.optimization_barrier((low_hidden, expert_parts))
    sums = kept_parts(slice_of, turned, (low_hidden, high_hidden))
    expert_out = jnp.sum(expert_parts.astype(jnp.float32), axis=0).astype(jnp.bfloat16)
    returned = lax.all_to_all(
        expert_out.T.reshape(node_count, NODE_CAP, slice_width), "node", split_axis=0, concat_axis=0, tiled=True
    ).reshape(slot_count, slice_width)
    route_term = (slot_gate[:, None] * returned.astype(jnp.float32)).astype(jnp.bfloat16)
    arrived, route_term = lax.optimization_barrier((arrived, route_term))
    terms = [[sums[s], arrived[s]] for s in range(4)]

    def added(s, low, high):
        return sum(term[low:high].astype(jnp.float32) for term in terms[s])

    for step in (1, 2, 3):
        half = 8 >> step
        for s in range(4):
            terms[s].append(flip_local(added(s, half, 2 * half).astype(jnp.bfloat16), STREAMS[s][step]))
    expert_part = lax.dot_general(
        route_term, chosen, (((0,), (1,)), ((), ())), preferred_element_type=jnp.float32
    )
    dense_part = jnp.concatenate([added(s, 0, 1)[0] for s in range(4)], axis=1)
    return (columns.astype(jnp.float32) + dense_part + expert_part).astype(jnp.bfloat16).T


def solution(mesh):
    return jax.shard_map(
        shards,
        mesh=mesh,
        in_specs=(
            P("node", "local"),
            P(),
            P(None, "local"),
            P(None, "local"),
            P("local", None),
            P("node", None, "local"),
            P("node", None, "local"),
            P("node", "local", None),
            P("node", None),
            P("node", None),
        ),
        out_specs=P("node", "local"),
        check_vma=False,
    )
```

```python
import functools

import jax
import jax.numpy as jnp
from jax import lax
from jax.experimental import pallas as pl
from jax.experimental.pallas import tpu as pltpu
from jax.sharding import PartitionSpec as P

EPSILON = 1e-05
NODE_CAP = 16
GRAY = (0, 1, 3, 2)

LOCAL_LABEL = [GRAY[i % 4] | GRAY[i // 4] << 2 for i in range(16)]
LOCAL_AT = {label: i for i, label in enumerate(LOCAL_LABEL)}

STREAMS = ((0, 1, 2, 3), (1, 2, 3, 0), (2, 3, 0, 1), (3, 0, 1, 2))


def flip_local(array, bit):
    return lax.ppermute(array, "local", [(i, LOCAL_AT[LOCAL_LABEL[i] ^ (1 << bit)]) for i in range(16)])


def route_slots(ids_block, window):
    flat_ids = ids_block.reshape(-1)
    expert_range = jnp.arange(window, dtype=jnp.int32)
    member = (flat_ids[:, None] == expert_range[None, :]).astype(jnp.int32)
    before = jnp.cumsum(member, axis=0) - member
    route_rank = jnp.sum(before * member, axis=1)
    kept = (jnp.sum(member, axis=1) > 0) & (route_rank < NODE_CAP)
    slot = jnp.where(kept, flat_ids * NODE_CAP + route_rank, -1)
    return slot.reshape(ids_block.shape)


def transposed_dot(weight, rows):
    return lax.dot_general(weight, rows, (((0,), (0,)), ((), ())), preferred_element_type=jnp.float32)


def silu(value):
    return value / (1.0 + jnp.exp(-value))


def send_kernel(first, slice_ref, gate_up_ref, scale_ref, turned_ref, hidden_ref, *outs):
    half = gate_up_ref.shape[0] // 2
    columns = outs[0].shape[-1]
    for i, out in enumerate(outs):
        here = slice((first + i) * columns, (first + i + 1) * columns)
        scale = scale_ref[:, here]
        hidden = (silu(gate_up_ref[:half, here] * scale) * (gate_up_ref[half:, here] * scale)).astype(jnp.bfloat16)
        hidden_ref[:, i * columns : (i + 1) * columns] = hidden
        for j in range(out.shape[0]):
            at = slice_ref[stream_mask(first + i, 1, j)]
            out[j] = jnp.dot(turned_ref[at], hidden, preferred_element_type=jnp.float32).astype(jnp.bfloat16)


def stream_mask(s, sent, j):
    a, b, c, d = STREAMS[s]
    return sent << a | ((j >> 2) & 1) << b | ((j >> 1) & 1) << c | (j & 1) << d


def sent_parts(first, slice_of, gate_up, scale, turned):
    both = gate_up.shape[0]
    columns = gate_up.shape[1] // 4
    blocks, slice_rows, deep = turned.shape
    in_vmem = pl.BlockSpec(memory_space=pltpu.VMEM)
    return pl.pallas_call(
        functools.partial(send_kernel, first),
        in_specs=[pl.BlockSpec(memory_space=pltpu.SMEM), in_vmem, in_vmem, in_vmem],
        out_specs=[in_vmem] * 3,
        out_shape=[jax.ShapeDtypeStruct((deep, 2 * columns), jnp.bfloat16)]
        + [jax.ShapeDtypeStruct((blocks // 2, slice_rows, columns), jnp.bfloat16)] * 2,
        compiler_params=pltpu.CompilerParams(vmem_limit_bytes=24 << 20),
        cost_estimate=pl.CostEstimate(
            flops=2 * blocks * slice_rows * deep * columns,
            bytes_accessed=2 * blocks * slice_rows * (deep + columns),
            transcendentals=0,
        ),
    )(slice_of, gate_up, scale, turned)


def keep_kernel(slice_ref, *refs):
    weights, hidden, outs = refs[:4], refs[4:6], refs[6:]
    columns = outs[0].shape[-1]
    for s in range(4):
        rows = hidden[s // 2][:, s % 2 * columns : (s % 2 + 1) * columns]
        outs[s][0] = jnp.dot(weights[s][0], rows, preferred_element_type=jnp.float32).astype(jnp.bfloat16)


def kept_parts(slice_of, turned, hidden):
    blocks, rows, deep = turned.shape
    columns = hidden[0].shape[1] // 2

    def weight_spec(s):
        return pl.BlockSpec((1, rows, deep), lambda j, at: (at[stream_mask(s, 0, j)], 0, 0))

    return pl.pallas_call(
        keep_kernel,
        grid_spec=pltpu.PrefetchScalarGridSpec(
            num_scalar_prefetch=1,
            grid=(blocks // 2,),
            in_specs=[weight_spec(s) for s in range(4)] + [pl.BlockSpec((deep, 2 * columns), lambda j, at: (0, 0))] * 2,
            out_specs=[pl.BlockSpec((1, rows, columns), lambda j, at: (j, 0, 0))] * 4,
        ),
        out_shape=[jax.ShapeDtypeStruct((blocks // 2, rows, columns), jnp.bfloat16)] * 4,
        compiler_params=pltpu.CompilerParams(vmem_limit_bytes=24 << 20),
        cost_estimate=pl.CostEstimate(
            flops=4 * blocks * rows * deep * columns, bytes_accessed=4 * blocks * rows * (deep + columns), transcendentals=0
        ),
    )(slice_of, *[turned] * 4, *hidden)


def expert_kernel(blocks, features, at_ref, x0, x1, x2, x3, gate_ref, up_ref, gain_ref, hidden_ref, gate_total, up_total, squares):
    step = pl.program_id(0)

    @pl.when(step == 0)
    def _():
        gate_total[...] = jnp.zeros_like(gate_total)
        up_total[...] = jnp.zeros_like(up_total)
        squares[...] = jnp.zeros_like(squares)

    as_float = jnp.concatenate([x0[0], x1[0], x2[0], x3[0]], axis=0).astype(jnp.float32)
    squares[...] += jnp.sum(as_float * as_float, axis=0, keepdims=True)
    rows = (as_float * gain_ref[...]).astype(jnp.bfloat16)
    gate_total[...] += transposed_dot(gate_ref[0], rows)
    up_total[...] += transposed_dot(up_ref[0], rows)

    @pl.when(step == blocks - 1)
    def _():
        scale = lax.rsqrt(squares[...] / features + EPSILON)
        hidden_ref[...] = (silu(gate_total[...] * scale) * (up_total[...] * scale)).astype(jnp.bfloat16)


def expert_gate_up(slice_of, pooled, gate_weight, up_weight, gain_column):
    blocks, quarter_rows, columns = pooled[0].shape
    rows = 4 * quarter_rows
    hidden = gate_weight.shape[-1]
    weight_spec = pl.BlockSpec((1, rows, hidden), lambda m, at: (0, at[m], 0))

    def stream_spec(s):
        a, b, c, d = STREAMS[s]

        def index(m, at):
            return ((m >> a) & 1) | ((m >> b) & 1) << 1 | ((m >> c) & 1) << 2 | ((m >> d) & 1) << 3, 0, 0

        return pl.BlockSpec((1, quarter_rows, columns), index)

    return pl.pallas_call(
        functools.partial(expert_kernel, blocks, blocks * rows),
        grid_spec=pltpu.PrefetchScalarGridSpec(
            num_scalar_prefetch=1,
            grid=(blocks,),
            in_specs=[stream_spec(s) for s in range(4)]
            + [weight_spec, weight_spec, pl.BlockSpec((rows, 1), lambda m, at: (at[m], 0))],
            out_specs=pl.BlockSpec((hidden, columns), lambda m, at: (0, 0)),
            scratch_shapes=[
                pltpu.VMEM((hidden, columns), jnp.float32),
                pltpu.VMEM((hidden, columns), jnp.float32),
                pltpu.VMEM((1, columns), jnp.float32),
            ],
        ),
        out_shape=jax.ShapeDtypeStruct((hidden, columns), jnp.bfloat16),
        compiler_params=pltpu.CompilerParams(vmem_limit_bytes=24 << 20),
        cost_estimate=pl.CostEstimate(
            flops=4 * blocks * rows * columns * hidden,
            bytes_accessed=2 * blocks * rows * (columns + 2 * hidden),
            transcendentals=0,
        ),
    )(slice_of, *pooled, gate_weight, up_weight, gain_column)


def expert_down_kernel(weight_ref, hidden_ref, out_ref):
    out_ref[...] = transposed_dot(weight_ref[0], hidden_ref[...]).astype(jnp.bfloat16)


def expert_down_parts(weight, hidden):
    _, deep, features = weight.shape
    columns = hidden.shape[1]
    wide = features // 4
    return pl.pallas_call(
        expert_down_kernel,
        grid=(features // wide,),
        in_specs=[
            pl.BlockSpec((1, deep, wide), lambda m: (0, 0, m)),
            pl.BlockSpec((deep, columns), lambda m: (0, 0)),
        ],
        out_specs=pl.BlockSpec((wide, columns), lambda m: (m, 0)),
        out_shape=jax.ShapeDtypeStruct((features, columns), jnp.bfloat16),
        compiler_params=pltpu.CompilerParams(vmem_limit_bytes=24 << 20),
        cost_estimate=pl.CostEstimate(
            flops=2 * features * deep * columns, bytes_accessed=2 * features * (deep + columns), transcendentals=0
        ),
    )(weight, hidden)


def shards(
    tokens,
    norm_gain,
    dense_gate,
    dense_up,
    dense_down,
    expert_gate,
    expert_up,
    expert_down,
    expert_ids,
    route_gates,
):
    node_count = lax.axis_size("node")
    local_index = lax.axis_index("local")
    slice_width = tokens.shape[1]
    width = slice_width * 16
    slot_count = node_count * NODE_CAP
    slice_table = [[LOCAL_AT[LOCAL_LABEL[i] ^ m] for m in range(16)] for i in range(16)]
    slice_of = jnp.asarray(slice_table, jnp.int32)[local_index]

    columns = tokens.T
    whole_columns = lax.all_gather(columns, "local", axis=0, tiled=True)

    slot = route_slots(expert_ids, node_count)
    slot_range = jnp.arange(slot_count, dtype=jnp.int32)
    match_float = (slot[:, :, None] == slot_range[None, None, :]).astype(jnp.float32)
    chosen = jnp.sum(match_float, axis=1).astype(jnp.bfloat16)
    slot_gate = jnp.sum(match_float * route_gates[:, :, None], axis=(0, 1))
    send_rows = lax.dot_general(
        chosen, tokens, (((0,), (0,)), ((), ())), preferred_element_type=jnp.float32
    ).astype(jnp.bfloat16)
    routed = lax.all_to_all(
        send_rows.reshape(node_count, NODE_CAP, slice_width), "node", split_axis=0, concat_axis=0, tiled=True
    )
    routed = routed.reshape(slot_count, slice_width).T

    as_float = columns.astype(jnp.float32)
    square_sum = jnp.sum(as_float * as_float, axis=0, keepdims=True)
    gain_column = norm_gain[:, None]
    part = slice_width // 4
    pooled = [routed[None, s * part : (s + 1) * part] for s in range(4)]
    for step in range(4):
        got = [flip_local(pooled[s], STREAMS[s][step]) for s in range(4)]
        square_sum = square_sum + flip_local(square_sum, step)
        if step == 1:
            dense_gate, dense_up, _ = lax.optimization_barrier((dense_gate, dense_up, pooled))
            weight = jnp.concatenate(
                [(w.astype(jnp.float32) * gain_column).astype(jnp.bfloat16) for w in (dense_gate, dense_up)], axis=1
            )
            got, weight = lax.optimization_barrier((got, weight))
        if step == 2:
            dense_down, _ = lax.optimization_barrier((dense_down, pooled))
            turned = dense_down.T.reshape(16, slice_width, dense_down.shape[0])
            got, turned = lax.optimization_barrier((got, turned))
        pooled = [jnp.concatenate([pooled[s], got[s]], axis=0) for s in range(4)]
    scale = lax.rsqrt(square_sum / width + EPSILON)

    expert_hidden = expert_gate_up(slice_of, pooled, expert_gate, expert_up, gain_column)
    expert_partial = expert_down_parts(expert_down, expert_hidden)
    _, scale, whole_columns = lax.optimization_barrier((expert_partial, scale, whole_columns))
    expert_parts = lax.all_to_all(
        expert_partial.reshape(16, slice_width, slot_count), "local", split_axis=0, concat_axis=0, tiled=True
    )

    gate_up = transposed_dot(weight, whole_columns)
    low_hidden, *sent = sent_parts(0, slice_of, gate_up, scale, turned)
    high_hidden, *more = sent_parts(2, slice_of, gate_up, scale, turned)
    sent += more
    arrived = [flip_local(sent[s], STREAMS[s][0]) for s in range(4)]
    low_hidden, expert_parts = lax.optimization_barrier((low_hidden, expert_parts))
    sums = kept_parts(slice_of, turned, (low_hidden, high_hidden))
    expert_out = jnp.sum(expert_parts.astype(jnp.float32), axis=0).astype(jnp.bfloat16)
    returned = lax.all_to_all(
        expert_out.T.reshape(node_count, NODE_CAP, slice_width), "node", split_axis=0, concat_axis=0, tiled=True
    ).reshape(slot_count, slice_width)
    route_term = (slot_gate[:, None] * returned.astype(jnp.float32)).astype(jnp.bfloat16)
    arrived[1], route_term = lax.optimization_barrier((arrived[1], route_term))
    terms = [[sums[s], arrived[s]] for s in range(4)]

    def added(s, low, high):
        return sum(term[low:high].astype(jnp.float32) for term in terms[s])

    for step in (1, 2, 3):
        half = 8 >> step
        for s in range(4):
            terms[s].append(flip_local(added(s, half, 2 * half).astype(jnp.bfloat16), STREAMS[s][step]))
    expert_part = lax.dot_general(
        route_term, chosen, (((0,), (1,)), ((), ())), preferred_element_type=jnp.float32
    )
    dense_part = jnp.concatenate([added(s, 0, 1)[0] for s in range(4)], axis=1)
    return (columns.astype(jnp.float32) + dense_part + expert_part).astype(jnp.bfloat16).T


def solution(mesh):
    return jax.shard_map(
        shards,
        mesh=mesh,
        in_specs=(
            P("node", "local"),
            P(),
            P(None, "local"),
            P(None, "local"),
            P("local", None),
            P("node", None, "local"),
            P("node", None, "local"),
            P("node", "local", None),
            P("node", None),
            P("node", None),
        ),
        out_specs=P("node", "local"),
        check_vma=False,
    )
```

```python
import functools

import jax
import jax.numpy as jnp
from jax import lax
from jax.experimental import pallas as pl
from jax.experimental.pallas import tpu as pltpu
from jax.sharding import PartitionSpec as P

EPSILON = 1e-05
NODE_CAP = 16
GRAY = (0, 1, 3, 2)

LOCAL_LABEL = [GRAY[i % 4] | GRAY[i // 4] << 2 for i in range(16)]
LOCAL_AT = {label: i for i, label in enumerate(LOCAL_LABEL)}

STREAMS = ((0, 1, 2, 3), (1, 2, 3, 0), (2, 3, 0, 1), (3, 0, 1, 2))


def flip_local(array, bit):
    return lax.ppermute(array, "local", [(i, LOCAL_AT[LOCAL_LABEL[i] ^ (1 << bit)]) for i in range(16)])


def route_slots(ids_block, window):
    flat_ids = ids_block.reshape(-1)
    expert_range = jnp.arange(window, dtype=jnp.int32)
    member = (flat_ids[:, None] == expert_range[None, :]).astype(jnp.int32)
    before = jnp.cumsum(member, axis=0) - member
    route_rank = jnp.sum(before * member, axis=1)
    kept = (jnp.sum(member, axis=1) > 0) & (route_rank < NODE_CAP)
    slot = jnp.where(kept, flat_ids * NODE_CAP + route_rank, -1)
    return slot.reshape(ids_block.shape)


def transposed_dot(weight, rows):
    return lax.dot_general(weight, rows, (((0,), (0,)), ((), ())), preferred_element_type=jnp.float32)


def silu(value):
    return value / (1.0 + jnp.exp(-value))


def send_kernel(first, slice_ref, gate_up_ref, scale_ref, turned_ref, hidden_ref, *outs):
    half = gate_up_ref.shape[0] // 2
    columns = outs[0].shape[-1]
    for i, out in enumerate(outs):
        here = slice((first + i) * columns, (first + i + 1) * columns)
        scale = scale_ref[:, here]
        hidden = (silu(gate_up_ref[:half, here] * scale) * (gate_up_ref[half:, here] * scale)).astype(jnp.bfloat16)
        hidden_ref[:, i * columns : (i + 1) * columns] = hidden
        for j in range(out.shape[0]):
            at = slice_ref[stream_mask(first + i, 1, j)]
            out[j] = jnp.dot(turned_ref[at], hidden, preferred_element_type=jnp.float32).astype(jnp.bfloat16)


def stream_mask(s, sent, j):
    a, b, c, d = STREAMS[s]
    return sent << a | ((j >> 2) & 1) << b | ((j >> 1) & 1) << c | (j & 1) << d


def sent_parts(first, slice_of, gate_up, scale, turned):
    both = gate_up.shape[0]
    columns = gate_up.shape[1] // 4
    blocks, slice_rows, deep = turned.shape
    in_vmem = pl.BlockSpec(memory_space=pltpu.VMEM)
    return pl.pallas_call(
        functools.partial(send_kernel, first),
        in_specs=[pl.BlockSpec(memory_space=pltpu.SMEM), in_vmem, in_vmem, in_vmem],
        out_specs=[in_vmem] * 3,
        out_shape=[jax.ShapeDtypeStruct((deep, 2 * columns), jnp.bfloat16)]
        + [jax.ShapeDtypeStruct((blocks // 2, slice_rows, columns), jnp.bfloat16)] * 2,
        compiler_params=pltpu.CompilerParams(vmem_limit_bytes=24 << 20),
        cost_estimate=pl.CostEstimate(
            flops=2 * blocks * slice_rows * deep * columns,
            bytes_accessed=2 * blocks * slice_rows * (deep + columns),
            transcendentals=0,
        ),
    )(slice_of, gate_up, scale, turned)


def keep_kernel(slice_ref, *refs):
    weights, hidden, outs = refs[:4], refs[4:6], refs[6:]
    columns = outs[0].shape[-1]
    for s in range(4):
        rows = hidden[s // 2][:, s % 2 * columns : (s % 2 + 1) * columns]
        outs[s][0] = jnp.dot(weights[s][0], rows, preferred_element_type=jnp.float32).astype(jnp.bfloat16)


def kept_parts(slice_of, turned, hidden):
    blocks, rows, deep = turned.shape
    columns = hidden[0].shape[1] // 2

    def weight_spec(s):
        return pl.BlockSpec((1, rows, deep), lambda j, at: (at[stream_mask(s, 0, j)], 0, 0))

    return pl.pallas_call(
        keep_kernel,
        grid_spec=pltpu.PrefetchScalarGridSpec(
            num_scalar_prefetch=1,
            grid=(blocks // 2,),
            in_specs=[weight_spec(s) for s in range(4)] + [pl.BlockSpec((deep, 2 * columns), lambda j, at: (0, 0))] * 2,
            out_specs=[pl.BlockSpec((1, rows, columns), lambda j, at: (j, 0, 0))] * 4,
        ),
        out_shape=[jax.ShapeDtypeStruct((blocks // 2, rows, columns), jnp.bfloat16)] * 4,
        compiler_params=pltpu.CompilerParams(vmem_limit_bytes=24 << 20),
        cost_estimate=pl.CostEstimate(
            flops=4 * blocks * rows * deep * columns, bytes_accessed=4 * blocks * rows * (deep + columns), transcendentals=0
        ),
    )(slice_of, *[turned] * 4, *hidden)


def expert_kernel(blocks, features, at_ref, x0, x1, x2, x3, gate_ref, up_ref, gain_ref, hidden_ref, gate_total, up_total, squares):
    step = pl.program_id(0)

    @pl.when(step == 0)
    def _():
        gate_total[...] = jnp.zeros_like(gate_total)
        up_total[...] = jnp.zeros_like(up_total)
        squares[...] = jnp.zeros_like(squares)

    as_float = jnp.concatenate([x0[0], x1[0], x2[0], x3[0]], axis=0).astype(jnp.float32)
    squares[...] += jnp.sum(as_float * as_float, axis=0, keepdims=True)
    rows = (as_float * gain_ref[...]).astype(jnp.bfloat16)
    gate_total[...] += transposed_dot(gate_ref[0], rows)
    up_total[...] += transposed_dot(up_ref[0], rows)

    @pl.when(step == blocks - 1)
    def _():
        scale = lax.rsqrt(squares[...] / features + EPSILON)
        hidden_ref[...] = (silu(gate_total[...] * scale) * (up_total[...] * scale)).astype(jnp.bfloat16)


def expert_gate_up(slice_of, pooled, gate_weight, up_weight, gain_column):
    blocks, quarter_rows, columns = pooled[0].shape
    rows = 4 * quarter_rows
    hidden = gate_weight.shape[-1]
    weight_spec = pl.BlockSpec((1, rows, hidden), lambda m, at: (0, at[m], 0))

    def stream_spec(s):
        a, b, c, d = STREAMS[s]

        def index(m, at):
            return ((m >> a) & 1) | ((m >> b) & 1) << 1 | ((m >> c) & 1) << 2 | ((m >> d) & 1) << 3, 0, 0

        return pl.BlockSpec((1, quarter_rows, columns), index)

    return pl.pallas_call(
        functools.partial(expert_kernel, blocks, blocks * rows),
        grid_spec=pltpu.PrefetchScalarGridSpec(
            num_scalar_prefetch=1,
            grid=(blocks,),
            in_specs=[stream_spec(s) for s in range(4)]
            + [weight_spec, weight_spec, pl.BlockSpec((rows, 1), lambda m, at: (at[m], 0))],
            out_specs=pl.BlockSpec((hidden, columns), lambda m, at: (0, 0)),
            scratch_shapes=[
                pltpu.VMEM((hidden, columns), jnp.float32),
                pltpu.VMEM((hidden, columns), jnp.float32),
                pltpu.VMEM((1, columns), jnp.float32),
            ],
        ),
        out_shape=jax.ShapeDtypeStruct((hidden, columns), jnp.bfloat16),
        compiler_params=pltpu.CompilerParams(vmem_limit_bytes=24 << 20),
        cost_estimate=pl.CostEstimate(
            flops=4 * blocks * rows * columns * hidden,
            bytes_accessed=2 * blocks * rows * (columns + 2 * hidden),
            transcendentals=0,
        ),
    )(slice_of, *pooled, gate_weight, up_weight, gain_column)


def expert_down_kernel(weight_ref, hidden_ref, out_ref):
    out_ref[...] = transposed_dot(weight_ref[0], hidden_ref[...]).astype(jnp.bfloat16)


def expert_down_parts(weight, hidden):
    _, deep, features = weight.shape
    columns = hidden.shape[1]
    wide = features // 4
    return pl.pallas_call(
        expert_down_kernel,
        grid=(features // wide,),
        in_specs=[
            pl.BlockSpec((1, deep, wide), lambda m: (0, 0, m)),
            pl.BlockSpec((deep, columns), lambda m: (0, 0)),
        ],
        out_specs=pl.BlockSpec((wide, columns), lambda m: (m, 0)),
        out_shape=jax.ShapeDtypeStruct((features, columns), jnp.bfloat16),
        compiler_params=pltpu.CompilerParams(vmem_limit_bytes=24 << 20),
        cost_estimate=pl.CostEstimate(
            flops=2 * features * deep * columns, bytes_accessed=2 * features * (deep + columns), transcendentals=0
        ),
    )(weight, hidden)


def shards(
    tokens,
    norm_gain,
    dense_gate,
    dense_up,
    dense_down,
    expert_gate,
    expert_up,
    expert_down,
    expert_ids,
    route_gates,
):
    node_count = lax.axis_size("node")
    local_index = lax.axis_index("local")
    slice_width = tokens.shape[1]
    width = slice_width * 16
    slot_count = node_count * NODE_CAP
    slice_table = [[LOCAL_AT[LOCAL_LABEL[i] ^ m] for m in range(16)] for i in range(16)]
    slice_of = jnp.asarray(slice_table, jnp.int32)[local_index]

    columns = tokens.T
    whole_columns = lax.all_gather(columns, "local", axis=0, tiled=True)

    slot = route_slots(expert_ids, node_count)
    slot_range = jnp.arange(slot_count, dtype=jnp.int32)
    match_float = (slot[:, :, None] == slot_range[None, None, :]).astype(jnp.float32)
    chosen = jnp.sum(match_float, axis=1).astype(jnp.bfloat16)
    slot_gate = jnp.sum(match_float * route_gates[:, :, None], axis=(0, 1))
    send_rows = lax.dot_general(
        chosen, tokens, (((0,), (0,)), ((), ())), preferred_element_type=jnp.float32
    ).astype(jnp.bfloat16)
    routed = lax.all_to_all(
        send_rows.reshape(node_count, NODE_CAP, slice_width), "node", split_axis=0, concat_axis=0, tiled=True
    )
    routed = routed.reshape(slot_count, slice_width).T

    as_float = columns.astype(jnp.float32)
    square_sum = jnp.sum(as_float * as_float, axis=0, keepdims=True)
    gain_column = norm_gain[:, None]
    part = slice_width // 4
    pooled = [routed[None, s * part : (s + 1) * part] for s in range(4)]
    for step in range(4):
        got = [flip_local(pooled[s], STREAMS[s][step]) for s in range(4)]
        square_sum = square_sum + flip_local(square_sum, step)
        if step == 1:
            dense_gate, dense_up, _ = lax.optimization_barrier((dense_gate, dense_up, pooled))
            weight = jnp.concatenate(
                [(w.astype(jnp.float32) * gain_column).astype(jnp.bfloat16) for w in (dense_gate, dense_up)], axis=1
            )
            got, weight = lax.optimization_barrier((got, weight))
        if step == 2:
            dense_down, _ = lax.optimization_barrier((dense_down, pooled))
            turned = dense_down.T.reshape(16, slice_width, dense_down.shape[0])
            got, turned = lax.optimization_barrier((got, turned))
        pooled = [jnp.concatenate([pooled[s], got[s]], axis=0) for s in range(4)]
    scale = lax.rsqrt(square_sum / width + EPSILON)

    expert_hidden = expert_gate_up(slice_of, pooled, expert_gate, expert_up, gain_column)
    expert_partial = expert_down_parts(expert_down, expert_hidden)
    expert_partial, scale, whole_columns = lax.optimization_barrier((expert_partial, scale, whole_columns))
    expert_parts = lax.all_to_all(
        expert_partial.reshape(16, slice_width, slot_count), "local", split_axis=0, concat_axis=0, tiled=True
    )

    gate_up = transposed_dot(weight, whole_columns)
    low_hidden, *sent = sent_parts(0, slice_of, gate_up, scale, turned)
    high_hidden, *more = sent_parts(2, slice_of, gate_up, scale, turned)
    sent += more
    arrived = [flip_local(sent[s], STREAMS[s][0]) for s in range(4)]
    low_hidden, expert_parts = lax.optimization_barrier((low_hidden, expert_parts))
    sums = kept_parts(slice_of, turned, (low_hidden, high_hidden))
    expert_out = jnp.sum(expert_parts.astype(jnp.float32), axis=0).astype(jnp.bfloat16)
    returned = lax.all_to_all(
        expert_out.T.reshape(node_count, NODE_CAP, slice_width), "node", split_axis=0, concat_axis=0, tiled=True
    ).reshape(slot_count, slice_width)
    route_term = (slot_gate[:, None] * returned.astype(jnp.float32)).astype(jnp.bfloat16)
    arrived[1], route_term = lax.optimization_barrier((arrived[1], route_term))
    terms = [[sums[s], arrived[s]] for s in range(4)]

    def added(s, low, high):
        return sum(term[low:high].astype(jnp.float32) for term in terms[s])

    for step in (1, 2, 3):
        half = 8 >> step
        for s in range(4):
            terms[s].append(flip_local(added(s, half, 2 * half).astype(jnp.bfloat16), STREAMS[s][step]))
    expert_part = lax.dot_general(
        route_term, chosen, (((0,), (1,)), ((), ())), preferred_element_type=jnp.float32
    )
    dense_part = jnp.concatenate([added(s, 0, 1)[0] for s in range(4)], axis=1)
    return (columns.astype(jnp.float32) + dense_part + expert_part).astype(jnp.bfloat16).T


def solution(mesh):
    return jax.shard_map(
        shards,
        mesh=mesh,
        in_specs=(
            P("node", "local"),
            P(),
            P(None, "local"),
            P(None, "local"),
            P("local", None),
            P("node", None, "local"),
            P("node", None, "local"),
            P("node", "local", None),
            P("node", None),
            P("node", None),
        ),
        out_specs=P("node", "local"),
        check_vma=False,
    )
```

```python
import functools

import jax
import jax.numpy as jnp
from jax import lax
from jax.experimental import pallas as pl
from jax.experimental.pallas import tpu as pltpu
from jax.sharding import PartitionSpec as P

EPSILON = 1e-05
NODE_CAP = 16
GRAY = (0, 1, 3, 2)

LOCAL_LABEL = [GRAY[i % 4] | GRAY[i // 4] << 2 for i in range(16)]
LOCAL_AT = {label: i for i, label in enumerate(LOCAL_LABEL)}

STREAMS = ((0, 1, 2, 3), (1, 2, 3, 0), (2, 3, 0, 1), (3, 0, 1, 2))


def flip_local(array, bit):
    return lax.ppermute(array, "local", [(i, LOCAL_AT[LOCAL_LABEL[i] ^ (1 << bit)]) for i in range(16)])


def route_slots(ids_block, window):
    flat_ids = ids_block.reshape(-1)
    expert_range = jnp.arange(window, dtype=jnp.int32)
    member = (flat_ids[:, None] == expert_range[None, :]).astype(jnp.int32)
    before = jnp.cumsum(member, axis=0) - member
    route_rank = jnp.sum(before * member, axis=1)
    kept = (jnp.sum(member, axis=1) > 0) & (route_rank < NODE_CAP)
    slot = jnp.where(kept, flat_ids * NODE_CAP + route_rank, -1)
    return slot.reshape(ids_block.shape)


def transposed_dot(weight, rows):
    return lax.dot_general(weight, rows, (((0,), (0,)), ((), ())), preferred_element_type=jnp.float32)


def silu(value):
    return value / (1.0 + jnp.exp(-value))


def send_kernel(first, slice_ref, gate_up_ref, scale_ref, turned_ref, hidden_ref, *outs):
    half = gate_up_ref.shape[0] // 2
    columns = outs[0].shape[-1]
    for i, out in enumerate(outs):
        here = slice((first + i) * columns, (first + i + 1) * columns)
        scale = scale_ref[:, here]
        hidden = (silu(gate_up_ref[:half, here] * scale) * (gate_up_ref[half:, here] * scale)).astype(jnp.bfloat16)
        hidden_ref[:, i * columns : (i + 1) * columns] = hidden
        for j in range(out.shape[0]):
            at = slice_ref[stream_mask(first + i, 1, j)]
            out[j] = jnp.dot(turned_ref[at], hidden, preferred_element_type=jnp.float32).astype(jnp.bfloat16)


def stream_mask(s, sent, j):
    a, b, c, d = STREAMS[s]
    return sent << a | ((j >> 2) & 1) << b | ((j >> 1) & 1) << c | (j & 1) << d


def sent_parts(first, slice_of, gate_up, scale, turned):
    both = gate_up.shape[0]
    columns = gate_up.shape[1] // 4
    blocks, slice_rows, deep = turned.shape
    in_vmem = pl.BlockSpec(memory_space=pltpu.VMEM)
    return pl.pallas_call(
        functools.partial(send_kernel, first),
        in_specs=[pl.BlockSpec(memory_space=pltpu.SMEM), in_vmem, in_vmem, in_vmem],
        out_specs=[in_vmem] * 3,
        out_shape=[jax.ShapeDtypeStruct((deep, 2 * columns), jnp.bfloat16)]
        + [jax.ShapeDtypeStruct((blocks // 2, slice_rows, columns), jnp.bfloat16)] * 2,
        compiler_params=pltpu.CompilerParams(vmem_limit_bytes=24 << 20),
        cost_estimate=pl.CostEstimate(
            flops=2 * blocks * slice_rows * deep * columns,
            bytes_accessed=2 * blocks * slice_rows * (deep + columns),
            transcendentals=0,
        ),
    )(slice_of, gate_up, scale, turned)


def keep_kernel(slice_ref, *refs):
    weights, hidden, outs = refs[:4], refs[4:6], refs[6:]
    columns = outs[0].shape[-1]
    for s in range(4):
        rows = hidden[s // 2][:, s % 2 * columns : (s % 2 + 1) * columns]
        outs[s][0] = jnp.dot(weights[s][0], rows, preferred_element_type=jnp.float32).astype(jnp.bfloat16)


def kept_parts(slice_of, turned, hidden):
    blocks, rows, deep = turned.shape
    columns = hidden[0].shape[1] // 2

    def weight_spec(s):
        return pl.BlockSpec((1, rows, deep), lambda j, at: (at[stream_mask(s, 0, j)], 0, 0))

    return pl.pallas_call(
        keep_kernel,
        grid_spec=pltpu.PrefetchScalarGridSpec(
            num_scalar_prefetch=1,
            grid=(blocks // 2,),
            in_specs=[weight_spec(s) for s in range(4)] + [pl.BlockSpec((deep, 2 * columns), lambda j, at: (0, 0))] * 2,
            out_specs=[pl.BlockSpec((1, rows, columns), lambda j, at: (j, 0, 0))] * 4,
        ),
        out_shape=[jax.ShapeDtypeStruct((blocks // 2, rows, columns), jnp.bfloat16)] * 4,
        compiler_params=pltpu.CompilerParams(vmem_limit_bytes=24 << 20),
        cost_estimate=pl.CostEstimate(
            flops=4 * blocks * rows * deep * columns, bytes_accessed=4 * blocks * rows * (deep + columns), transcendentals=0
        ),
    )(slice_of, *[turned] * 4, *hidden)


def expert_kernel(blocks, features, at_ref, x0, x1, x2, x3, gate_ref, up_ref, gain_ref, hidden_ref, gate_total, up_total, squares):
    step = pl.program_id(0)

    @pl.when(step == 0)
    def _():
        gate_total[...] = jnp.zeros_like(gate_total)
        up_total[...] = jnp.zeros_like(up_total)
        squares[...] = jnp.zeros_like(squares)

    as_float = jnp.concatenate([x0[0], x1[0], x2[0], x3[0]], axis=0).astype(jnp.float32)
    squares[...] += jnp.sum(as_float * as_float, axis=0, keepdims=True)
    rows = (as_float * gain_ref[...]).astype(jnp.bfloat16)
    gate_total[...] += transposed_dot(gate_ref[0], rows)
    up_total[...] += transposed_dot(up_ref[0], rows)

    @pl.when(step == blocks - 1)
    def _():
        scale = lax.rsqrt(squares[...] / features + EPSILON)
        hidden_ref[...] = (silu(gate_total[...] * scale) * (up_total[...] * scale)).astype(jnp.bfloat16)


def expert_gate_up(slice_of, pooled, gate_weight, up_weight, gain_column):
    blocks, quarter_rows, columns = pooled[0].shape
    rows = 4 * quarter_rows
    hidden = gate_weight.shape[-1]
    weight_spec = pl.BlockSpec((1, rows, hidden), lambda m, at: (0, at[m], 0))

    def stream_spec(s):
        a, b, c, d = STREAMS[s]

        def index(m, at):
            return ((m >> a) & 1) | ((m >> b) & 1) << 1 | ((m >> c) & 1) << 2 | ((m >> d) & 1) << 3, 0, 0

        return pl.BlockSpec((1, quarter_rows, columns), index)

    return pl.pallas_call(
        functools.partial(expert_kernel, blocks, blocks * rows),
        grid_spec=pltpu.PrefetchScalarGridSpec(
            num_scalar_prefetch=1,
            grid=(blocks,),
            in_specs=[stream_spec(s) for s in range(4)]
            + [weight_spec, weight_spec, pl.BlockSpec((rows, 1), lambda m, at: (at[m], 0))],
            out_specs=pl.BlockSpec((hidden, columns), lambda m, at: (0, 0)),
            scratch_shapes=[
                pltpu.VMEM((hidden, columns), jnp.float32),
                pltpu.VMEM((hidden, columns), jnp.float32),
                pltpu.VMEM((1, columns), jnp.float32),
            ],
        ),
        out_shape=jax.ShapeDtypeStruct((hidden, columns), jnp.bfloat16),
        compiler_params=pltpu.CompilerParams(vmem_limit_bytes=24 << 20),
        cost_estimate=pl.CostEstimate(
            flops=4 * blocks * rows * columns * hidden,
            bytes_accessed=2 * blocks * rows * (columns + 2 * hidden),
            transcendentals=0,
        ),
    )(slice_of, *pooled, gate_weight, up_weight, gain_column)


def expert_down_kernel(weight_ref, hidden_ref, out_ref):
    out_ref[...] = transposed_dot(weight_ref[0], hidden_ref[...]).astype(jnp.bfloat16)


def expert_down_parts(weight, hidden):
    _, deep, features = weight.shape
    columns = hidden.shape[1]
    wide = features // 4
    return pl.pallas_call(
        expert_down_kernel,
        grid=(features // wide,),
        in_specs=[
            pl.BlockSpec((1, deep, wide), lambda m: (0, 0, m)),
            pl.BlockSpec((deep, columns), lambda m: (0, 0)),
        ],
        out_specs=pl.BlockSpec((wide, columns), lambda m: (m, 0)),
        out_shape=jax.ShapeDtypeStruct((features, columns), jnp.bfloat16),
        compiler_params=pltpu.CompilerParams(vmem_limit_bytes=24 << 20),
        cost_estimate=pl.CostEstimate(
            flops=2 * features * deep * columns, bytes_accessed=2 * features * (deep + columns), transcendentals=0
        ),
    )(weight, hidden)


def shards(
    tokens,
    norm_gain,
    dense_gate,
    dense_up,
    dense_down,
    expert_gate,
    expert_up,
    expert_down,
    expert_ids,
    route_gates,
):
    node_count = lax.axis_size("node")
    local_index = lax.axis_index("local")
    slice_width = tokens.shape[1]
    width = slice_width * 16
    slot_count = node_count * NODE_CAP
    slice_table = [[LOCAL_AT[LOCAL_LABEL[i] ^ m] for m in range(16)] for i in range(16)]
    slice_of = jnp.asarray(slice_table, jnp.int32)[local_index]

    columns = tokens.T
    whole_columns = lax.all_gather(columns, "local", axis=0, tiled=True)

    slot = route_slots(expert_ids, node_count)
    slot_range = jnp.arange(slot_count, dtype=jnp.int32)
    match_float = (slot[:, :, None] == slot_range[None, None, :]).astype(jnp.float32)
    chosen = jnp.sum(match_float, axis=1).astype(jnp.bfloat16)
    slot_gate = jnp.sum(match_float * route_gates[:, :, None], axis=(0, 1))
    send_rows = lax.dot_general(
        chosen, tokens, (((0,), (0,)), ((), ())), preferred_element_type=jnp.float32
    ).astype(jnp.bfloat16)
    routed = lax.all_to_all(
        send_rows.reshape(node_count, NODE_CAP, slice_width), "node", split_axis=0, concat_axis=0, tiled=True
    )
    routed = routed.reshape(slot_count, slice_width).T

    as_float = columns.astype(jnp.float32)
    square_sum = jnp.sum(as_float * as_float, axis=0, keepdims=True)
    gain_column = norm_gain[:, None]
    part = slice_width // 4
    pooled = [routed[None, s * part : (s + 1) * part] for s in range(4)]
    for step in range(4):
        got = [flip_local(pooled[s], STREAMS[s][step]) for s in range(4)]
        square_sum = square_sum + flip_local(square_sum, step)
        if step == 1:
            dense_gate, dense_up, _ = lax.optimization_barrier((dense_gate, dense_up, pooled))
            folded = [(w.astype(jnp.float32) * gain_column).astype(jnp.bfloat16) for w in (dense_gate, dense_up)]
            got, folded = lax.optimization_barrier((got, folded))
        if step == 2:
            dense_down, _ = lax.optimization_barrier((dense_down, pooled))
            turned = dense_down.T.reshape(16, slice_width, dense_down.shape[0])
            got, turned = lax.optimization_barrier((got, turned))
        pooled = [jnp.concatenate([pooled[s], got[s]], axis=0) for s in range(4)]
    scale = lax.rsqrt(square_sum / width + EPSILON)

    expert_hidden = expert_gate_up(slice_of, pooled, expert_gate, expert_up, gain_column)
    expert_partial = expert_down_parts(expert_down, expert_hidden)
    expert_partial, scale, whole_columns, folded = lax.optimization_barrier(
        (expert_partial, scale, whole_columns, folded)
    )
    expert_parts = lax.all_to_all(
        expert_partial.reshape(16, slice_width, slot_count), "local", split_axis=0, concat_axis=0, tiled=True
    )

    gate_up = transposed_dot(jnp.concatenate(folded, axis=1), whole_columns)
    low_hidden, *sent = sent_parts(0, slice_of, gate_up, scale, turned)
    high_hidden, *more = sent_parts(2, slice_of, gate_up, scale, turned)
    sent += more
    arrived = [flip_local(sent[s], STREAMS[s][0]) for s in range(4)]
    low_hidden, expert_parts = lax.optimization_barrier((low_hidden, expert_parts))
    sums = kept_parts(slice_of, turned, (low_hidden, high_hidden))
    expert_out = jnp.sum(expert_parts.astype(jnp.float32), axis=0).astype(jnp.bfloat16)
    returned = lax.all_to_all(
        expert_out.T.reshape(node_count, NODE_CAP, slice_width), "node", split_axis=0, concat_axis=0, tiled=True
    ).reshape(slot_count, slice_width)
    route_term = (slot_gate[:, None] * returned.astype(jnp.float32)).astype(jnp.bfloat16)
    arrived[1], route_term = lax.optimization_barrier((arrived[1], route_term))
    terms = [[sums[s], arrived[s]] for s in range(4)]

    def added(s, low, high):
        return sum(term[low:high].astype(jnp.float32) for term in terms[s])

    for step in (1, 2, 3):
        half = 8 >> step
        for s in range(4):
            terms[s].append(flip_local(added(s, half, 2 * half).astype(jnp.bfloat16), STREAMS[s][step]))
    expert_part = lax.dot_general(
        route_term, chosen, (((0,), (1,)), ((), ())), preferred_element_type=jnp.float32
    )
    dense_part = jnp.concatenate([added(s, 0, 1)[0] for s in range(4)], axis=1)
    return (columns.astype(jnp.float32) + dense_part + expert_part).astype(jnp.bfloat16).T


def solution(mesh):
    return jax.shard_map(
        shards,
        mesh=mesh,
        in_specs=(
            P("node", "local"),
            P(),
            P(None, "local"),
            P(None, "local"),
            P("local", None),
            P("node", None, "local"),
            P("node", None, "local"),
            P("node", "local", None),
            P("node", None),
            P("node", None),
        ),
        out_specs=P("node", "local"),
        check_vma=False,
    )
```

```python
import functools

import jax
import jax.numpy as jnp
from jax import lax
from jax.experimental import pallas as pl
from jax.experimental.pallas import tpu as pltpu
from jax.sharding import PartitionSpec as P

EPSILON = 1e-05
NODE_CAP = 16
GRAY = (0, 1, 3, 2)

LOCAL_LABEL = [GRAY[i % 4] | GRAY[i // 4] << 2 for i in range(16)]
LOCAL_AT = {label: i for i, label in enumerate(LOCAL_LABEL)}

STREAMS = ((0, 1, 2, 3), (1, 2, 3, 0), (2, 3, 0, 1), (3, 0, 1, 2))


def flip_local(array, bit):
    return lax.ppermute(array, "local", [(i, LOCAL_AT[LOCAL_LABEL[i] ^ (1 << bit)]) for i in range(16)])


def route_slots(ids_block, window):
    flat_ids = ids_block.reshape(-1)
    expert_range = jnp.arange(window, dtype=jnp.int32)
    member = (flat_ids[:, None] == expert_range[None, :]).astype(jnp.int32)
    before = jnp.cumsum(member, axis=0) - member
    route_rank = jnp.sum(before * member, axis=1)
    kept = (jnp.sum(member, axis=1) > 0) & (route_rank < NODE_CAP)
    slot = jnp.where(kept, flat_ids * NODE_CAP + route_rank, -1)
    return slot.reshape(ids_block.shape)


def transposed_dot(weight, rows):
    return lax.dot_general(weight, rows, (((0,), (0,)), ((), ())), preferred_element_type=jnp.float32)


def silu(value):
    return value / (1.0 + jnp.exp(-value))


def send_kernel(first, slice_ref, gate_up_ref, scale_ref, turned_ref, hidden_ref, *outs):
    half = gate_up_ref.shape[0] // 2
    columns = outs[0].shape[-1]
    for i, out in enumerate(outs):
        here = slice((first + i) * columns, (first + i + 1) * columns)
        scale = scale_ref[:, here]
        hidden = (silu(gate_up_ref[:half, here] * scale) * (gate_up_ref[half:, here] * scale)).astype(jnp.bfloat16)
        hidden_ref[:, i * columns : (i + 1) * columns] = hidden
        for j in range(out.shape[0]):
            at = slice_ref[stream_mask(first + i, 1, j)]
            out[j] = jnp.dot(turned_ref[at], hidden, preferred_element_type=jnp.float32).astype(jnp.bfloat16)


def stream_mask(s, sent, j):
    a, b, c, d = STREAMS[s]
    return sent << a | ((j >> 2) & 1) << b | ((j >> 1) & 1) << c | (j & 1) << d


def sent_parts(first, slice_of, gate_up, scale, turned):
    both = gate_up.shape[0]
    columns = gate_up.shape[1] // 4
    blocks, slice_rows, deep = turned.shape
    in_vmem = pl.BlockSpec(memory_space=pltpu.VMEM)
    return pl.pallas_call(
        functools.partial(send_kernel, first),
        in_specs=[pl.BlockSpec(memory_space=pltpu.SMEM), in_vmem, in_vmem, in_vmem],
        out_specs=[in_vmem] * 3,
        out_shape=[jax.ShapeDtypeStruct((deep, 2 * columns), jnp.bfloat16)]
        + [jax.ShapeDtypeStruct((blocks // 2, slice_rows, columns), jnp.bfloat16)] * 2,
        compiler_params=pltpu.CompilerParams(vmem_limit_bytes=24 << 20),
        cost_estimate=pl.CostEstimate(
            flops=2 * blocks * slice_rows * deep * columns,
            bytes_accessed=2 * blocks * slice_rows * (deep + columns),
            transcendentals=0,
        ),
    )(slice_of, gate_up, scale, turned)


def keep_kernel(slice_ref, *refs):
    weights, hidden, outs = refs[:4], refs[4:6], refs[6:]
    columns = outs[0].shape[-1]
    for s in range(4):
        rows = hidden[s // 2][:, s % 2 * columns : (s % 2 + 1) * columns]
        outs[s][0] = jnp.dot(weights[s][0], rows, preferred_element_type=jnp.float32).astype(jnp.bfloat16)


def kept_parts(slice_of, turned, hidden):
    blocks, rows, deep = turned.shape
    columns = hidden[0].shape[1] // 2

    def weight_spec(s):
        return pl.BlockSpec((1, rows, deep), lambda j, at: (at[stream_mask(s, 0, j)], 0, 0))

    return pl.pallas_call(
        keep_kernel,
        grid_spec=pltpu.PrefetchScalarGridSpec(
            num_scalar_prefetch=1,
            grid=(blocks // 2,),
            in_specs=[weight_spec(s) for s in range(4)] + [pl.BlockSpec((deep, 2 * columns), lambda j, at: (0, 0))] * 2,
            out_specs=[pl.BlockSpec((1, rows, columns), lambda j, at: (j, 0, 0))] * 4,
        ),
        out_shape=[jax.ShapeDtypeStruct((blocks // 2, rows, columns), jnp.bfloat16)] * 4,
        compiler_params=pltpu.CompilerParams(vmem_limit_bytes=24 << 20),
        cost_estimate=pl.CostEstimate(
            flops=4 * blocks * rows * deep * columns, bytes_accessed=4 * blocks * rows * (deep + columns), transcendentals=0
        ),
    )(slice_of, *[turned] * 4, *hidden)


def expert_kernel(blocks, features, at_ref, x0, x1, x2, x3, gate_ref, up_ref, gain_ref, hidden_ref, gate_total, up_total, squares):
    step = pl.program_id(0)

    @pl.when(step == 0)
    def _():
        gate_total[...] = jnp.zeros_like(gate_total)
        up_total[...] = jnp.zeros_like(up_total)
        squares[...] = jnp.zeros_like(squares)

    as_float = jnp.concatenate([x0[0], x1[0], x2[0], x3[0]], axis=0).astype(jnp.float32)
    squares[...] += jnp.sum(as_float * as_float, axis=0, keepdims=True)
    rows = (as_float * gain_ref[...]).astype(jnp.bfloat16)
    gate_total[...] += transposed_dot(gate_ref[0], rows)
    up_total[...] += transposed_dot(up_ref[0], rows)

    @pl.when(step == blocks - 1)
    def _():
        scale = lax.rsqrt(squares[...] / features + EPSILON)
        hidden_ref[...] = (silu(gate_total[...] * scale) * (up_total[...] * scale)).astype(jnp.bfloat16)


def expert_gate_up(slice_of, pooled, gate_weight, up_weight, gain_column):
    blocks, quarter_rows, columns = pooled[0].shape
    rows = 4 * quarter_rows
    hidden = gate_weight.shape[-1]
    weight_spec = pl.BlockSpec((1, rows, hidden), lambda m, at: (0, at[m], 0))

    def stream_spec(s):
        a, b, c, d = STREAMS[s]

        def index(m, at):
            return ((m >> a) & 1) | ((m >> b) & 1) << 1 | ((m >> c) & 1) << 2 | ((m >> d) & 1) << 3, 0, 0

        return pl.BlockSpec((1, quarter_rows, columns), index)

    return pl.pallas_call(
        functools.partial(expert_kernel, blocks, blocks * rows),
        grid_spec=pltpu.PrefetchScalarGridSpec(
            num_scalar_prefetch=1,
            grid=(blocks,),
            in_specs=[stream_spec(s) for s in range(4)]
            + [weight_spec, weight_spec, pl.BlockSpec((rows, 1), lambda m, at: (at[m], 0))],
            out_specs=pl.BlockSpec((hidden, columns), lambda m, at: (0, 0)),
            scratch_shapes=[
                pltpu.VMEM((hidden, columns), jnp.float32),
                pltpu.VMEM((hidden, columns), jnp.float32),
                pltpu.VMEM((1, columns), jnp.float32),
            ],
        ),
        out_shape=jax.ShapeDtypeStruct((hidden, columns), jnp.bfloat16),
        compiler_params=pltpu.CompilerParams(vmem_limit_bytes=24 << 20),
        cost_estimate=pl.CostEstimate(
            flops=4 * blocks * rows * columns * hidden,
            bytes_accessed=2 * blocks * rows * (columns + 2 * hidden),
            transcendentals=0,
        ),
    )(slice_of, *pooled, gate_weight, up_weight, gain_column)


def expert_down_kernel(weight_ref, hidden_ref, out_ref):
    out_ref[...] = transposed_dot(weight_ref[0], hidden_ref[...]).astype(jnp.bfloat16)


def expert_down_parts(weight, hidden):
    _, deep, features = weight.shape
    columns = hidden.shape[1]
    wide = features // 4
    return pl.pallas_call(
        expert_down_kernel,
        grid=(features // wide,),
        in_specs=[
            pl.BlockSpec((1, deep, wide), lambda m: (0, 0, m)),
            pl.BlockSpec((deep, columns), lambda m: (0, 0)),
        ],
        out_specs=pl.BlockSpec((wide, columns), lambda m: (m, 0)),
        out_shape=jax.ShapeDtypeStruct((features, columns), jnp.bfloat16),
        compiler_params=pltpu.CompilerParams(vmem_limit_bytes=24 << 20),
        cost_estimate=pl.CostEstimate(
            flops=2 * features * deep * columns, bytes_accessed=2 * features * (deep + columns), transcendentals=0
        ),
    )(weight, hidden)


def shards(
    tokens,
    norm_gain,
    dense_gate,
    dense_up,
    dense_down,
    expert_gate,
    expert_up,
    expert_down,
    expert_ids,
    route_gates,
):
    node_count = lax.axis_size("node")
    local_index = lax.axis_index("local")
    slice_width = tokens.shape[1]
    width = slice_width * 16
    slot_count = node_count * NODE_CAP
    slice_table = [[LOCAL_AT[LOCAL_LABEL[i] ^ m] for m in range(16)] for i in range(16)]
    slice_of = jnp.asarray(slice_table, jnp.int32)[local_index]

    columns = tokens.T
    whole_columns = lax.all_gather(columns, "local", axis=0, tiled=True)

    slot = route_slots(expert_ids, node_count)
    slot_range = jnp.arange(slot_count, dtype=jnp.int32)
    match_float = (slot[:, :, None] == slot_range[None, None, :]).astype(jnp.float32)
    chosen = jnp.sum(match_float, axis=1).astype(jnp.bfloat16)
    slot_gate = jnp.sum(match_float * route_gates[:, :, None], axis=(0, 1))
    send_rows = lax.dot_general(
        chosen, tokens, (((0,), (0,)), ((), ())), preferred_element_type=jnp.float32
    ).astype(jnp.bfloat16)
    routed = lax.all_to_all(
        send_rows.reshape(node_count, NODE_CAP, slice_width), "node", split_axis=0, concat_axis=0, tiled=True
    )
    routed = routed.reshape(slot_count, slice_width).T

    as_float = columns.astype(jnp.float32)
    square_sum = jnp.sum(as_float * as_float, axis=0, keepdims=True)
    gain_column = norm_gain[:, None]
    part = slice_width // 4
    pooled = [routed[None, s * part : (s + 1) * part] for s in range(4)]
    for step in range(4):
        got = [flip_local(pooled[s], STREAMS[s][step]) for s in range(4)]
        square_sum = square_sum + flip_local(square_sum, step)
        if step == 1:
            dense_gate, dense_up, _ = lax.optimization_barrier((dense_gate, dense_up, pooled))
            folded = [(w.astype(jnp.float32) * gain_column).astype(jnp.bfloat16) for w in (dense_gate, dense_up)]
            got, folded = lax.optimization_barrier((got, folded))
        if step == 2:
            dense_down, _ = lax.optimization_barrier((dense_down, pooled))
            turned = dense_down.T.reshape(16, slice_width, dense_down.shape[0])
            got, turned = lax.optimization_barrier((got, turned))
        if step == 3:
            folded, _ = lax.optimization_barrier((folded, pooled))
            weight = jnp.concatenate([w.T for w in folded], axis=0)
            got, weight = lax.optimization_barrier((got, weight))
        pooled = [jnp.concatenate([pooled[s], got[s]], axis=0) for s in range(4)]
    scale = lax.rsqrt(square_sum / width + EPSILON)

    expert_hidden = expert_gate_up(slice_of, pooled, expert_gate, expert_up, gain_column)
    expert_partial = expert_down_parts(expert_down, expert_hidden)
    expert_partial, scale, whole_columns = lax.optimization_barrier((expert_partial, scale, whole_columns))
    expert_parts = lax.all_to_all(
        expert_partial.reshape(16, slice_width, slot_count), "local", split_axis=0, concat_axis=0, tiled=True
    )

    gate_up = jnp.dot(weight, whole_columns, preferred_element_type=jnp.float32)
    low_hidden, *sent = sent_parts(0, slice_of, gate_up, scale, turned)
    high_hidden, *more = sent_parts(2, slice_of, gate_up, scale, turned)
    sent += more
    arrived = [flip_local(sent[s], STREAMS[s][0]) for s in range(4)]
    low_hidden, expert_parts = lax.optimization_barrier((low_hidden, expert_parts))
    sums = kept_parts(slice_of, turned, (low_hidden, high_hidden))
    expert_out = jnp.sum(expert_parts.astype(jnp.float32), axis=0).astype(jnp.bfloat16)
    returned = lax.all_to_all(
        expert_out.T.reshape(node_count, NODE_CAP, slice_width), "node", split_axis=0, concat_axis=0, tiled=True
    ).reshape(slot_count, slice_width)
    route_term = (slot_gate[:, None] * returned.astype(jnp.float32)).astype(jnp.bfloat16)
    arrived[1], route_term = lax.optimization_barrier((arrived[1], route_term))
    terms = [[sums[s], arrived[s]] for s in range(4)]

    def added(s, low, high):
        return sum(term[low:high].astype(jnp.float32) for term in terms[s])

    for step in (1, 2, 3):
        half = 8 >> step
        for s in range(4):
            terms[s].append(flip_local(added(s, half, 2 * half).astype(jnp.bfloat16), STREAMS[s][step]))
    expert_part = lax.dot_general(
        route_term, chosen, (((0,), (1,)), ((), ())), preferred_element_type=jnp.float32
    )
    dense_part = jnp.concatenate([added(s, 0, 1)[0] for s in range(4)], axis=1)
    return (columns.astype(jnp.float32) + dense_part + expert_part).astype(jnp.bfloat16).T


def solution(mesh):
    return jax.shard_map(
        shards,
        mesh=mesh,
        in_specs=(
            P("node", "local"),
            P(),
            P(None, "local"),
            P(None, "local"),
            P("local", None),
            P("node", None, "local"),
            P("node", None, "local"),
            P("node", "local", None),
            P("node", None),
            P("node", None),
        ),
        out_specs=P("node", "local"),
        check_vma=False,
    )
```
